128 devices in a mesh: noise: 16 (over y_hi, z, core), dp: 8 (over y_lo, x).
Axes of the slice: x: 4, y: 4 (y_hi: 2, y_lo: 2; y = y_hi * 2 + y_lo), z: 4, core: 2. Of those that a mesh axis runs over, the one named last changes fastest.
Arguments:
- noise_latents: float32 [6144, 4096], P(('noise', 'dp')), may hold values from -6.5 to 6.5
- data_latents: float32 [6144, 4096], P(('dp', 'noise')), may hold values from -6.5 to 6.5
Outputs:
- targets: float32 [6144, 4096], P(('noise', 'dp'))
- noise_potential: float32 [6144], P('noise')
- data_potential: float32 [6144], P('dp')
The draws below stay inside these ranges and needn't reach their ends.
All inputs are finite; a program needn't handle non-finite values.
Results may differ from the reference program's by a relative error of at most 0.0003.
Values sent between devices are 32-bit elements; how exact they have to be, the bound alone decides.
A program may use at most 64 MiB of HBM per device.

```python
import math
import jax
import jax.numpy as jnp
from jax import lax

WIDTH = 4096
ITERS = 3
NSAMP = 6144


def own_values(key):
    return jax.random.normal(key, (NSAMP, WIDTH), jnp.float32)


def row_scale(rows, period):
    return jnp.where(rows >= period - 2, 1.8, 1.0)


def draw_noise_latents(key, part):
    key = jax.random.fold_in(key, 1)
    values = own_values(key)
    period = NSAMP // 8
    rows = jnp.arange(NSAMP)[:, None] % period
    values = values * row_scale(rows, period)
    return jnp.clip(values, -6.0, 6.0)


def draw_data_latents(key, part):
    key = jax.random.fold_in(key, 2)
    values = own_values(key)
    period = NSAMP // 8
    rows = jnp.arange(NSAMP)[:, None] % period
    values = values * row_scale(rows, period)
    return jnp.clip(values, -6.0, 6.0)


def setup_inputs(seed: int = 0) -> dict:
    streams_of = jax.random.split(jax.random.key(seed), 3)
    return {
        "noise_latents": draw_noise_latents(jax.random.fold_in(streams_of[2], 71), 0),
        "data_latents": draw_data_latents(jax.random.fold_in(streams_of[2], 71), 0),
    }


EPS = 0.01


def log_sum(scores, axis):
    top = jnp.max(scores, axis=axis, keepdims=True)
    total = jnp.sum(jnp.exp(scores - top), axis=axis)
    return jnp.squeeze(top, axis) + jnp.log(total)


def reference(noise_latents, data_latents):
    row_sq = jnp.sum(noise_latents * noise_latents, axis=1)
    col_sq = jnp.sum(data_latents * data_latents, axis=1)
    cross = lax.dot_general(noise_latents, data_latents, (((1,), (1,)), ((), ())), precision=lax.Precision.HIGHEST, preferred_element_type=jnp.float32)
    cost = (row_sq[:, None] + col_sq[None, :] - 2.0 * cross) / WIDTH
    log_mass = -math.log(NSAMP)
    data_potential = jnp.zeros((NSAMP,), jnp.float32)
    noise_potential = jnp.zeros((NSAMP,), jnp.float32)
    for step in range(ITERS):
        noise_potential = -EPS * (log_sum((data_potential[None, :] - cost) / EPS, 1) + log_mass)
        data_potential = -EPS * (log_sum((noise_potential[:, None] - cost) / EPS, 0) + log_mass)
    logits = (data_potential[None, :] - cost) / EPS
    total = log_sum(logits, 1)
    weights = jnp.exp(logits - total[:, None])
    targets = jnp.dot(weights, data_latents, precision=lax.Precision.HIGHEST, preferred_element_type=jnp.float32)
    return targets, noise_potential, data_potential
```

```python
import functools
import math

import jax
import jax.numpy as jnp
from jax import lax
from jax.experimental import pallas as pl
from jax.experimental.pallas import tpu as pltpu
from jax.sharding import PartitionSpec as P

MESH = pl.DeviceIdType.MESH
F32 = jnp.float32
BF16 = jnp.bfloat16
EPS = 0.01

OWN = 48
WIDTH = 4096
HALF = WIDTH // 2
ROWS = 384
COLS = 768
BLK = 96
NB = COLS // BLK
NSAMP = 6144
LOGN = math.log(NSAMP)
SCALE = 1.0 / (WIDTH * EPS)
CH = 4
CW = HALF // CH


def split(v):
    hi = v.astype(BF16)
    return hi, (v - hi.astype(F32)).astype(BF16)


def dot_nt(a, b):
    return lax.dot_general(a, b, (((1,), (1,)), ((), ())), preferred_element_type=F32)


def dot_nn(a, b):
    return lax.dot_general(a, b, (((1,), (0,)), ((), ())), preferred_element_type=F32)


def pack_block(k, val):
    v3 = val.reshape(12, 8, 1)
    lane = lax.broadcasted_iota(jnp.int32, (12, 8, 128), 2)
    lead = lax.broadcasted_iota(jnp.int32, (12, 8, 128), 0) + 12 * k
    return jnp.sum(jnp.where(lane == lead, v3, 0.0), axis=0)


def unpack(packed, first, count):
    lane = lax.broadcasted_iota(jnp.int32, (count, 8, 128), 2)
    lead = lax.broadcasted_iota(jnp.int32, (count, 8, 128), 0) + first
    v3 = jnp.sum(jnp.where(lane == lead, packed[None], 0.0), axis=2, keepdims=True)
    return v3.reshape(8 * count, 1)


def to_row(col):
    r = lax.broadcasted_iota(jnp.int32, (128, 128), 0)
    c = lax.broadcasted_iota(jnp.int32, (128, 128), 1)
    return jnp.sum(jnp.where(r == c, col, 0.0), axis=0, keepdims=True)


def packed_row(packed):
    return jnp.concatenate([to_row(unpack(packed, 16 * q, 16)) for q in range(6)], axis=1)


def rows3(v):
    return [v[:, 128 * q : 128 * q + 128] for q in range(3)]


def flat3(v):
    return jnp.concatenate([v[q : q + 1] for q in range(3)], axis=1)


def kernel(
    x_hbm, y_hbm, t_out, f_out, g_out,
    xb, yb, xh, xl, yh_, yl_, xs, rsq, ps, pr, lg, lo, q_, pn, po, wh, wl, tp, r1, r2, pf,
    rx, cx1, cx, go, vo,
    loc, xr, yr, yr2, prs, lsem, rxs, cx1s, cxs, gs, r1s, r2s, pfs, ssem,
):
    n = lax.axis_index("noise")
    d = lax.axis_index("dp")
    core = lax.rem(n, 2)
    z = lax.rem(n // 2, 4)
    yhi = n // 8
    x = lax.rem(d, 4)
    ylo = d // 4
    h = lax.rem(yhi + ylo, 2)

    def at_z(k):
        return lax.rem(z + k, 4)

    def at_x(k):
        return lax.rem(x + k, 4)

    sib = (n + 1 - 2 * core, d)
    pa = (n, (1 - ylo) * 4 + x)
    pb = (((1 - yhi) * 4 + z) * 2 + core, (1 - ylo) * 4 + x)
    zp = ((yhi * 4 + at_z(1)) * 2 + core, d)
    zm = ((yhi * 4 + at_z(3)) * 2 + core, d)
    xp = (n, ylo * 4 + at_x(1))
    xm = (n, ylo * 4 + at_x(3))

    SRC = {"o": (yhi, ylo), "a": (yhi, 1 - ylo), "b": (1 - yhi, 1 - ylo), "c": (1 - yhi, ylo)}

    def slot(dz, who):
        hi, low = SRC[who]
        return low * 8 + hi * 4 + at_z(dz)

    kmine = pl.ds(pl.multiple_of(h * HALF, HALF), HALF)
    kother = pl.ds(pl.multiple_of((1 - h) * HALF, HALF), HALF)

    cx_own = pltpu.make_async_copy(x_hbm.at[:, kmine], xb.at[d], loc.at[0])
    cy_own = pltpu.make_async_copy(y_hbm.at[:, kmine], yb.at[slot(0, "o"), core], loc.at[1])
    cx_own.start()
    cy_own.start()

    barrier = pltpu.get_barrier_semaphore()

    def greet_dp(k, c):
        pl.semaphore_signal(barrier, inc=1, device_id=(n, lax.rem(d + k, 8)), device_id_type=MESH)
        return c

    def greet_noise(k, c):
        pl.semaphore_signal(barrier, inc=1, device_id=(lax.rem(n + k, 16), d), device_id_type=MESH)
        return c

    lax.fori_loop(1, 8, greet_dp, 0)
    lax.fori_loop(1, 16, greet_noise, 0)
    pl.semaphore_signal(barrier, inc=1, device_id=pb, device_id_type=MESH)
    pl.semaphore_wait(barrier, 23)

    sent = []

    def send(src, dst, rsem, dev):
        c = pltpu.make_async_remote_copy(
            src_ref=src, dst_ref=dst, send_sem=ssem.at[len(sent)], recv_sem=rsem, device_id=dev, device_id_type=MESH
        )
        c.start()
        sent.append(c)
        return c

    def arrived(dst, rsem):
        pltpu.make_async_remote_copy(
            src_ref=dst, dst_ref=dst, send_sem=ssem.at[0], recv_sem=rsem, device_id=sib, device_id_type=MESH
        ).wait_recv()

    def send_y(s, dev):
        return send(yb.at[s, core], yb.at[s, core], yr.at[s], dev)

    def cross_y(s):
        send(yb.at[s, core], yb.at[s, core], yr2.at[s], sib)

    def got_y(s):
        arrived(yb.at[s, core], yr.at[s])
        cross_y(s)

    def send_x(i, dev):
        return send(xb.at[i], xb.at[i], xr.at[i], dev)

    def got_x(i):
        arrived(xb.at[i], xr.at[i])

    xa = (1 - ylo) * 4
    xo = ylo * 4

    to_a = send(x_hbm.at[:, kother], xb.at[d], xr.at[d], pa)
    cx_own.wait()
    send_x(d, xp)
    send_x(d, xm)
    cy_own.wait()
    s = slot(0, "o")
    send_y(s, zp)
    send_y(s, zm)
    send_y(s, pb)
    cross_y(s)

    got_x(xa + x)
    send_x(xa + x, xp)
    send_x(xa + x, xm)
    to_a.wait_send()
    sent.remove(to_a)
    sent.append(None)
    send(y_hbm.at[:, kother], yb.at[slot(0, "o"), core], yr.at[slot(0, "o")], pa)
    got_y(slot(3, "o"))
    send_y(slot(3, "o"), zp)
    got_y(slot(0, "b"))
    send_y(slot(0, "b"), zm)
    got_y(slot(1, "o"))
    got_x(xo + at_x(1))
    got_x(xo + at_x(3))

    got_y(slot(0, "a"))
    send_y(slot(0, "a"), zp)
    send_y(slot(0, "a"), zm)
    send_y(slot(0, "a"), pb)
    got_x(xa + at_x(1))
    send_x(xo + at_x(3), xp)
    send_x(xa + at_x(1), xm)
    got_x(xa + at_x(3))
    got_y(slot(2, "o"))
    got_y(slot(1, "b"))

    def split_x(i, c):
        v = xb[i]
        hi, low = split(v)
        at = pl.ds(pl.multiple_of(i * OWN, OWN), OWN)
        xh[at, :] = hi
        xl[at, :] = low
        xs[at, :] = jnp.broadcast_to(jnp.sum(v * v, axis=1, keepdims=True), (OWN, 128))
        return c

    got_y(slot(0, "c"))
    got_y(slot(3, "a"))
    got_y(slot(1, "a"))
    send_y(slot(1, "a"), zm)
    send_y(slot(0, "b"), zp)
    send_y(slot(2, "o"), pb)
    got_x(xo + at_x(2))
    got_x(xa + at_x(2))
    lax.fori_loop(0, 8, split_x, 0)
    r = lax.broadcasted_iota(jnp.int32, (128, 128), 0)
    c = lax.broadcasted_iota(jnp.int32, (128, 128), 1)
    for i in range(3):
        piece = jnp.sum(jnp.where(r == c, xs[128 * i : 128 * i + 128, :], 0.0), axis=0, keepdims=True)
        rsq[:, 128 * i : 128 * i + 128] = jnp.broadcast_to(piece, (8, 128))

    def block(s):
        arrived(yb.at[s, 1 - core], yr2.at[s])
        v = yb[s].reshape(BLK, HALF)
        hi, low = split(v)
        at = pl.ds(pl.multiple_of(s * BLK, BLK), BLK)
        yh_[at, :] = hi
        yl_[at, :] = low
        csq = jnp.sum(v * v, axis=1, keepdims=True)
        both = dot_nt(jnp.concatenate([hi, low], axis=0), xh[...])
        cross = both[:BLK] + both[BLK:] + dot_nt(hi, xl[...])
        return (2.0 * cross - csq - rsq[0:1, :]) * SCALE

    def pair_block(dz, is_b, idx):
        hi = is_b * (1 - yhi) + (1 - is_b) * yhi
        k = hi * 4 + at_z(dz)
        ps[k] = block((1 - ylo) * 8 + k)
        pltpu.make_async_remote_copy(
            src_ref=ps.at[k], dst_ref=pr.at[k], send_sem=prs.at[0, k], recv_sem=prs.at[1, k], device_id=pa, device_id_type=MESH
        ).start()

    def own_block(dz, is_c):
        hi = is_c * (1 - yhi) + (1 - is_c) * yhi
        k = hi * 4 + at_z(dz)
        lg[pl.ds(pl.multiple_of(k * BLK, BLK), BLK), :] = block(ylo * 8 + k)

    def group1(i, c):
        pair_block(i // 2 + i // 4, (1 - lax.rem(i, 2)) * (1 - i // 4), i)
        return c

    def group2(i, c):
        pair_block(2 + lax.rem(i, 2), (i + 1) // 2, i)
        return c

    def group3(i, c):
        own_block(lax.rem(i, 4), i // 4)
        return c

    def group4(i, c):
        own_block(i + 1, 1)
        return c

    lax.fori_loop(0, 5, group1, 0)
    got_y(slot(2, "a"))
    send_y(slot(2, "a"), pb)
    send_y(slot(0, "c"), zp)
    send_y(slot(0, "c"), zm)
    got_y(slot(3, "b"))
    got_y(slot(2, "b"))
    lax.fori_loop(0, 3, group2, 0)
    lax.fori_loop(0, 5, group3, 0)
    got_y(slot(1, "c"))
    got_y(slot(3, "c"))
    got_y(slot(2, "c"))
    lax.fori_loop(0, 3, group4, 0)

    def pair_wait(k, c):
        d = pltpu.make_async_remote_copy(
            src_ref=ps.at[k], dst_ref=pr.at[k], send_sem=prs.at[0, k], recv_sem=prs.at[1, k], device_id=pa, device_id_type=MESH
        )
        d.wait_recv()
        d.wait_send()
        at = pl.ds(pl.multiple_of(k * BLK, BLK), BLK)
        lg[at, :] = lg[at, :] + pr[k]
        return c

    lax.fori_loop(0, NB, pair_wait, 0)
    send(lg, lo, lsem, pa)

    def ex_rows(rnd, msg):
        rx[rnd, d] = msg

        def go_(k, c):
            p = lax.rem(d + k, 8)
            pltpu.make_async_remote_copy(
                src_ref=rx.at[rnd, d], dst_ref=rx.at[rnd, d], send_sem=rxs.at[0, rnd, p], recv_sem=rxs.at[1, rnd, d],
                device_id=(n, p), device_id_type=MESH,
            ).start()
            return c

        lax.fori_loop(1, 8, go_, 0)

        def done():
            def wt(k, c):
                p = lax.rem(d + k, 8)
                w = pltpu.make_async_remote_copy(
                    src_ref=rx.at[rnd, p], dst_ref=rx.at[rnd, p], send_sem=rxs.at[0, rnd, p], recv_sem=rxs.at[1, rnd, p],
                    device_id=(n, p), device_id_type=MESH,
                )
                w.wait_recv()
                return c

            lax.fori_loop(1, 8, wt, 0)
            return rx[rnd]

        return done

    def ex_cols(buf, sem, msg, rnd):
        buf[rnd, n] = msg

        def go_(k, c):
            p = lax.rem(n + k, 16)
            pltpu.make_async_remote_copy(
                src_ref=buf.at[rnd, n], dst_ref=buf.at[rnd, n], send_sem=sem.at[0, rnd, p], recv_sem=sem.at[1, rnd, n],
                device_id=(p, d), device_id_type=MESH,
            ).start()
            return c

        lax.fori_loop(1, 16, go_, 0)

        def done():
            def wt(k, c):
                p = lax.rem(n + k, 16)
                pltpu.make_async_remote_copy(
                    src_ref=buf.at[rnd, p], dst_ref=buf.at[rnd, p], send_sem=sem.at[0, rnd, p], recv_sem=sem.at[1, rnd, p],
                    device_id=(p, d), device_id_type=MESH,
                ).wait_recv()
                return c

            lax.fori_loop(1, 16, wt, 0)
            return buf[rnd]

        return done

    def row_msg(parts):
        parts = parts + [jnp.zeros((1, 128), F32)] * (8 - len(parts))
        return jnp.concatenate(parts, axis=0)

    def blk(k):
        return slice(BLK * k, BLK * k + BLK)

    def col_max(values):
        m = values[0:8]
        for i in range(1, values.shape[0] // 8):
            m = jnp.maximum(m, values[8 * i : 8 * i + 8])
        return m

    m8 = None
    for k in range(NB):
        piece = jnp.max(lg[blk(k), :].reshape(12, 8, ROWS), axis=0)
        m8 = piece if m8 is None else jnp.maximum(m8, piece)
    m = jnp.max(m8, axis=0, keepdims=True)
    s8 = jnp.zeros((8, ROWS), F32)
    for k in range(NB):
        s8 = s8 + jnp.sum(jnp.exp(lg[blk(k), :] - m).reshape(12, 8, ROWS), axis=0)
    tot = jnp.sum(s8, axis=0, keepdims=True)
    everyone = ex_rows(0, row_msg(rows3(m) + rows3(tot)))()
    mm = everyone[:, 0:3, :]
    top = jnp.max(mm, axis=0)
    tt = jnp.sum(everyone[:, 3:6, :] * jnp.exp(mm - top[None]), axis=0)
    f1 = flat3(LOGN - top - jnp.log(tt))

    pm = jnp.zeros((8, 128), F32)
    pt = jnp.zeros((8, 128), F32)
    for k in range(NB):
        a = lg[blk(k), :] + f1
        cm = jnp.max(a, axis=1, keepdims=True)
        ct = jnp.sum(jnp.exp(a - cm), axis=1, keepdims=True)
        pm = pm + pack_block(k, cm)
        pt = pt + pack_block(k, ct)
    everyone = ex_cols(cx1, cx1s, jnp.concatenate([pm, pt], axis=0), 0)()
    mm = everyone[:, 0:8, :]
    top = jnp.max(mm, axis=0)
    tt = jnp.sum(everyone[:, 8:16, :] * jnp.exp(mm - top[None]), axis=0)
    used = lax.broadcasted_iota(jnp.int32, (8, 128), 1) < 96
    g1 = jnp.where(used, LOGN - top - jnp.log(jnp.where(used, tt, 1.0)), 0.0)
    go[0] = g1
    send(go.at[0], go.at[1], gs.at[0], pa)

    s8 = jnp.zeros((8, ROWS), F32)
    for k in range(NB):
        p = jnp.exp(lg[blk(k), :] + f1 + unpack(g1, 12 * k, 12))
        q_[blk(k), :] = p
        s8 = s8 + jnp.sum(p.reshape(12, 8, ROWS), axis=0)

    def row_step(rnd, s8, between):
        done = ex_rows(rnd, row_msg(rows3(jnp.sum(s8, axis=0, keepdims=True))))
        between()
        return flat3(NSAMP / jnp.sum(done()[:, 0:3, :], axis=0))

    def col_step(rnd, u, between):
        pk = jnp.zeros((8, 128), F32)
        for k in range(NB):
            pk = pk + pack_block(k, jnp.sum(q_[blk(k), :] * u, axis=1, keepdims=True))
        done = ex_cols(cx, cxs, pk, rnd)
        between()
        tt = jnp.sum(done(), axis=0)
        return NSAMP / jnp.where(used, tt, 1.0)

    def row_sums(v):
        s8 = jnp.zeros((8, ROWS), F32)
        for k in range(NB):
            s8 = s8 + jnp.sum((q_[blk(k), :] * unpack(v, 12 * k, 12)).reshape(12, 8, ROWS), axis=0)
        return s8

    def turn(src, dst, some):
        for q in some:
            dst[:, 128 * q : 128 * q + 128] = src[128 * q : 128 * q + 128, :].T

    u = row_step(1, s8, lambda: turn(q_, pn, range(0, 3)))
    v = col_step(0, u, lambda: turn(q_, pn, range(3, 6)))
    u = row_step(2, row_sums(v), lambda: None)

    def other_half():
        arrived(lo, lsem)
        arrived(go.at[1], gs.at[0])
        g2 = go[1]
        for k in range(6):
            at = slice(128 * k, 128 * k + 128)
            po[:, at] = jnp.exp(lo[at, :] + f1 + unpack(g2, 16 * k, 16)).T

    v = col_step(1, u, other_half)
    vo[0] = v
    send(vo.at[0], vo.at[1], gs.at[1], pa)
    total = ex_rows(3, row_msg(rows3(jnp.sum(row_sums(v), axis=0, keepdims=True))))

    hi, low = split(pn[...] * packed_row(v))
    wh[0] = hi
    wl[0] = low

    own_rows = pl.ds(pl.multiple_of(ylo * COLS, COLS), COLS)
    far_rows = pl.ds(pl.multiple_of((1 - ylo) * COLS, COLS), COLS)

    def part(i, rows, cols):
        return (
            dot_nn(wh[i], yh_[rows, cols]) + dot_nn(wh[i], yl_[rows, cols]) + dot_nn(wl[i], yh_[rows, cols])
        )

    def cols_of(c):
        return slice(CW * c, CW * c + CW)

    def compute(c):
        t = part(0, own_rows, cols_of(c))
        if c == 0:
            arrived(vo.at[1], gs.at[1])
            hi, low = split(po[...] * packed_row(vo[1]))
            wh[1] = hi
            wl[1] = low
        t = t + part(1, far_rows, cols_of(c))
        tp[c] = t.reshape(8, OWN, CW)

    def hop1(c):
        send(tp.at[c, xa + at_x(2)], r1.at[c, 0], r1s.at[c, 0], xp)
        send(tp.at[c, xo + at_x(2)], r1.at[c, 1], r1s.at[c, 1], xm)

    def hop2(c):
        send(tp.at[c, xa + at_x(3)], r2.at[c, 0], r2s.at[c, 0], xm)
        arrived(r1.at[c, 0], r1s.at[c, 0])
        tp[c, xa + at_x(1)] = tp[c, xa + at_x(1)] + r1[c, 0]
        send(tp.at[c, xa + at_x(1)], r2.at[c, 1], r2s.at[c, 1], xp)
        arrived(r1.at[c, 1], r1s.at[c, 1])
        tp[c, xo + at_x(3)] = tp[c, xo + at_x(3)] + r1[c, 1]
        send(tp.at[c, xo + at_x(3)], r2.at[c, 2], r2s.at[c, 2], xm)
        send(tp.at[c, xo + at_x(1)], r2.at[c, 3], r2s.at[c, 3], xp)

    def final_pair(c):
        arrived(r2.at[c, 0], r2s.at[c, 0])
        arrived(r2.at[c, 1], r2s.at[c, 1])
        tp[c, xa + x] = tp[c, xa + x] + r2[c, 0] + r2[c, 1]
        send(tp.at[c, xa + x], pf.at[c], pfs.at[c], pa)

    compute(0)
    hop1(0)
    compute(1)
    hop1(1)
    hop2(0)
    compute(2)
    hop1(2)
    hop2(1)
    compute(3)
    hop1(3)
    final_pair(0)
    hop2(2)
    final_pair(1)
    hop2(3)

    fin = flat3(jnp.sum(total()[:, 0:3, :], axis=0))
    lane = lax.broadcasted_iota(jnp.int32, (OWN, ROWS), 1)
    row = lax.broadcasted_iota(jnp.int32, (OWN, ROWS), 0) + d * OWN
    norm = 1.0 / jnp.sum(jnp.where(lane == row, fin, 0.0), axis=1, keepdims=True)
    f_out[...] = EPS * (f1 + jnp.log(u))
    g_out[...] = EPS * packed_row(g1 + jnp.log(v))

    for c in range(2, CH):
        final_pair(c)
    for c in range(CH):
        arrived(r2.at[c, 2], r2s.at[c, 2])
        arrived(r2.at[c, 3], r2s.at[c, 3])
        t = tp[c, xo + x] + r2[c, 2] + r2[c, 3]
        t_out[:, pl.ds(pl.multiple_of(h * HALF + c * CW, CW), CW)] = t * norm
    for c in range(CH):
        arrived(pf.at[c], pfs.at[c])
        t_out[:, pl.ds(pl.multiple_of((1 - h) * HALF + c * CW, CW), CW)] = pf[c] * norm

    for cp in sent:
        if cp is not None:
            cp.wait_send()

    def drain_rows(k, c):
        p = lax.rem(d + k, 8)
        for rnd in range(4):
            pltpu.make_async_remote_copy(
                src_ref=rx.at[rnd, d], dst_ref=rx.at[rnd, d], send_sem=rxs.at[0, rnd, p], recv_sem=rxs.at[1, rnd, d],
                device_id=(n, p), device_id_type=MESH,
            ).wait_send()
        return c

    def drain_cols(k, c):
        p = lax.rem(n + k, 16)
        for buf, sem, rnd in ((cx1, cx1s, 0), (cx, cxs, 0), (cx, cxs, 1)):
            pltpu.make_async_remote_copy(
                src_ref=buf.at[rnd, n], dst_ref=buf.at[rnd, n], send_sem=sem.at[0, rnd, p], recv_sem=sem.at[1, rnd, n],
                device_id=(p, d), device_id_type=MESH,
            ).wait_send()
        return c

    lax.fori_loop(1, 8, drain_rows, 0)
    lax.fori_loop(1, 16, drain_cols, 0)


def body(noise_latents, data_latents):
    dma = pltpu.SemaphoreType.DMA
    vm = pltpu.VMEM
    scratch = [
        vm((8, OWN, HALF), F32),
        vm((16, 2, OWN, HALF), F32),
        vm((ROWS, HALF), BF16),
        vm((ROWS, HALF), BF16),
        vm((2 * COLS, HALF), BF16),
        vm((2 * COLS, HALF), BF16),
        vm((ROWS, 128), F32),
        vm((8, ROWS), F32),
        vm((NB, BLK, ROWS), F32),
        vm((NB, BLK, ROWS), F32),
        vm((COLS, ROWS), F32),
        vm((COLS, ROWS), F32),
        vm((COLS, ROWS), F32),
        vm((ROWS, COLS), F32),
        vm((ROWS, COLS), F32),
        vm((2, ROWS, COLS), BF16),
        vm((2, ROWS, COLS), BF16),
        vm((CH, 8, OWN, CW), F32),
        vm((CH, 2, OWN, CW), F32),
        vm((CH, 4, OWN, CW), F32),
        vm((CH, OWN, CW), F32),
        vm((4, 8, 8, 128), F32),
        vm((1, 16, 16, 128), F32),
        vm((2, 16, 8, 128), F32),
        vm((2, 8, 128), F32),
        vm((2, 8, 128), F32),
        dma((2,)),
        dma((8,)),
        dma((16,)),
        dma((16,)),
        dma((2, NB)),
        dma,
        dma((2, 4, 8)),
        dma((2, 1, 16)),
        dma((2, 2, 16)),
        dma((2,)),
        dma((CH, 2)),
        dma((CH, 4)),
        dma((CH,)),
        dma((96,)),
    ]
    t, f, g = pl.pallas_call(
        kernel,
        out_shape=(
            jax.ShapeDtypeStruct((OWN, WIDTH), F32),
            jax.ShapeDtypeStruct((1, ROWS), F32),
            jax.ShapeDtypeStruct((1, COLS), F32),
        ),
        in_specs=[pl.BlockSpec(memory_space=pl.ANY)] * 2,
        out_specs=(pl.BlockSpec(memory_space=pltpu.VMEM),) * 3,
        scratch_shapes=scratch,
        compiler_params=pltpu.CompilerParams(
            collective_id=0, has_side_effects=True, vmem_limit_bytes=60 * 2**20
        ),
        name="coupling",
    )(noise_latents, data_latents)
    return t, f.reshape(ROWS), g.reshape(COLS)


def solution(mesh):
    placed = (P(("noise", "dp"), None), P(("dp", "noise"), None))
    return jax.shard_map(
        body,
        mesh=mesh,
        in_specs=placed,
        out_specs=(P(("noise", "dp"), None), P("noise"), P("dp")),
        check_vma=False,
    )
```

```python
import functools
import math

import jax
import jax.numpy as jnp
from jax import lax
from jax.experimental import pallas as pl
from jax.experimental.pallas import tpu as pltpu
from jax.sharding import PartitionSpec as P

MESH = pl.DeviceIdType.MESH
F32 = jnp.float32
BF16 = jnp.bfloat16
EPS = 0.01

OWN = 48
WIDTH = 4096
HALF = WIDTH // 2
ROWS = 384
COLS = 768
BLK = 96
NB = COLS // BLK
PIECE = OWN // 2
LO_AT = (0, 320, 576, 768)
NSAMP = 6144
LOGN = math.log(NSAMP)
SCALE = 1.0 / (WIDTH * EPS)
CH = 4
CW = HALF // CH


def split(v):
    hi = v.astype(BF16)
    return hi, (v - hi.astype(F32)).astype(BF16)


def dot_nt(a, b):
    return lax.dot_general(a, b, (((1,), (1,)), ((), ())), preferred_element_type=F32)


def dot_nn(a, b):
    return lax.dot_general(a, b, (((1,), (0,)), ((), ())), preferred_element_type=F32)


def pack_block(k, val):
    v3 = val.reshape(12, 8, 1)
    lane = lax.broadcasted_iota(jnp.int32, (12, 8, 128), 2)
    lead = lax.broadcasted_iota(jnp.int32, (12, 8, 128), 0) + 12 * k
    return jnp.sum(jnp.where(lane == lead, v3, 0.0), axis=0)


def unpack(packed, first, count):
    lane = lax.broadcasted_iota(jnp.int32, (count, 8, 128), 2)
    lead = lax.broadcasted_iota(jnp.int32, (count, 8, 128), 0) + first
    v3 = jnp.sum(jnp.where(lane == lead, packed[None], 0.0), axis=2, keepdims=True)
    return v3.reshape(8 * count, 1)


def to_row(col):
    r = lax.broadcasted_iota(jnp.int32, (128, 128), 0)
    c = lax.broadcasted_iota(jnp.int32, (128, 128), 1)
    return jnp.sum(jnp.where(r == c, col, 0.0), axis=0, keepdims=True)


def packed_row(packed):
    return jnp.concatenate([to_row(unpack(packed, 16 * q, 16)) for q in range(6)], axis=1)


def rows3(v):
    return [v[:, 128 * q : 128 * q + 128] for q in range(3)]


def flat3(v):
    return jnp.concatenate([v[q : q + 1] for q in range(3)], axis=1)


def kernel(
    x_hbm, y_hbm, t_out, f_out, g_out,
    xb, yb, xh, xl, yh_, yl_, xs, rsq, ps, pr, lg, lo, q_, pn, po, wh, wl, tp, r1, r2, pf,
    rx, cx1, cx, go, vo,
    loc, xr, yr, yr2, prs, lsem, rxs, cx1s, cxs, gs, r1s, r2s, pfs, ssem,
):
    n = lax.axis_index("noise")
    d = lax.axis_index("dp")
    core = lax.rem(n, 2)
    z = lax.rem(n // 2, 4)
    yhi = n // 8
    x = lax.rem(d, 4)
    ylo = d // 4
    h = lax.rem(yhi + ylo, 2)

    def at_z(k):
        return lax.rem(z + k, 4)

    def at_x(k):
        return lax.rem(x + k, 4)

    sib = (n + 1 - 2 * core, d)
    pa = (n, (1 - ylo) * 4 + x)
    pb = (((1 - yhi) * 4 + z) * 2 + core, (1 - ylo) * 4 + x)
    zp = ((yhi * 4 + at_z(1)) * 2 + core, d)
    zm = ((yhi * 4 + at_z(3)) * 2 + core, d)
    xp = (n, ylo * 4 + at_x(1))
    xm = (n, ylo * 4 + at_x(3))

    SRC = {"o": (yhi, h), "a": (yhi, 1 - h), "b": (1 - yhi, h), "c": (1 - yhi, 1 - h)}

    def slot(dz, who):
        hi, tile = SRC[who]
        return tile * 8 + hi * 4 + at_z(dz)

    def col_dev(p):
        return (p, lax.rem(p // 8 + h, 2) * 4 + x)

    kmine = pl.ds(pl.multiple_of(h * HALF, HALF), HALF)
    kother = pl.ds(pl.multiple_of((1 - h) * HALF, HALF), HALF)

    cx_own = [
        pltpu.make_async_copy(x_hbm.at[pl.ds(k * PIECE, PIECE), kmine], xb.at[d, k], loc.at[0, k]) for k in range(2)
    ]
    cy_own = [
        pltpu.make_async_copy(y_hbm.at[pl.ds(k * PIECE, PIECE), kmine], yb.at[slot(0, "o"), core, k], loc.at[1, k])
        for k in range(2)
    ]
    for cp in cx_own + cy_own:
        cp.start()

    barrier = pltpu.get_barrier_semaphore()

    def greet_dp(k, c):
        pl.semaphore_signal(barrier, inc=1, device_id=(n, lax.rem(d + k, 8)), device_id_type=MESH)
        return c

    def greet_noise(k, c):
        pl.semaphore_signal(barrier, inc=1, device_id=col_dev(lax.rem(n + k, 16)), device_id_type=MESH)
        return c

    lax.fori_loop(1, 8, greet_dp, 0)
    lax.fori_loop(1, 16, greet_noise, 0)
    pl.semaphore_wait(barrier, 22)

    sent = []

    def send(src, dst, rsem, dev):
        c = pltpu.make_async_remote_copy(
            src_ref=src, dst_ref=dst, send_sem=ssem.at[len(sent)], recv_sem=rsem, device_id=dev, device_id_type=MESH
        )
        c.start()
        sent.append(c)
        return c

    def arrived(dst, rsem):
        pltpu.make_async_remote_copy(
            src_ref=dst, dst_ref=dst, send_sem=ssem.at[0], recv_sem=rsem, device_id=sib, device_id_type=MESH
        ).wait_recv()

    def send_y(s, k, dev):
        send(yb.at[s, core, k], yb.at[s, core, k], yr.at[s, k], dev)

    def cross_y(s, k):
        send(yb.at[s, core, k], yb.at[s, core, k], yr2.at[s, k], sib)

    def got_y(s, k):
        arrived(yb.at[s, core, k], yr.at[s, k])
        cross_y(s, k)

    def send_x(i, k, dev):
        send(xb.at[i, k], xb.at[i, k], xr.at[i, k], dev)

    def got_x(i, k):
        arrived(xb.at[i, k], xr.at[i, k])

    xa = (1 - ylo) * 4
    xo = ylo * 4

    for k in range(2):
        send(x_hbm.at[pl.ds(k * PIECE, PIECE), kother], xb.at[d, k], xr.at[d, k], pa)
    for k in range(2):
        mine = slot(0, "o")
        send(y_hbm.at[pl.ds(k * PIECE, PIECE), kother], yb.at[mine, core, k], yr.at[mine, k], pa)
    for k in range(2):
        cx_own[k].wait()
        send_x(d, k, xp)
        send_x(d, k, xm)
        cy_own[k].wait()
        send_y(mine, k, zp)
        send_y(mine, k, zm)
        send_y(mine, k, pb)
        cross_y(mine, k)

    for k in range(2):
        got_x(xa + x, k)
        send_x(xa + x, k, xp)
        send_x(xa + x, k, xm)
        got_y(slot(3, "o"), k)
        send_y(slot(3, "o"), k, zp)
        got_y(slot(0, "b"), k)
        send_y(slot(0, "b"), k, zm)
        got_y(slot(1, "o"), k)
        got_x(xo + at_x(1), k)
        got_x(xo + at_x(3), k)
        send_x(xo + at_x(3), k, xp)

    for k in range(2):
        got_y(slot(0, "a"), k)
        send_y(slot(0, "a"), k, zp)
        send_y(slot(0, "a"), k, zm)
        send_y(slot(0, "a"), k, pb)
        got_x(xa + at_x(1), k)
        send_x(xa + at_x(1), k, xm)
        got_x(xa + at_x(3), k)
        got_y(slot(2, "o"), k)
        got_y(slot(1, "b"), k)
    for k in range(2):
        send_y(slot(2, "o"), k, pb)

    def split_x(i, c):
        v = xb[i].reshape(OWN, HALF)
        hi, low = split(v)
        at = pl.ds(pl.multiple_of(i * OWN, OWN), OWN)
        xh[at, :] = hi
        xl[at, :] = low
        xs[at, :] = jnp.broadcast_to(jnp.sum(v * v, axis=1, keepdims=True), (OWN, 128))
        return c

    for k in range(2):
        got_y(slot(0, "c"), k)
        send_y(slot(0, "c"), k, zp)
        got_y(slot(1, "a"), k)
        send_y(slot(1, "a"), k, zm)
        got_y(slot(3, "a"), k)
        got_x(xo + at_x(2), k)
        got_x(xa + at_x(2), k)
    for k in range(2):
        send_y(slot(0, "b"), k, zp)
        send_y(slot(0, "c"), k, zm)
    lax.fori_loop(0, 8, split_x, 0)
    r = lax.broadcasted_iota(jnp.int32, (128, 128), 0)
    c = lax.broadcasted_iota(jnp.int32, (128, 128), 1)
    for i in range(3):
        piece = jnp.sum(jnp.where(r == c, xs[128 * i : 128 * i + 128, :], 0.0), axis=0, keepdims=True)
        rsq[:, 128 * i : 128 * i + 128] = jnp.broadcast_to(piece, (8, 128))

    def block(s):
        for k in range(2):
            arrived(yb.at[s, 1 - core, k], yr2.at[s, k])
        v = yb[s].reshape(BLK, HALF)
        hi, low = split(v)
        at = pl.ds(pl.multiple_of(s * BLK, BLK), BLK)
        yh_[at, :] = hi
        yl_[at, :] = low
        csq = jnp.sum(v * v, axis=1, keepdims=True)
        both = dot_nt(jnp.concatenate([hi, low], axis=0), xh[...])
        cross = both[:BLK] + both[BLK:] + dot_nt(hi, xl[...])
        return (2.0 * cross - csq - rsq[0:1, :]) * SCALE

    def pair_block(dz, is_c):
        k = (is_c * (1 - yhi) + (1 - is_c) * yhi) * 4 + at_z(dz)
        ps[k] = block((1 - h) * 8 + k)
        pltpu.make_async_remote_copy(
            src_ref=ps.at[k], dst_ref=pr.at[k], send_sem=prs.at[0, k], recv_sem=prs.at[1, k], device_id=pa, device_id_type=MESH
        ).start()

    def own_block(dz, is_b):
        k = (is_b * (1 - yhi) + (1 - is_b) * yhi) * 4 + at_z(dz)
        lg[pl.ds(pl.multiple_of(k * BLK, BLK), BLK), :] = block(h * 8 + k)

    def group1(i, c):
        pair_block(lax.rem(i, 2) + 2 * (i // 3), lax.rem(i // 2 + i // 3, 2))
        return c

    def group2(i, c):
        pair_block(2 + i, i)
        return c

    def group3(i, c):
        own_block(lax.rem(i, 4), i // 4)
        return c

    def group4(i, c):
        pair_block(1 + i, 1)
        return c

    lax.fori_loop(0, 4, group1, 0)
    for k in range(2):
        got_y(slot(2, "a"), k)
        send_y(slot(2, "a"), k, pb)
        got_y(slot(3, "c"), k)
        got_y(slot(2, "b"), k)
    lax.fori_loop(0, 2, group2, 0)
    lax.fori_loop(0, 7, group3, 0)
    for k in range(2):
        got_y(slot(1, "c"), k)
        got_y(slot(2, "c"), k)
        got_y(slot(3, "b"), k)
    lax.fori_loop(0, 2, group4, 0)
    own_block(3, 1)

    def pair_wait(k, c):
        d = pltpu.make_async_remote_copy(
            src_ref=ps.at[k], dst_ref=pr.at[k], send_sem=prs.at[0, k], recv_sem=prs.at[1, k], device_id=pa, device_id_type=MESH
        )
        d.wait_recv()
        d.wait_send()
        at = pl.ds(pl.multiple_of(k * BLK, BLK), BLK)
        lg[at, :] = lg[at, :] + pr[k]
        return c

    lax.fori_loop(0, NB, pair_wait, 0)

    def send_logits(k):
        at = pl.ds(LO_AT[k], LO_AT[k + 1] - LO_AT[k])
        send(lg.at[at], lo.at[at], lsem.at[k], pa)

    def got_logits(k):
        at = pl.ds(LO_AT[k], LO_AT[k + 1] - LO_AT[k])
        arrived(lo.at[at], lsem.at[k])

    def ex_rows(rnd, msg):
        rx[rnd, d] = msg

        def go_(k, c):
            p = lax.rem(d + k, 8)
            pltpu.make_async_remote_copy(
                src_ref=rx.at[rnd, d], dst_ref=rx.at[rnd, d], send_sem=rxs.at[0, rnd, p], recv_sem=rxs.at[1, rnd, d],
                device_id=(n, p), device_id_type=MESH,
            ).start()
            return c

        lax.fori_loop(1, 8, go_, 0)

        def done():
            def wt(k, c):
                p = lax.rem(d + k, 8)
                w = pltpu.make_async_remote_copy(
                    src_ref=rx.at[rnd, p], dst_ref=rx.at[rnd, p], send_sem=rxs.at[0, rnd, p], recv_sem=rxs.at[1, rnd, p],
                    device_id=(n, p), device_id_type=MESH,
                )
                w.wait_recv()
                return c

            lax.fori_loop(1, 8, wt, 0)
            return rx[rnd]

        return done

    def ex_cols(buf, sem, msg, rnd):
        buf[rnd, n] = msg

        def go_(k, c):
            p = lax.rem(n + k, 16)
            pltpu.make_async_remote_copy(
                src_ref=buf.at[rnd, n], dst_ref=buf.at[rnd, n], send_sem=sem.at[0, rnd, p], recv_sem=sem.at[1, rnd, n],
                device_id=col_dev(p), device_id_type=MESH,
            ).start()
            return c

        lax.fori_loop(1, 16, go_, 0)

        def done():
            def wt(k, c):
                p = lax.rem(n + k, 16)
                pltpu.make_async_remote_copy(
                    src_ref=buf.at[rnd, p], dst_ref=buf.at[rnd, p], send_sem=sem.at[0, rnd, p], recv_sem=sem.at[1, rnd, p],
                    device_id=col_dev(p), device_id_type=MESH,
                ).wait_recv()
                return c

            lax.fori_loop(1, 16, wt, 0)
            return buf[rnd]

        return done

    def row_msg(parts):
        parts = parts + [jnp.zeros((1, 128), F32)] * (8 - len(parts))
        return jnp.concatenate(parts, axis=0)

    def blk(k):
        return slice(BLK * k, BLK * k + BLK)

    m8 = None
    for k in range(NB):
        piece = jnp.max(lg[blk(k), :].reshape(12, 8, ROWS), axis=0)
        m8 = piece if m8 is None else jnp.maximum(m8, piece)
    m = jnp.max(m8, axis=0, keepdims=True)
    s8 = jnp.zeros((8, ROWS), F32)
    for k in range(NB):
        s8 = s8 + jnp.sum(jnp.exp(lg[blk(k), :] - m).reshape(12, 8, ROWS), axis=0)
    tot = jnp.sum(s8, axis=0, keepdims=True)
    done = ex_rows(0, row_msg(rows3(m) + rows3(tot)))
    send_logits(0)
    everyone = done()
    mm = everyone[:, 0:3, :]
    top = jnp.max(mm, axis=0)
    tt = jnp.sum(everyone[:, 3:6, :] * jnp.exp(mm - top[None]), axis=0)
    f1 = flat3(LOGN - top - jnp.log(tt))

    pm = jnp.zeros((8, 128), F32)
    pt = jnp.zeros((8, 128), F32)
    for k in range(NB):
        a = lg[blk(k), :] + f1
        cm = jnp.max(a, axis=1, keepdims=True)
        ct = jnp.sum(jnp.exp(a - cm), axis=1, keepdims=True)
        pm = pm + pack_block(k, cm)
        pt = pt + pack_block(k, ct)
    everyone = ex_cols(cx1, cx1s, jnp.concatenate([pm, pt], axis=0), 0)()
    mm = everyone[:, 0:8, :]
    top = jnp.max(mm, axis=0)
    tt = jnp.sum(everyone[:, 8:16, :] * jnp.exp(mm - top[None]), axis=0)
    used = lax.broadcasted_iota(jnp.int32, (8, 128), 1) < 96
    g1 = jnp.where(used, LOGN - top - jnp.log(jnp.where(used, tt, 1.0)), 0.0)
    go[0] = g1
    send(go.at[0], go.at[1], gs.at[0], pa)

    s8 = jnp.zeros((8, ROWS), F32)
    for k in range(NB):
        p = jnp.exp(lg[blk(k), :] + f1 + unpack(g1, 12 * k, 12))
        q_[blk(k), :] = p
        s8 = s8 + jnp.sum(p.reshape(12, 8, ROWS), axis=0)

    def row_step(rnd, s8, between):
        done = ex_rows(rnd, row_msg(rows3(jnp.sum(s8, axis=0, keepdims=True))))
        between()
        return flat3(NSAMP / jnp.sum(done()[:, 0:3, :], axis=0))

    def col_step(rnd, u, between):
        pk = jnp.zeros((8, 128), F32)
        for k in range(NB):
            pk = pk + pack_block(k, jnp.sum(q_[blk(k), :] * u, axis=1, keepdims=True))
        done = ex_cols(cx, cxs, pk, rnd)
        between()
        tt = jnp.sum(done(), axis=0)
        return NSAMP / jnp.where(used, tt, 1.0)

    def row_sums(v):
        s8 = jnp.zeros((8, ROWS), F32)
        for k in range(NB):
            s8 = s8 + jnp.sum((q_[blk(k), :] * unpack(v, 12 * k, 12)).reshape(12, 8, ROWS), axis=0)
        return s8

    def turn(src, dst, some):
        for q in some:
            dst[:, 128 * q : 128 * q + 128] = src[128 * q : 128 * q + 128, :].T

    def far(some):
        for q in some:
            at = slice(128 * q, 128 * q + 128)
            po[:, at] = jnp.exp(lo[at, :] + f1 + unpack(go[1], 16 * q, 16)).T

    def in_row1():
        send_logits(1)
        turn(q_, pn, range(0, 3))

    def in_row2():
        send_logits(2)
        arrived(go.at[1], gs.at[0])
        got_logits(0)
        far(range(0, 2))

    def in_col2():
        got_logits(1)
        far(range(2, 4))
        got_logits(2)
        far(range(4, 6))

    u = row_step(1, s8, in_row1)
    v = col_step(0, u, lambda: turn(q_, pn, range(3, 6)))
    u = row_step(2, row_sums(v), in_row2)
    v = col_step(1, u, in_col2)
    vo[0] = v
    send(vo.at[0], vo.at[1], gs.at[1], pa)
    total = ex_rows(3, row_msg(rows3(jnp.sum(row_sums(v), axis=0, keepdims=True))))

    hi, low = split(pn[...] * packed_row(v))
    wh[0] = hi
    wl[0] = low

    own_rows = pl.ds(pl.multiple_of(h * COLS, COLS), COLS)
    far_rows = pl.ds(pl.multiple_of((1 - h) * COLS, COLS), COLS)

    def part(i, rows, cols):
        return (
            dot_nn(wh[i], yh_[rows, cols]) + dot_nn(wh[i], yl_[rows, cols]) + dot_nn(wl[i], yh_[rows, cols])
        )

    def cols_of(c):
        return slice(CW * c, CW * c + CW)

    def compute(c):
        t = part(0, own_rows, cols_of(c))
        if c == 0:
            arrived(vo.at[1], gs.at[1])
            hi, low = split(po[...] * packed_row(vo[1]))
            wh[1] = hi
            wl[1] = low
        t = t + part(1, far_rows, cols_of(c))
        tp[c] = t.reshape(8, OWN, CW)

    def start_pair(c):
        send(tp.at[c, xa + at_x(2)], r1.at[c, 0], r1s.at[c, 0], xp)
        send(tp.at[c, xa + at_x(3)], r2.at[c, 0], r2s.at[c, 0], xm)

    def pass_pair(c):
        arrived(r1.at[c, 0], r1s.at[c, 0])
        tp[c, xa + at_x(1)] = tp[c, xa + at_x(1)] + r1[c, 0]
        send(tp.at[c, xa + at_x(1)], r2.at[c, 1], r2s.at[c, 1], xp)

    def start_own(c):
        send(tp.at[c, xo + at_x(2)], r1.at[c, 1], r1s.at[c, 1], xm)
        send(tp.at[c, xo + at_x(1)], r2.at[c, 3], r2s.at[c, 3], xp)

    def pass_own(c):
        arrived(r1.at[c, 1], r1s.at[c, 1])
        tp[c, xo + at_x(3)] = tp[c, xo + at_x(3)] + r1[c, 1]
        send(tp.at[c, xo + at_x(3)], r2.at[c, 2], r2s.at[c, 2], xm)

    def final_pair(c):
        arrived(r2.at[c, 0], r2s.at[c, 0])
        arrived(r2.at[c, 1], r2s.at[c, 1])
        tp[c, xa + x] = tp[c, xa + x] + r2[c, 0] + r2[c, 1]
        send(tp.at[c, xa + x], pf.at[c], pfs.at[c], pa)

    for c in range(CH):
        compute(c)
        start_pair(c)
        if c:
            pass_pair(c - 1)
    pass_pair(CH - 1)
    for c in range(CH):
        start_own(c)

    fin = flat3(jnp.sum(total()[:, 0:3, :], axis=0))
    lane = lax.broadcasted_iota(jnp.int32, (OWN, ROWS), 1)
    row = lax.broadcasted_iota(jnp.int32, (OWN, ROWS), 0) + d * OWN
    norm = 1.0 / jnp.sum(jnp.where(lane == row, fin, 0.0), axis=1, keepdims=True)
    f_out[...] = EPS * (f1 + jnp.log(u))
    near = lax.broadcasted_iota(jnp.int32, (8, 128), 1) // 48 == yhi
    g_out[...] = EPS * packed_row(jnp.where(near, g1 + jnp.log(v), go[1] + jnp.log(vo[1])))

    for c in range(CH):
        final_pair(c)
        if c:
            pass_own(c - 1)
    pass_own(CH - 1)
    for c in range(CH):
        arrived(r2.at[c, 2], r2s.at[c, 2])
        arrived(r2.at[c, 3], r2s.at[c, 3])
        t = tp[c, xo + x] + r2[c, 2] + r2[c, 3]
        t_out[:, pl.ds(pl.multiple_of(h * HALF + c * CW, CW), CW)] = t * norm
    for c in range(CH):
        arrived(pf.at[c], pfs.at[c])
        t_out[:, pl.ds(pl.multiple_of((1 - h) * HALF + c * CW, CW), CW)] = pf[c] * norm

    for cp in sent:
        cp.wait_send()

    def drain_rows(k, c):
        p = lax.rem(d + k, 8)
        for rnd in range(4):
            pltpu.make_async_remote_copy(
                src_ref=rx.at[rnd, d], dst_ref=rx.at[rnd, d], send_sem=rxs.at[0, rnd, p], recv_sem=rxs.at[1, rnd, d],
                device_id=(n, p), device_id_type=MESH,
            ).wait_send()
        return c

    def drain_cols(k, c):
        p = lax.rem(n + k, 16)
        for buf, sem, rnd in ((cx1, cx1s, 0), (cx, cxs, 0), (cx, cxs, 1)):
            pltpu.make_async_remote_copy(
                src_ref=buf.at[rnd, n], dst_ref=buf.at[rnd, n], send_sem=sem.at[0, rnd, p], recv_sem=sem.at[1, rnd, n],
                device_id=col_dev(p), device_id_type=MESH,
            ).wait_send()
        return c

    lax.fori_loop(1, 8, drain_rows, 0)
    lax.fori_loop(1, 16, drain_cols, 0)


def body(noise_latents, data_latents):
    dma = pltpu.SemaphoreType.DMA
    vm = pltpu.VMEM
    scratch = [
        vm((8, 2, PIECE, HALF), F32),
        vm((16, 2, 2, PIECE, HALF), F32),
        vm((ROWS, HALF), BF16),
        vm((ROWS, HALF), BF16),
        vm((2 * COLS, HALF), BF16),
        vm((2 * COLS, HALF), BF16),
        vm((ROWS, 128), F32),
        vm((8, ROWS), F32),
        vm((NB, BLK, ROWS), F32),
        vm((NB, BLK, ROWS), F32),
        vm((COLS, ROWS), F32),
        vm((COLS, ROWS), F32),
        vm((COLS, ROWS), F32),
        vm((ROWS, COLS), F32),
        vm((ROWS, COLS), F32),
        vm((2, ROWS, COLS), BF16),
        vm((2, ROWS, COLS), BF16),
        vm((CH, 8, OWN, CW), F32),
        vm((CH, 2, OWN, CW), F32),
        vm((CH, 4, OWN, CW), F32),
        vm((CH, OWN, CW), F32),
        vm((4, 8, 8, 128), F32),
        vm((1, 16, 16, 128), F32),
        vm((2, 16, 8, 128), F32),
        vm((2, 8, 128), F32),
        vm((2, 8, 128), F32),
        dma((2, 2)),
        dma((8, 2)),
        dma((16, 2)),
        dma((16, 2)),
        dma((2, NB)),
        dma((3,)),
        dma((2, 4, 8)),
        dma((2, 1, 16)),
        dma((2, 2, 16)),
        dma((2,)),
        dma((CH, 2)),
        dma((CH, 4)),
        dma((CH,)),
        dma((160,)),
    ]
    t, f, g = pl.pallas_call(
        kernel,
        out_shape=(
            jax.ShapeDtypeStruct((OWN, WIDTH), F32),
            jax.ShapeDtypeStruct((1, ROWS), F32),
            jax.ShapeDtypeStruct((1, COLS), F32),
        ),
        in_specs=[pl.BlockSpec(memory_space=pl.ANY)] * 2,
        out_specs=(pl.BlockSpec(memory_space=pltpu.VMEM),) * 3,
        scratch_shapes=scratch,
        compiler_params=pltpu.CompilerParams(
            collective_id=0, has_side_effects=True, vmem_limit_bytes=60 * 2**20
        ),
        name="coupling",
    )(noise_latents, data_latents)
    return t, f.reshape(ROWS), g.reshape(COLS)


def solution(mesh):
    placed = (P(("noise", "dp"), None), P(("dp", "noise"), None))
    return jax.shard_map(
        body,
        mesh=mesh,
        in_specs=placed,
        out_specs=(P(("noise", "dp"), None), P("noise"), P("dp")),
        check_vma=False,
    )
```

```python
import functools
import math

import jax
import jax.numpy as jnp
from jax import lax
from jax.experimental import pallas as pl
from jax.experimental.pallas import tpu as pltpu
from jax.sharding import PartitionSpec as P

MESH = pl.DeviceIdType.MESH
F32 = jnp.float32
BF16 = jnp.bfloat16
EPS = 0.01

OWN = 48
WIDTH = 4096
HALF = WIDTH // 2
ROWS = 384
COLS = 768
BLK = 96
NB = COLS // BLK
PIECE = OWN // 2
LO_AT = (0, 320, 576, 768)
NSAMP = 6144
LOGN = math.log(NSAMP)
SCALE = 1.0 / (WIDTH * EPS)
CH = 8
CW = HALF // CH


def split(v):
    hi = v.astype(BF16)
    return hi, (v - hi.astype(F32)).astype(BF16)


def dot_nt(a, b):
    return lax.dot_general(a, b, (((1,), (1,)), ((), ())), preferred_element_type=F32)


def dot_nn(a, b):
    return lax.dot_general(a, b, (((1,), (0,)), ((), ())), preferred_element_type=F32)


def pack_block(k, val):
    v3 = val.reshape(12, 8, 1)
    lane = lax.broadcasted_iota(jnp.int32, (12, 8, 128), 2)
    lead = lax.broadcasted_iota(jnp.int32, (12, 8, 128), 0) + 12 * k
    return jnp.sum(jnp.where(lane == lead, v3, 0.0), axis=0)


def unpack(packed, first, count):
    lane = lax.broadcasted_iota(jnp.int32, (count, 8, 128), 2)
    lead = lax.broadcasted_iota(jnp.int32, (count, 8, 128), 0) + first
    v3 = jnp.sum(jnp.where(lane == lead, packed[None], 0.0), axis=2, keepdims=True)
    return v3.reshape(8 * count, 1)


def to_row(col):
    r = lax.broadcasted_iota(jnp.int32, (128, 128), 0)
    c = lax.broadcasted_iota(jnp.int32, (128, 128), 1)
    return jnp.sum(jnp.where(r == c, col, 0.0), axis=0, keepdims=True)


def packed_row(packed):
    return jnp.concatenate([to_row(unpack(packed, 16 * q, 16)) for q in range(6)], axis=1)


def rows3(v):
    return [v[:, 128 * q : 128 * q + 128] for q in range(3)]


def flat3(v):
    return jnp.concatenate([v[q : q + 1] for q in range(3)], axis=1)


def kernel(
    x_hbm, y_hbm, t_out, f_out, g_out,
    xb, yb, xh, xl, yh_, yl_, xs, cs, rsq, ps, pr, lg, lo, q_, pn, po, wh, wl, tp, r1, r2, pf,
    rx, cx1, cx, go, vo,
    loc, xr, yr, yr2, prs, lsem, rxs, cx1s, cxs, gs, r1s, r2s, pfs, ssem,
):
    n = lax.axis_index("noise")
    d = lax.axis_index("dp")
    core = lax.rem(n, 2)
    z = lax.rem(n // 2, 4)
    yhi = n // 8
    x = lax.rem(d, 4)
    ylo = d // 4
    h = lax.rem(yhi + ylo, 2)

    def at_z(k):
        return lax.rem(z + k, 4)

    def at_x(k):
        return lax.rem(x + k, 4)

    sib = (n + 1 - 2 * core, d)
    pa = (n, (1 - ylo) * 4 + x)
    pb = (((1 - yhi) * 4 + z) * 2 + core, (1 - ylo) * 4 + x)
    zp = ((yhi * 4 + at_z(1)) * 2 + core, d)
    zm = ((yhi * 4 + at_z(3)) * 2 + core, d)
    xp = (n, ylo * 4 + at_x(1))
    xm = (n, ylo * 4 + at_x(3))

    SRC = {"o": (yhi, h), "a": (yhi, 1 - h), "b": (1 - yhi, h), "c": (1 - yhi, 1 - h)}

    def slot(dz, who):
        hi, tile = SRC[who]
        return tile * 8 + hi * 4 + at_z(dz)

    def col_dev(p):
        return (p, lax.rem(p // 8 + h, 2) * 4 + x)

    kmine = pl.ds(pl.multiple_of(h * HALF, HALF), HALF)
    kother = pl.ds(pl.multiple_of((1 - h) * HALF, HALF), HALF)

    cx_own = [
        pltpu.make_async_copy(x_hbm.at[pl.ds(k * PIECE, PIECE), kmine], xb.at[d, k], loc.at[0, k]) for k in range(2)
    ]
    cy_own = [
        pltpu.make_async_copy(y_hbm.at[pl.ds(k * PIECE, PIECE), kmine], yb.at[slot(0, "o"), core, k], loc.at[1, k])
        for k in range(2)
    ]
    for cp in cx_own + cy_own:
        cp.start()

    barrier = pltpu.get_barrier_semaphore()

    for dev in (pa, pb, zp, zm, xp, xm, sib):
        pl.semaphore_signal(barrier, inc=1, device_id=dev, device_id_type=MESH)
    pl.semaphore_wait(barrier, 7)

    sent = []

    def send(src, dst, rsem, dev):
        c = pltpu.make_async_remote_copy(
            src_ref=src, dst_ref=dst, send_sem=ssem.at[len(sent)], recv_sem=rsem, device_id=dev, device_id_type=MESH
        )
        c.start()
        sent.append(c)
        return c

    def arrived(dst, rsem):
        pltpu.make_async_remote_copy(
            src_ref=dst, dst_ref=dst, send_sem=ssem.at[0], recv_sem=rsem, device_id=sib, device_id_type=MESH
        ).wait_recv()

    def send_y(s, k, dev):
        send(yb.at[s, core, k], yb.at[s, core, k], yr.at[s, k], dev)

    def cross_y(s, k):
        send(yb.at[s, core, k], yb.at[s, core, k], yr2.at[s, k], sib)

    def got_y(s, k):
        arrived(yb.at[s, core, k], yr.at[s, k])
        cross_y(s, k)

    def send_x(i, k, dev):
        send(xb.at[i, k], xb.at[i, k], xr.at[i, k], dev)

    def got_x(i, k):
        arrived(xb.at[i, k], xr.at[i, k])

    xa = (1 - ylo) * 4
    xo = ylo * 4

    def split_x(i):
        v = xb[i].reshape(OWN, HALF)
        hi, low = split(v)
        at = pl.ds(pl.multiple_of(i * OWN, OWN), OWN)
        xh[at, :] = hi
        xl[at, :] = low
        xs[at, :] = jnp.broadcast_to(jnp.sum(v * v, axis=1, keepdims=True), (OWN, 128))

    def split_xs(i, c):
        split_x(at_x(i))
        split_x(4 + at_x(i))
        return c

    def split_y(s):
        for k in range(2):
            arrived(yb.at[s, 1 - core, k], yr2.at[s, k])
        v = yb[s].reshape(BLK, HALF)
        hi, low = split(v)
        at = pl.ds(pl.multiple_of(s * BLK, BLK), BLK)
        yh_[at, :] = hi
        yl_[at, :] = low
        cs[at, :] = jnp.broadcast_to(jnp.sum(v * v, axis=1, keepdims=True), (BLK, 128))

    for k in range(2):
        send(x_hbm.at[pl.ds(k * PIECE, PIECE), kother], xb.at[d, k], xr.at[d, k], pa)
    for k in range(2):
        mine = slot(0, "o")
        send(y_hbm.at[pl.ds(k * PIECE, PIECE), kother], yb.at[mine, core, k], yr.at[mine, k], pa)
    for k in range(2):
        cx_own[k].wait()
        send_x(d, k, xp)
        send_x(d, k, xm)
        cy_own[k].wait()
        send_y(mine, k, zp)
        send_y(mine, k, zm)
        send_y(mine, k, pb)
        cross_y(mine, k)

    for k in range(2):
        got_x(xa + x, k)
        send_x(xa + x, k, xp)
        send_x(xa + x, k, xm)
        got_y(slot(3, "o"), k)
        send_y(slot(3, "o"), k, zp)
        got_y(slot(0, "b"), k)
        send_y(slot(0, "b"), k, zm)
        got_y(slot(1, "o"), k)
        got_x(xo + at_x(1), k)
        got_x(xo + at_x(3), k)
        send_x(xo + at_x(3), k, xp)

    lax.fori_loop(0, 1, split_xs, 0)

    for k in range(2):
        got_y(slot(0, "a"), k)
        send_y(slot(0, "a"), k, zp)
        send_y(slot(0, "a"), k, zm)
        send_y(slot(0, "a"), k, pb)
        got_x(xa + at_x(1), k)
        send_x(xa + at_x(1), k, xm)
        got_x(xa + at_x(3), k)
        got_y(slot(2, "o"), k)
        got_y(slot(1, "b"), k)
    for k in range(2):
        send_y(slot(2, "o"), k, pb)
    lax.fori_loop(0, 2, lambda i, c: split_xs(1 + 2 * i, c), 0)

    def early(i, c):
        g = (i + 3) // 4
        split_y((g * h + (1 - g) * (1 - h)) * 8 + yhi * 4 + at_z(lax.rem(i + 3, 4) * g))
        return c

    def early2(i, c):
        split_y(h * 8 + (1 - yhi) * 4 + at_z(i))
        return c

    lax.fori_loop(0, 5, early, 0)
    lax.fori_loop(0, 2, early2, 0)

    for k in range(2):
        got_y(slot(0, "c"), k)
        send_y(slot(0, "c"), k, zp)
        got_y(slot(1, "a"), k)
        send_y(slot(1, "a"), k, zm)
        got_y(slot(3, "a"), k)
        got_x(xo + at_x(2), k)
        got_x(xa + at_x(2), k)
    for k in range(2):
        send_y(slot(0, "b"), k, zp)
        send_y(slot(0, "c"), k, zm)
    lax.fori_loop(2, 3, split_xs, 0)
    r = lax.broadcasted_iota(jnp.int32, (128, 128), 0)
    c = lax.broadcasted_iota(jnp.int32, (128, 128), 1)
    for i in range(3):
        piece = jnp.sum(jnp.where(r == c, xs[128 * i : 128 * i + 128, :], 0.0), axis=0, keepdims=True)
        rsq[:, 128 * i : 128 * i + 128] = jnp.broadcast_to(piece, (8, 128))

    def block(s):
        at = pl.ds(pl.multiple_of(s * BLK, BLK), BLK)
        hi = yh_[at, :]
        both = dot_nt(jnp.concatenate([hi, yl_[at, :]], axis=0), xh[...])
        cross = both[:BLK] + both[BLK:] + dot_nt(hi, xl[...])
        return (2.0 * cross - cs[at, 0:1] - rsq[0:1, :]) * SCALE

    def pair_block(dz, is_c, ready=False):
        k = (is_c * (1 - yhi) + (1 - is_c) * yhi) * 4 + at_z(dz)
        if not ready:
            split_y((1 - h) * 8 + k)
        ps[k] = block((1 - h) * 8 + k)
        pltpu.make_async_remote_copy(
            src_ref=ps.at[k], dst_ref=pr.at[k], send_sem=prs.at[0, k], recv_sem=prs.at[1, k], device_id=pa, device_id_type=MESH
        ).start()

    def own_block(dz, is_b, ready=False):
        k = (is_b * (1 - yhi) + (1 - is_b) * yhi) * 4 + at_z(dz)
        if not ready:
            split_y(h * 8 + k)
        lg[pl.ds(pl.multiple_of(k * BLK, BLK), BLK), :] = block(h * 8 + k)

    def group1(i, c):
        pair_block(lax.rem(1 + 2 * i, 4) * (1 - i // 2), i // 2)
        return c

    def group2(i, c):
        pair_block(2 + i, i)
        return c

    def group3(i, c):
        own_block(lax.rem(i, 4), i // 4, True)
        return c

    def group4(i, c):
        pair_block(1 + i, 1)
        return c

    def group5(i, c):
        own_block(2 + i, 1)
        return c

    pair_block(0, 0, True)
    lax.fori_loop(0, 3, group1, 0)
    for k in range(2):
        got_y(slot(2, "a"), k)
        send_y(slot(2, "a"), k, pb)
        got_y(slot(3, "c"), k)
        got_y(slot(2, "b"), k)
    lax.fori_loop(0, 2, group2, 0)
    lax.fori_loop(0, 6, group3, 0)
    for k in range(2):
        got_y(slot(1, "c"), k)
        got_y(slot(2, "c"), k)
        got_y(slot(3, "b"), k)
    lax.fori_loop(0, 2, group4, 0)
    lax.fori_loop(0, 2, group5, 0)

    def pair_wait(k, c):
        d = pltpu.make_async_remote_copy(
            src_ref=ps.at[k], dst_ref=pr.at[k], send_sem=prs.at[0, k], recv_sem=prs.at[1, k], device_id=pa, device_id_type=MESH
        )
        d.wait_recv()
        d.wait_send()
        at = pl.ds(pl.multiple_of(k * BLK, BLK), BLK)
        lg[at, :] = lg[at, :] + pr[k]
        return c

    lax.fori_loop(0, NB, pair_wait, 0)

    def send_logits(k):
        at = pl.ds(LO_AT[k], LO_AT[k + 1] - LO_AT[k])
        send(lg.at[at], lo.at[at], lsem.at[k], pa)

    def got_logits(k):
        at = pl.ds(LO_AT[k], LO_AT[k + 1] - LO_AT[k])
        arrived(lo.at[at], lsem.at[k])

    def ex_rows(rnd, msg):
        rx[rnd, d] = msg

        def go_(k, c):
            p = lax.rem(d + k, 8)
            pltpu.make_async_remote_copy(
                src_ref=rx.at[rnd, d], dst_ref=rx.at[rnd, d], send_sem=rxs.at[0, rnd, p], recv_sem=rxs.at[1, rnd, d],
                device_id=(n, p), device_id_type=MESH,
            ).start()
            return c

        lax.fori_loop(1, 8, go_, 0)

        def done():
            def wt(k, c):
                p = lax.rem(d + k, 8)
                w = pltpu.make_async_remote_copy(
                    src_ref=rx.at[rnd, p], dst_ref=rx.at[rnd, p], send_sem=rxs.at[0, rnd, p], recv_sem=rxs.at[1, rnd, p],
                    device_id=(n, p), device_id_type=MESH,
                )
                w.wait_recv()
                return c

            lax.fori_loop(1, 8, wt, 0)
            return rx[rnd]

        return done

    def ex_cols(buf, sem, msg, rnd):
        buf[rnd, n] = msg

        def go_(k, c):
            p = lax.rem(n + k, 16)
            pltpu.make_async_remote_copy(
                src_ref=buf.at[rnd, n], dst_ref=buf.at[rnd, n], send_sem=sem.at[0, rnd, p], recv_sem=sem.at[1, rnd, n],
                device_id=col_dev(p), device_id_type=MESH,
            ).start()
            return c

        lax.fori_loop(1, 16, go_, 0)

        def done():
            def wt(k, c):
                p = lax.rem(n + k, 16)
                pltpu.make_async_remote_copy(
                    src_ref=buf.at[rnd, p], dst_ref=buf.at[rnd, p], send_sem=sem.at[0, rnd, p], recv_sem=sem.at[1, rnd, p],
                    device_id=col_dev(p), device_id_type=MESH,
                ).wait_recv()
                return c

            lax.fori_loop(1, 16, wt, 0)
            return buf[rnd]

        return done

    def row_msg(parts):
        parts = parts + [jnp.zeros((1, 128), F32)] * (8 - len(parts))
        return jnp.concatenate(parts, axis=0)

    def blk(k):
        return slice(BLK * k, BLK * k + BLK)

    m8 = None
    for k in range(NB):
        piece = jnp.max(lg[blk(k), :].reshape(12, 8, ROWS), axis=0)
        m8 = piece if m8 is None else jnp.maximum(m8, piece)
    m = jnp.max(m8, axis=0, keepdims=True)
    s8 = jnp.zeros((8, ROWS), F32)
    for k in range(NB):
        s8 = s8 + jnp.sum(jnp.exp(lg[blk(k), :] - m).reshape(12, 8, ROWS), axis=0)
    tot = jnp.sum(s8, axis=0, keepdims=True)
    done = ex_rows(0, row_msg(rows3(m) + rows3(tot)))
    send_logits(0)
    everyone = done()
    mm = everyone[:, 0:3, :]
    top = jnp.max(mm, axis=0)
    tt = jnp.sum(everyone[:, 3:6, :] * jnp.exp(mm - top[None]), axis=0)
    f1 = flat3(LOGN - top - jnp.log(tt))

    pm = jnp.zeros((8, 128), F32)
    pt = jnp.zeros((8, 128), F32)
    for k in range(NB):
        a = lg[blk(k), :] + f1
        cm = jnp.max(a, axis=1, keepdims=True)
        ct = jnp.sum(jnp.exp(a - cm), axis=1, keepdims=True)
        pm = pm + pack_block(k, cm)
        pt = pt + pack_block(k, ct)
    everyone = ex_cols(cx1, cx1s, jnp.concatenate([pm, pt], axis=0), 0)()
    mm = everyone[:, 0:8, :]
    top = jnp.max(mm, axis=0)
    tt = jnp.sum(everyone[:, 8:16, :] * jnp.exp(mm - top[None]), axis=0)
    used = lax.broadcasted_iota(jnp.int32, (8, 128), 1) < 96
    g1 = jnp.where(used, LOGN - top - jnp.log(jnp.where(used, tt, 1.0)), 0.0)
    go[0] = g1
    send(go.at[0], go.at[1], gs.at[0], pa)

    s8 = jnp.zeros((8, ROWS), F32)
    for k in range(NB):
        p = jnp.exp(lg[blk(k), :] + f1 + unpack(g1, 12 * k, 12))
        q_[blk(k), :] = p
        s8 = s8 + jnp.sum(p.reshape(12, 8, ROWS), axis=0)

    def row_step(rnd, s8, between):
        done = ex_rows(rnd, row_msg(rows3(jnp.sum(s8, axis=0, keepdims=True))))
        between()
        return flat3(NSAMP / jnp.sum(done()[:, 0:3, :], axis=0))

    def col_step(rnd, u, between):
        pk = jnp.zeros((8, 128), F32)
        for k in range(NB):
            pk = pk + pack_block(k, jnp.sum(q_[blk(k), :] * u, axis=1, keepdims=True))
        done = ex_cols(cx, cxs, pk, rnd)
        between()
        tt = jnp.sum(done(), axis=0)
        return NSAMP / jnp.where(used, tt, 1.0)

    def row_sums(v):
        s8 = jnp.zeros((8, ROWS), F32)
        for k in range(NB):
            s8 = s8 + jnp.sum((q_[blk(k), :] * unpack(v, 12 * k, 12)).reshape(12, 8, ROWS), axis=0)
        return s8

    def turn(src, dst, some):
        for q in some:
            dst[:, 128 * q : 128 * q + 128] = src[128 * q : 128 * q + 128, :].T

    def far(some):
        for q in some:
            at = slice(128 * q, 128 * q + 128)
            po[:, at] = jnp.exp(lo[at, :] + f1 + unpack(go[1], 16 * q, 16)).T

    def in_row1():
        send_logits(1)
        turn(q_, pn, range(0, 3))

    def in_row2():
        send_logits(2)
        arrived(go.at[1], gs.at[0])
        got_logits(0)
        far(range(0, 2))

    def in_col2():
        got_logits(1)
        far(range(2, 4))
        got_logits(2)
        far(range(4, 6))

    u = row_step(1, s8, in_row1)
    v = col_step(0, u, lambda: turn(q_, pn, range(3, 6)))
    u = row_step(2, row_sums(v), in_row2)
    v = col_step(1, u, in_col2)
    vo[0] = v
    send(vo.at[0], vo.at[1], gs.at[1], pa)
    total = ex_rows(3, row_msg(rows3(jnp.sum(row_sums(v), axis=0, keepdims=True))))

    hi, low = split(pn[...] * packed_row(v))
    wh[0] = hi
    wl[0] = low

    own_rows = pl.ds(pl.multiple_of(h * COLS, COLS), COLS)
    far_rows = pl.ds(pl.multiple_of((1 - h) * COLS, COLS), COLS)

    def part(i, rows, cols):
        return (
            dot_nn(wh[i], yh_[rows, cols]) + dot_nn(wh[i], yl_[rows, cols]) + dot_nn(wl[i], yh_[rows, cols])
        )

    def cols_of(c):
        return slice(CW * c, CW * c + CW)

    def compute(c):
        t = part(0, own_rows, cols_of(c))
        if c == 0:
            arrived(vo.at[1], gs.at[1])
            hi, low = split(po[...] * packed_row(vo[1]))
            wh[1] = hi
            wl[1] = low
        t = t + part(1, far_rows, cols_of(c))
        tp[c] = t.reshape(8, OWN, CW)

    def start_pair(c):
        send(tp.at[c, xa + at_x(2)], r1.at[c, 0], r1s.at[c, 0], xp)
        send(tp.at[c, xa + at_x(3)], r2.at[c, 0], r2s.at[c, 0], xm)

    def pass_pair(c):
        arrived(r1.at[c, 0], r1s.at[c, 0])
        tp[c, xa + at_x(1)] = tp[c, xa + at_x(1)] + r1[c, 0]
        send(tp.at[c, xa + at_x(1)], r2.at[c, 1], r2s.at[c, 1], xp)

    def start_own(c):
        send(tp.at[c, xo + at_x(2)], r1.at[c, 1], r1s.at[c, 1], xm)
        send(tp.at[c, xo + at_x(1)], r2.at[c, 3], r2s.at[c, 3], xp)

    def pass_own(c):
        arrived(r1.at[c, 1], r1s.at[c, 1])
        tp[c, xo + at_x(3)] = tp[c, xo + at_x(3)] + r1[c, 1]
        send(tp.at[c, xo + at_x(3)], r2.at[c, 2], r2s.at[c, 2], xm)

    def final_pair(c):
        arrived(r2.at[c, 0], r2s.at[c, 0])
        arrived(r2.at[c, 1], r2s.at[c, 1])
        tp[c, xa + x] = tp[c, xa + x] + r2[c, 0] + r2[c, 1]
        send(tp.at[c, xa + x], pf.at[c], pfs.at[c], pa)

    for c in range(CH):
        compute(c)
        start_pair(c)
        if c:
            pass_pair(c - 1)
    pass_pair(CH - 1)
    for c in range(CH):
        start_own(c)

    fin = flat3(jnp.sum(total()[:, 0:3, :], axis=0))
    lane = lax.broadcasted_iota(jnp.int32, (OWN, ROWS), 1)
    row = lax.broadcasted_iota(jnp.int32, (OWN, ROWS), 0) + d * OWN
    norm = 1.0 / jnp.sum(jnp.where(lane == row, fin, 0.0), axis=1, keepdims=True)
    f_out[...] = EPS * (f1 + jnp.log(u))
    near = lax.broadcasted_iota(jnp.int32, (8, 128), 1) // 48 == yhi
    g_out[...] = EPS * packed_row(jnp.where(near, g1 + jnp.log(v), go[1] + jnp.log(vo[1])))

    for c in range(CH):
        final_pair(c)
        if c:
            pass_own(c - 1)
    pass_own(CH - 1)
    for c in range(CH):
        arrived(r2.at[c, 2], r2s.at[c, 2])
        arrived(r2.at[c, 3], r2s.at[c, 3])
        t = tp[c, xo + x] + r2[c, 2] + r2[c, 3]
        t_out[:, pl.ds(pl.multiple_of(h * HALF + c * CW, CW), CW)] = t * norm
    for c in range(CH):
        arrived(pf.at[c], pfs.at[c])
        t_out[:, pl.ds(pl.multiple_of((1 - h) * HALF + c * CW, CW), CW)] = pf[c] * norm

    for cp in sent:
        cp.wait_send()

    def drain_rows(k, c):
        p = lax.rem(d + k, 8)
        for rnd in range(4):
            pltpu.make_async_remote_copy(
                src_ref=rx.at[rnd, d], dst_ref=rx.at[rnd, d], send_sem=rxs.at[0, rnd, p], recv_sem=rxs.at[1, rnd, d],
                device_id=(n, p), device_id_type=MESH,
            ).wait_send()
        return c

    def drain_cols(k, c):
        p = lax.rem(n + k, 16)
        for buf, sem, rnd in ((cx1, cx1s, 0), (cx, cxs, 0), (cx, cxs, 1)):
            pltpu.make_async_remote_copy(
                src_ref=buf.at[rnd, n], dst_ref=buf.at[rnd, n], send_sem=sem.at[0, rnd, p], recv_sem=sem.at[1, rnd, n],
                device_id=col_dev(p), device_id_type=MESH,
            ).wait_send()
        return c

    lax.fori_loop(1, 8, drain_rows, 0)
    lax.fori_loop(1, 16, drain_cols, 0)


def hand_out(t_in, f_in, g_in, t_out, f_out, g_out, sem):
    parts = [
        pltpu.make_async_copy(t_in.at[pl.ds(8 * k, 8)], t_out.at[pl.ds(8 * k, 8)], sem.at[k]) for k in range(OWN // 8)
    ]
    for cp in parts:
        cp.start()
    f_out[...] = f_in[...].reshape(ROWS)
    g_out[...] = g_in[...].reshape(COLS)
    for cp in parts:
        cp.wait()


def body(noise_latents, data_latents):
    dma = pltpu.SemaphoreType.DMA
    vm = pltpu.VMEM
    scratch = [
        vm((8, 2, PIECE, HALF), F32),
        vm((16, 2, 2, PIECE, HALF), F32),
        vm((ROWS, HALF), BF16),
        vm((ROWS, HALF), BF16),
        vm((2 * COLS, HALF), BF16),
        vm((2 * COLS, HALF), BF16),
        vm((ROWS, 128), F32),
        vm((2 * COLS, 128), F32),
        vm((8, ROWS), F32),
        vm((NB, BLK, ROWS), F32),
        vm((NB, BLK, ROWS), F32),
        vm((COLS, ROWS), F32),
        vm((COLS, ROWS), F32),
        vm((COLS, ROWS), F32),
        vm((ROWS, COLS), F32),
        vm((ROWS, COLS), F32),
        vm((2, ROWS, COLS), BF16),
        vm((2, ROWS, COLS), BF16),
        vm((CH, 8, OWN, CW), F32),
        vm((CH, 2, OWN, CW), F32),
        vm((CH, 4, OWN, CW), F32),
        vm((CH, OWN, CW), F32),
        vm((4, 8, 8, 128), F32),
        vm((1, 16, 16, 128), F32),
        vm((2, 16, 8, 128), F32),
        vm((2, 8, 128), F32),
        vm((2, 8, 128), F32),
        dma((2, 2)),
        dma((8, 2)),
        dma((16, 2)),
        dma((16, 2)),
        dma((2, NB)),
        dma((3,)),
        dma((2, 4, 8)),
        dma((2, 1, 16)),
        dma((2, 2, 16)),
        dma((2,)),
        dma((CH, 2)),
        dma((CH, 4)),
        dma((CH,)),
        dma((192,)),
    ]
    t, f, g = pl.pallas_call(
        kernel,
        out_shape=(
            vm((OWN, WIDTH), F32),
            vm((1, ROWS), F32),
            vm((1, COLS), F32),
        ),
        in_specs=[pl.BlockSpec(memory_space=pl.ANY)] * 2,
        out_specs=(pl.BlockSpec(memory_space=pltpu.VMEM),) * 3,
        scratch_shapes=scratch,
        compiler_params=pltpu.CompilerParams(
            collective_id=0, has_side_effects=True, vmem_limit_bytes=60 * 2**20
        ),
        name="coupling",
    )(noise_latents, data_latents)
    return pl.pallas_call(
        hand_out,
        out_shape=(
            jax.ShapeDtypeStruct((OWN, WIDTH), F32),
            jax.ShapeDtypeStruct((ROWS,), F32),
            jax.ShapeDtypeStruct((COLS,), F32),
        ),
        in_specs=[pl.BlockSpec(memory_space=pltpu.VMEM)] * 3,
        out_specs=(pl.BlockSpec(memory_space=pl.ANY),) + (pl.BlockSpec(memory_space=pltpu.VMEM),) * 2,
        scratch_shapes=[pltpu.SemaphoreType.DMA((OWN // 8,))],
        name="hand_out",
    )(t, f, g)


def solution(mesh):
    placed = (P(("noise", "dp"), None), P(("dp", "noise"), None))
    return jax.shard_map(
        body,
        mesh=mesh,
        in_specs=placed,
        out_specs=(P(("noise", "dp"), None), P("noise"), P("dp")),
        check_vma=False,
    )
```

```python
import functools
import math

import jax
import jax.numpy as jnp
from jax import lax
from jax.experimental import pallas as pl
from jax.experimental.pallas import tpu as pltpu
from jax.sharding import PartitionSpec as P

MESH = pl.DeviceIdType.MESH
F32 = jnp.float32
BF16 = jnp.bfloat16
EPS = 0.01

OWN = 48
WIDTH = 4096
HALF = WIDTH // 2
ROWS = 384
COLS = 768
BLK = 96
NB = COLS // BLK
PIECE = OWN // 2
LO_AT = (0, 320, 576, 768)
NSAMP = 6144
LOGN = math.log(NSAMP)
SCALE = 1.0 / (WIDTH * EPS)
CH = 4
CW = HALF // CH


def split(v):
    hi = v.astype(BF16)
    return hi, (v - hi.astype(F32)).astype(BF16)


def dot_nt(a, b):
    return lax.dot_general(a, b, (((1,), (1,)), ((), ())), preferred_element_type=F32)


def dot_nn(a, b):
    return lax.dot_general(a, b, (((1,), (0,)), ((), ())), preferred_element_type=F32)


def pack_block(k, val):
    v3 = val.reshape(12, 8, 1)
    lane = lax.broadcasted_iota(jnp.int32, (12, 8, 128), 2)
    lead = lax.broadcasted_iota(jnp.int32, (12, 8, 128), 0) + 12 * k
    return jnp.sum(jnp.where(lane == lead, v3, 0.0), axis=0)


def unpack(packed, first, count):
    lane = lax.broadcasted_iota(jnp.int32, (count, 8, 128), 2)
    lead = lax.broadcasted_iota(jnp.int32, (count, 8, 128), 0) + first
    v3 = jnp.sum(jnp.where(lane == lead, packed[None], 0.0), axis=2, keepdims=True)
    return v3.reshape(8 * count, 1)


def to_row(col):
    r = lax.broadcasted_iota(jnp.int32, (128, 128), 0)
    c = lax.broadcasted_iota(jnp.int32, (128, 128), 1)
    return jnp.sum(jnp.where(r == c, col, 0.0), axis=0, keepdims=True)


def packed_row(packed):
    return jnp.concatenate([to_row(unpack(packed, 16 * q, 16)) for q in range(6)], axis=1)


def rows3(v):
    return [v[:, 128 * q : 128 * q + 128] for q in range(3)]


def flat3(v):
    return jnp.concatenate([v[q : q + 1] for q in range(3)], axis=1)


def kernel(
    x_hbm, y_hbm, t_out, f_out, g_out,
    xb, yb, xh, xl, yh_, yl_, xs, rsq, ps, pr, lg, lo, q_, pn, po, wh, wl, tp, r1, r2, pf,
    rx, cx1, cx, go, vo,
    loc, xr, yr, yr2, prs, lsem, rxs, cx1s, cxs, gs, r1s, r2s, pfs, ssem,
):
    n = lax.axis_index("noise")
    d = lax.axis_index("dp")
    core = lax.rem(n, 2)
    z = lax.rem(n // 2, 4)
    yhi = n // 8
    x = lax.rem(d, 4)
    ylo = d // 4
    h = lax.rem(yhi + ylo, 2)

    def at_z(k):
        return lax.rem(z + k, 4)

    def at_x(k):
        return lax.rem(x + k, 4)

    sib = (n + 1 - 2 * core, d)
    pa = (n, (1 - ylo) * 4 + x)
    pb = (((1 - yhi) * 4 + z) * 2 + core, (1 - ylo) * 4 + x)
    zp = ((yhi * 4 + at_z(1)) * 2 + core, d)
    zm = ((yhi * 4 + at_z(3)) * 2 + core, d)
    xp = (n, ylo * 4 + at_x(1))
    xm = (n, ylo * 4 + at_x(3))

    SRC = {"o": (yhi, h), "a": (yhi, 1 - h), "b": (1 - yhi, h), "c": (1 - yhi, 1 - h)}

    def slot(dz, who):
        hi, tile = SRC[who]
        return tile * 8 + hi * 4 + at_z(dz)

    def col_dev(p):
        return (p, lax.rem(p // 8 + h, 2) * 4 + x)

    kmine = pl.ds(pl.multiple_of(h * HALF, HALF), HALF)
    kother = pl.ds(pl.multiple_of((1 - h) * HALF, HALF), HALF)

    cx_own = [
        pltpu.make_async_copy(x_hbm.at[pl.ds(k * PIECE, PIECE), kmine], xb.at[d, k], loc.at[0, k]) for k in range(2)
    ]
    cy_own = [
        pltpu.make_async_copy(y_hbm.at[pl.ds(k * PIECE, PIECE), kmine], yb.at[slot(0, "o"), core, k], loc.at[1, k])
        for k in range(2)
    ]
    for cp in cx_own + cy_own:
        cp.start()

    barrier = pltpu.get_barrier_semaphore()

    for dev in (pa, pb, zp, zm, xp, xm, sib):
        pl.semaphore_signal(barrier, inc=1, device_id=dev, device_id_type=MESH)
    pl.semaphore_wait(barrier, 7)

    sent = []

    def send(src, dst, rsem, dev):
        c = pltpu.make_async_remote_copy(
            src_ref=src, dst_ref=dst, send_sem=ssem.at[len(sent)], recv_sem=rsem, device_id=dev, device_id_type=MESH
        )
        c.start()
        sent.append(c)
        return c

    def arrived(dst, rsem):
        pltpu.make_async_remote_copy(
            src_ref=dst, dst_ref=dst, send_sem=ssem.at[0], recv_sem=rsem, device_id=sib, device_id_type=MESH
        ).wait_recv()

    def send_y(s, k, dev):
        send(yb.at[s, core, k], yb.at[s, core, k], yr.at[s, k], dev)

    def cross_y(s, k):
        send(yb.at[s, core, k], yb.at[s, core, k], yr2.at[s, k], sib)

    def got_y(s, k):
        arrived(yb.at[s, core, k], yr.at[s, k])
        cross_y(s, k)

    def send_x(i, k, dev):
        send(xb.at[i, k], xb.at[i, k], xr.at[i, k], dev)

    def got_x(i, k):
        arrived(xb.at[i, k], xr.at[i, k])

    xa = (1 - ylo) * 4
    xo = ylo * 4

    def split_x(i):
        v = xb[i].reshape(OWN, HALF)
        hi, low = split(v)
        at = pl.ds(pl.multiple_of(i * OWN, OWN), OWN)
        xh[at, :] = hi
        xl[at, :] = low
        xs[at, :] = jnp.broadcast_to(jnp.sum(v * v, axis=1, keepdims=True), (OWN, 128))

    def split_xs(i, c):
        split_x(at_x(i))
        split_x(4 + at_x(i))
        return c

    def split_y(s):
        for k in range(2):
            arrived(yb.at[s, 1 - core, k], yr2.at[s, k])
        v = yb[s].reshape(BLK, HALF)
        hi, low = split(v)
        at = pl.ds(pl.multiple_of(s * BLK, BLK), BLK)
        yh_[at, :] = hi
        yl_[at, :] = low
        return hi, low, jnp.sum(v * v, axis=1, keepdims=True)

    for k in range(2):
        send(x_hbm.at[pl.ds(k * PIECE, PIECE), kother], xb.at[d, k], xr.at[d, k], pa)
    for k in range(2):
        mine = slot(0, "o")
        send(y_hbm.at[pl.ds(k * PIECE, PIECE), kother], yb.at[mine, core, k], yr.at[mine, k], pa)
    for k in range(2):
        cx_own[k].wait()
        send_x(d, k, xp)
        send_x(d, k, xm)
        cy_own[k].wait()
        send_y(mine, k, zp)
        send_y(mine, k, zm)
        send_y(mine, k, pb)
        cross_y(mine, k)

    for k in range(2):
        got_x(xa + x, k)
        send_x(xa + x, k, xp)
        send_x(xa + x, k, xm)
        got_y(slot(3, "o"), k)
        send_y(slot(3, "o"), k, zp)
        got_y(slot(0, "b"), k)
        send_y(slot(0, "b"), k, zm)
        got_y(slot(1, "o"), k)
        got_x(xo + at_x(1), k)
        got_x(xo + at_x(3), k)
        send_x(xo + at_x(3), k, xp)

    lax.fori_loop(0, 1, split_xs, 0)

    for k in range(2):
        got_y(slot(0, "a"), k)
        send_y(slot(0, "a"), k, zp)
        send_y(slot(0, "a"), k, zm)
        send_y(slot(0, "a"), k, pb)
        got_x(xa + at_x(1), k)
        send_x(xa + at_x(1), k, xm)
        got_x(xa + at_x(3), k)
        got_y(slot(2, "o"), k)
        got_y(slot(1, "b"), k)
    for k in range(2):
        send_y(slot(2, "o"), k, pb)
    lax.fori_loop(0, 2, lambda i, c: split_xs(1 + 2 * i, c), 0)

    for k in range(2):
        got_y(slot(0, "c"), k)
        send_y(slot(0, "c"), k, zp)
        got_y(slot(1, "a"), k)
        send_y(slot(1, "a"), k, zm)
        got_y(slot(3, "a"), k)
        got_x(xo + at_x(2), k)
        got_x(xa + at_x(2), k)
    for k in range(2):
        send_y(slot(0, "b"), k, zp)
        send_y(slot(0, "c"), k, zm)
    lax.fori_loop(2, 3, split_xs, 0)
    r = lax.broadcasted_iota(jnp.int32, (128, 128), 0)
    c = lax.broadcasted_iota(jnp.int32, (128, 128), 1)
    for i in range(3):
        piece = jnp.sum(jnp.where(r == c, xs[128 * i : 128 * i + 128, :], 0.0), axis=0, keepdims=True)
        rsq[:, 128 * i : 128 * i + 128] = jnp.broadcast_to(piece, (8, 128))

    def block(s):
        hi, low, csq = split_y(s)
        both = dot_nt(jnp.concatenate([hi, low], axis=0), xh[...])
        cross = both[:BLK] + both[BLK:] + dot_nt(hi, xl[...])
        return (2.0 * cross - csq - rsq[0:1, :]) * SCALE

    def pair_block(dz, is_c):
        k = (is_c * (1 - yhi) + (1 - is_c) * yhi) * 4 + at_z(dz)
        ps[k] = block((1 - h) * 8 + k)
        pltpu.make_async_remote_copy(
            src_ref=ps.at[k], dst_ref=pr.at[k], send_sem=prs.at[0, k], recv_sem=prs.at[1, k], device_id=pa, device_id_type=MESH
        ).start()

    def own_block(dz, is_b):
        k = (is_b * (1 - yhi) + (1 - is_b) * yhi) * 4 + at_z(dz)
        lg[pl.ds(pl.multiple_of(k * BLK, BLK), BLK), :] = block(h * 8 + k)

    def group1(i, c):
        pair_block(lax.rem(i, 2) + 2 * (i // 3), lax.rem(i // 2 + i // 3, 2))
        return c

    def group2(i, c):
        pair_block(2 + i, i)
        return c

    def group3(i, c):
        own_block(lax.rem(i, 4), i // 4)
        return c

    def group4(i, c):
        pair_block(1 + i, 1)
        return c

    def group5(i, c):
        own_block(2 + i, 1)
        return c

    lax.fori_loop(0, 4, group1, 0)
    for k in range(2):
        got_y(slot(2, "a"), k)
        send_y(slot(2, "a"), k, pb)
        got_y(slot(3, "c"), k)
        got_y(slot(2, "b"), k)
    lax.fori_loop(0, 2, group2, 0)
    lax.fori_loop(0, 6, group3, 0)
    for k in range(2):
        got_y(slot(1, "c"), k)
        got_y(slot(2, "c"), k)
        got_y(slot(3, "b"), k)
    lax.fori_loop(0, 2, group4, 0)
    lax.fori_loop(0, 2, group5, 0)

    def pair_wait(k, c):
        d = pltpu.make_async_remote_copy(
            src_ref=ps.at[k], dst_ref=pr.at[k], send_sem=prs.at[0, k], recv_sem=prs.at[1, k], device_id=pa, device_id_type=MESH
        )
        d.wait_recv()
        d.wait_send()
        at = pl.ds(pl.multiple_of(k * BLK, BLK), BLK)
        lg[at, :] = lg[at, :] + pr[k]
        return c

    lax.fori_loop(0, NB, pair_wait, 0)

    def send_logits(k):
        at = pl.ds(LO_AT[k], LO_AT[k + 1] - LO_AT[k])
        send(lg.at[at], lo.at[at], lsem.at[k], pa)

    def got_logits(k):
        at = pl.ds(LO_AT[k], LO_AT[k + 1] - LO_AT[k])
        arrived(lo.at[at], lsem.at[k])

    def ex_rows(rnd, msg):
        rx[rnd, d] = msg

        def go_(k, c):
            p = lax.rem(d + k, 8)
            pltpu.make_async_remote_copy(
                src_ref=rx.at[rnd, d], dst_ref=rx.at[rnd, d], send_sem=rxs.at[0, rnd, p], recv_sem=rxs.at[1, rnd, d],
                device_id=(n, p), device_id_type=MESH,
            ).start()
            return c

        lax.fori_loop(1, 8, go_, 0)

        def done():
            def wt(k, c):
                p = lax.rem(d + k, 8)
                w = pltpu.make_async_remote_copy(
                    src_ref=rx.at[rnd, p], dst_ref=rx.at[rnd, p], send_sem=rxs.at[0, rnd, p], recv_sem=rxs.at[1, rnd, p],
                    device_id=(n, p), device_id_type=MESH,
                )
                w.wait_recv()
                return c

            lax.fori_loop(1, 8, wt, 0)
            return rx[rnd]

        return done

    def ex_cols(buf, sem, msg, rnd):
        buf[rnd, n] = msg

        def go_(k, c):
            p = lax.rem(n + k, 16)
            pltpu.make_async_remote_copy(
                src_ref=buf.at[rnd, n], dst_ref=buf.at[rnd, n], send_sem=sem.at[0, rnd, p], recv_sem=sem.at[1, rnd, n],
                device_id=col_dev(p), device_id_type=MESH,
            ).start()
            return c

        lax.fori_loop(1, 16, go_, 0)

        def done():
            def wt(k, c):
                p = lax.rem(n + k, 16)
                pltpu.make_async_remote_copy(
                    src_ref=buf.at[rnd, p], dst_ref=buf.at[rnd, p], send_sem=sem.at[0, rnd, p], recv_sem=sem.at[1, rnd, p],
                    device_id=col_dev(p), device_id_type=MESH,
                ).wait_recv()
                return c

            lax.fori_loop(1, 16, wt, 0)
            return buf[rnd]

        return done

    def row_msg(parts):
        parts = parts + [jnp.zeros((1, 128), F32)] * (8 - len(parts))
        return jnp.concatenate(parts, axis=0)

    def blk(k):
        return slice(BLK * k, BLK * k + BLK)

    m8 = None
    for k in range(NB):
        piece = jnp.max(lg[blk(k), :].reshape(12, 8, ROWS), axis=0)
        m8 = piece if m8 is None else jnp.maximum(m8, piece)
    m = jnp.max(m8, axis=0, keepdims=True)
    s8 = jnp.zeros((8, ROWS), F32)
    for k in range(NB):
        s8 = s8 + jnp.sum(jnp.exp(lg[blk(k), :] - m).reshape(12, 8, ROWS), axis=0)
    tot = jnp.sum(s8, axis=0, keepdims=True)
    done = ex_rows(0, row_msg(rows3(m) + rows3(tot)))
    send_logits(0)
    everyone = done()
    mm = everyone[:, 0:3, :]
    top = jnp.max(mm, axis=0)
    tt = jnp.sum(everyone[:, 3:6, :] * jnp.exp(mm - top[None]), axis=0)
    f1 = flat3(LOGN - top - jnp.log(tt))

    pm = jnp.zeros((8, 128), F32)
    pt = jnp.zeros((8, 128), F32)
    for k in range(NB):
        a = lg[blk(k), :] + f1
        cm = jnp.max(a, axis=1, keepdims=True)
        ct = jnp.sum(jnp.exp(a - cm), axis=1, keepdims=True)
        pm = pm + pack_block(k, cm)
        pt = pt + pack_block(k, ct)
    everyone = ex_cols(cx1, cx1s, jnp.concatenate([pm, pt], axis=0), 0)()
    mm = everyone[:, 0:8, :]
    top = jnp.max(mm, axis=0)
    tt = jnp.sum(everyone[:, 8:16, :] * jnp.exp(mm - top[None]), axis=0)
    used = lax.broadcasted_iota(jnp.int32, (8, 128), 1) < 96
    g1 = jnp.where(used, LOGN - top - jnp.log(jnp.where(used, tt, 1.0)), 0.0)
    go[0] = g1
    send(go.at[0], go.at[1], gs.at[0], pa)

    s8 = jnp.zeros((8, ROWS), F32)
    for k in range(NB):
        p = jnp.exp(lg[blk(k), :] + f1 + unpack(g1, 12 * k, 12))
        q_[blk(k), :] = p
        s8 = s8 + jnp.sum(p.reshape(12, 8, ROWS), axis=0)

    def row_step(rnd, s8, between):
        done = ex_rows(rnd, row_msg(rows3(jnp.sum(s8, axis=0, keepdims=True))))
        between()
        return flat3(NSAMP / jnp.sum(done()[:, 0:3, :], axis=0))

    def col_step(rnd, u, between):
        pk = jnp.zeros((8, 128), F32)
        for k in range(NB):
            pk = pk + pack_block(k, jnp.sum(q_[blk(k), :] * u, axis=1, keepdims=True))
        done = ex_cols(cx, cxs, pk, rnd)
        between()
        tt = jnp.sum(done(), axis=0)
        return NSAMP / jnp.where(used, tt, 1.0)

    def row_sums(v):
        s8 = jnp.zeros((8, ROWS), F32)
        for k in range(NB):
            s8 = s8 + jnp.sum((q_[blk(k), :] * unpack(v, 12 * k, 12)).reshape(12, 8, ROWS), axis=0)
        return s8

    def turn(src, dst, some):
        for q in some:
            dst[:, 128 * q : 128 * q + 128] = src[128 * q : 128 * q + 128, :].T

    def far(some):
        for q in some:
            at = slice(128 * q, 128 * q + 128)
            po[:, at] = jnp.exp(lo[at, :] + f1 + unpack(go[1], 16 * q, 16)).T

    def in_row1():
        send_logits(1)
        turn(q_, pn, range(0, 3))

    def in_row2():
        send_logits(2)
        arrived(go.at[1], gs.at[0])
        got_logits(0)
        far(range(0, 2))

    def in_col2():
        got_logits(1)
        far(range(2, 4))
        got_logits(2)
        far(range(4, 6))

    u = row_step(1, s8, in_row1)
    v = col_step(0, u, lambda: turn(q_, pn, range(3, 6)))
    u = row_step(2, row_sums(v), in_row2)
    v = col_step(1, u, in_col2)
    vo[0] = v
    send(vo.at[0], vo.at[1], gs.at[1], pa)
    total = ex_rows(3, row_msg(rows3(jnp.sum(row_sums(v), axis=0, keepdims=True))))

    hi, low = split(pn[...] * packed_row(v))
    wh[0] = hi
    wl[0] = low

    own_rows = pl.ds(pl.multiple_of(h * COLS, COLS), COLS)
    far_rows = pl.ds(pl.multiple_of((1 - h) * COLS, COLS), COLS)

    def part(i, rows, cols):
        return (
            dot_nn(wh[i], yh_[rows, cols]) + dot_nn(wh[i], yl_[rows, cols]) + dot_nn(wl[i], yh_[rows, cols])
        )

    def cols_of(c):
        return slice(CW * c, CW * c + CW)

    def compute(c):
        t = part(0, own_rows, cols_of(c))
        if c == 0:
            arrived(vo.at[1], gs.at[1])
            hi, low = split(po[...] * packed_row(vo[1]))
            wh[1] = hi
            wl[1] = low
        t = t + part(1, far_rows, cols_of(c))
        tp[c] = t.reshape(8, OWN, CW)

    def start_pair(c):
        send(tp.at[c, xa + at_x(2)], r1.at[c, 0], r1s.at[c, 0], xp)
        send(tp.at[c, xa + at_x(3)], r2.at[c, 0], r2s.at[c, 0], xm)

    def pass_pair(c):
        arrived(r1.at[c, 0], r1s.at[c, 0])
        tp[c, xa + at_x(1)] = tp[c, xa + at_x(1)] + r1[c, 0]
        send(tp.at[c, xa + at_x(1)], r2.at[c, 1], r2s.at[c, 1], xp)

    def start_own(c):
        send(tp.at[c, xo + at_x(2)], r1.at[c, 1], r1s.at[c, 1], xm)
        send(tp.at[c, xo + at_x(1)], r2.at[c, 3], r2s.at[c, 3], xp)

    def pass_own(c):
        arrived(r1.at[c, 1], r1s.at[c, 1])
        tp[c, xo + at_x(3)] = tp[c, xo + at_x(3)] + r1[c, 1]
        send(tp.at[c, xo + at_x(3)], r2.at[c, 2], r2s.at[c, 2], xm)

    def final_pair(c):
        arrived(r2.at[c, 0], r2s.at[c, 0])
        arrived(r2.at[c, 1], r2s.at[c, 1])
        tp[c, xa + x] = tp[c, xa + x] + r2[c, 0] + r2[c, 1]
        send(tp.at[c, xa + x], pf.at[c], pfs.at[c], pa)

    for c in range(CH):
        compute(c)
        start_pair(c)
        if c:
            pass_pair(c - 1)
    pass_pair(CH - 1)
    for c in range(CH):
        start_own(c)

    fin = flat3(jnp.sum(total()[:, 0:3, :], axis=0))
    lane = lax.broadcasted_iota(jnp.int32, (OWN, ROWS), 1)
    row = lax.broadcasted_iota(jnp.int32, (OWN, ROWS), 0) + d * OWN
    norm = 1.0 / jnp.sum(jnp.where(lane == row, fin, 0.0), axis=1, keepdims=True)
    f_out[...] = EPS * (f1 + jnp.log(u))
    near = lax.broadcasted_iota(jnp.int32, (8, 128), 1) // 48 == yhi
    g_out[...] = EPS * packed_row(jnp.where(near, g1 + jnp.log(v), go[1] + jnp.log(vo[1])))

    for c in range(CH):
        final_pair(c)
        if c:
            pass_own(c - 1)
    pass_own(CH - 1)
    for c in range(CH):
        arrived(r2.at[c, 2], r2s.at[c, 2])
        arrived(r2.at[c, 3], r2s.at[c, 3])
        t = tp[c, xo + x] + r2[c, 2] + r2[c, 3]
        t_out[:, pl.ds(pl.multiple_of(h * HALF + c * CW, CW), CW)] = t * norm
    for c in range(CH):
        arrived(pf.at[c], pfs.at[c])
        t_out[:, pl.ds(pl.multiple_of((1 - h) * HALF + c * CW, CW), CW)] = pf[c] * norm

    for cp in sent:
        cp.wait_send()

    def drain_rows(k, c):
        p = lax.rem(d + k, 8)
        for rnd in range(4):
            pltpu.make_async_remote_copy(
                src_ref=rx.at[rnd, d], dst_ref=rx.at[rnd, d], send_sem=rxs.at[0, rnd, p], recv_sem=rxs.at[1, rnd, d],
                device_id=(n, p), device_id_type=MESH,
            ).wait_send()
        return c

    def drain_cols(k, c):
        p = lax.rem(n + k, 16)
        for buf, sem, rnd in ((cx1, cx1s, 0), (cx, cxs, 0), (cx, cxs, 1)):
            pltpu.make_async_remote_copy(
                src_ref=buf.at[rnd, n], dst_ref=buf.at[rnd, n], send_sem=sem.at[0, rnd, p], recv_sem=sem.at[1, rnd, n],
                device_id=col_dev(p), device_id_type=MESH,
            ).wait_send()
        return c

    lax.fori_loop(1, 8, drain_rows, 0)
    lax.fori_loop(1, 16, drain_cols, 0)


def hand_out(t_in, f_in, g_in, t_out, f_out, g_out, sem):
    parts = [
        pltpu.make_async_copy(t_in.at[pl.ds(8 * k, 8)], t_out.at[pl.ds(8 * k, 8)], sem.at[k]) for k in range(OWN // 8)
    ]
    for cp in parts:
        cp.start()
    f_out[...] = f_in[...].reshape(ROWS)
    g_out[...] = g_in[...].reshape(COLS)
    for cp in parts:
        cp.wait()


def body(noise_latents, data_latents):
    dma = pltpu.SemaphoreType.DMA
    vm = pltpu.VMEM
    scratch = [
        vm((8, 2, PIECE, HALF), F32),
        vm((16, 2, 2, PIECE, HALF), F32),
        vm((ROWS, HALF), BF16),
        vm((ROWS, HALF), BF16),
        vm((2 * COLS, HALF), BF16),
        vm((2 * COLS, HALF), BF16),
        vm((ROWS, 128), F32),
        vm((8, ROWS), F32),
        vm((NB, BLK, ROWS), F32),
        vm((NB, BLK, ROWS), F32),
        vm((COLS, ROWS), F32),
        vm((COLS, ROWS), F32),
        vm((COLS, ROWS), F32),
        vm((ROWS, COLS), F32),
        vm((ROWS, COLS), F32),
        vm((2, ROWS, COLS), BF16),
        vm((2, ROWS, COLS), BF16),
        vm((CH, 8, OWN, CW), F32),
        vm((CH, 2, OWN, CW), F32),
        vm((CH, 4, OWN, CW), F32),
        vm((CH, OWN, CW), F32),
        vm((4, 8, 8, 128), F32),
        vm((1, 16, 16, 128), F32),
        vm((2, 16, 8, 128), F32),
        vm((2, 8, 128), F32),
        vm((2, 8, 128), F32),
        dma((2, 2)),
        dma((8, 2)),
        dma((16, 2)),
        dma((16, 2)),
        dma((2, NB)),
        dma((3,)),
        dma((2, 4, 8)),
        dma((2, 1, 16)),
        dma((2, 2, 16)),
        dma((2,)),
        dma((CH, 2)),
        dma((CH, 4)),
        dma((CH,)),
        dma((192,)),
    ]
    t, f, g = pl.pallas_call(
        kernel,
        out_shape=(
            vm((OWN, WIDTH), F32),
            vm((1, ROWS), F32),
            vm((1, COLS), F32),
        ),
        in_specs=[pl.BlockSpec(memory_space=pl.ANY)] * 2,
        out_specs=(pl.BlockSpec(memory_space=pltpu.VMEM),) * 3,
        scratch_shapes=scratch,
        compiler_params=pltpu.CompilerParams(
            collective_id=0, has_side_effects=True, vmem_limit_bytes=60 * 2**20
        ),
        name="coupling",
    )(noise_latents, data_latents)
    return pl.pallas_call(
        hand_out,
        out_shape=(
            jax.ShapeDtypeStruct((OWN, WIDTH), F32),
            jax.ShapeDtypeStruct((ROWS,), F32),
            jax.ShapeDtypeStruct((COLS,), F32),
        ),
        in_specs=[pl.BlockSpec(memory_space=pltpu.VMEM)] * 3,
        out_specs=(pl.BlockSpec(memory_space=pl.ANY),) + (pl.BlockSpec(memory_space=pltpu.VMEM),) * 2,
        scratch_shapes=[pltpu.SemaphoreType.DMA((OWN // 8,))],
        compiler_params=pltpu.CompilerParams(vmem_limit_bytes=2 * 2**20),
        name="hand_out",
    )(t, f, g)


def solution(mesh):
    placed = (P(("noise", "dp"), None), P(("dp", "noise"), None))
    return jax.shard_map(
        body,
        mesh=mesh,
        in_specs=placed,
        out_specs=(P(("noise", "dp"), None), P("noise"), P("dp")),
        check_vma=False,
    )
```

```python
import functools
import math

import jax
import jax.numpy as jnp
from jax import lax
from jax.experimental import pallas as pl
from jax.experimental.pallas import tpu as pltpu
from jax.sharding import PartitionSpec as P

MESH = pl.DeviceIdType.MESH
F32 = jnp.float32
BF16 = jnp.bfloat16
EPS = 0.01

OWN = 48
WIDTH = 4096
HALF = WIDTH // 2
ROWS = 384
COLS = 768
BLK = 96
NB = COLS // BLK
PIECE = OWN // 2
LO_AT = (0, 320, 576, 768)
NSAMP = 6144
LOGN = math.log(NSAMP)
SCALE = 1.0 / (WIDTH * EPS)
CUTS = (0, 256, 512, 1024, 1536, 2048)
CH = len(CUTS) - 1


def split(v):
    hi = v.astype(BF16)
    return hi, (v - hi.astype(F32)).astype(BF16)


def dot_nt(a, b):
    return lax.dot_general(a, b, (((1,), (1,)), ((), ())), preferred_element_type=F32)


def dot_nn(a, b):
    return lax.dot_general(a, b, (((1,), (0,)), ((), ())), preferred_element_type=F32)


def pack_block(k, val):
    v3 = val.reshape(12, 8, 1)
    lane = lax.broadcasted_iota(jnp.int32, (12, 8, 128), 2)
    lead = lax.broadcasted_iota(jnp.int32, (12, 8, 128), 0) + 12 * k
    return jnp.sum(jnp.where(lane == lead, v3, 0.0), axis=0)


def unpack(packed, first, count):
    lane = lax.broadcasted_iota(jnp.int32, (count, 8, 128), 2)
    lead = lax.broadcasted_iota(jnp.int32, (count, 8, 128), 0) + first
    v3 = jnp.sum(jnp.where(lane == lead, packed[None], 0.0), axis=2, keepdims=True)
    return v3.reshape(8 * count, 1)


def to_row(col):
    r = lax.broadcasted_iota(jnp.int32, (128, 128), 0)
    c = lax.broadcasted_iota(jnp.int32, (128, 128), 1)
    return jnp.sum(jnp.where(r == c, col, 0.0), axis=0, keepdims=True)


def packed_row(packed):
    return jnp.concatenate([to_row(unpack(packed, 16 * q, 16)) for q in range(6)], axis=1)


def rows3(v):
    return [v[:, 128 * q : 128 * q + 128] for q in range(3)]


def flat3(v):
    return jnp.concatenate([v[q : q + 1] for q in range(3)], axis=1)


def kernel(
    x_hbm, y_hbm, t_out, f_out, g_out,
    xb, yb, xh, xl, yh_, yl_, xs, rsq, ps, pr, lg, lo, q_, pn, po, wh, wl, tp, r1, r2, pf,
    rx, cx1, cx, go, vo,
    loc, xr, yr, yr2, prs, lsem, rxs, cx1s, cxs, gs, r1s, r2s, pfs, ssem,
):
    n = lax.axis_index("noise")
    d = lax.axis_index("dp")
    core = lax.rem(n, 2)
    z = lax.rem(n // 2, 4)
    yhi = n // 8
    x = lax.rem(d, 4)
    ylo = d // 4
    h = lax.rem(yhi + ylo, 2)

    def at_z(k):
        return lax.rem(z + k, 4)

    def at_x(k):
        return lax.rem(x + k, 4)

    sib = (n + 1 - 2 * core, d)
    pa = (n, (1 - ylo) * 4 + x)
    pb = (((1 - yhi) * 4 + z) * 2 + core, (1 - ylo) * 4 + x)
    zp = ((yhi * 4 + at_z(1)) * 2 + core, d)
    zm = ((yhi * 4 + at_z(3)) * 2 + core, d)
    xp = (n, ylo * 4 + at_x(1))
    xm = (n, ylo * 4 + at_x(3))

    SRC = {"o": (yhi, h), "a": (yhi, 1 - h), "b": (1 - yhi, h), "c": (1 - yhi, 1 - h)}

    def slot(dz, who):
        hi, tile = SRC[who]
        return tile * 8 + hi * 4 + at_z(dz)

    def col_dev(p):
        return (p, lax.rem(p // 8 + h, 2) * 4 + x)

    kmine = pl.ds(pl.multiple_of(h * HALF, HALF), HALF)
    kother = pl.ds(pl.multiple_of((1 - h) * HALF, HALF), HALF)

    cx_own = [
        pltpu.make_async_copy(x_hbm.at[pl.ds(k * PIECE, PIECE), kmine], xb.at[d, k], loc.at[0, k]) for k in range(2)
    ]
    cy_own = [
        pltpu.make_async_copy(y_hbm.at[pl.ds(k * PIECE, PIECE), kmine], yb.at[slot(0, "o"), core, k], loc.at[1, k])
        for k in range(2)
    ]
    for cp in cx_own + cy_own:
        cp.start()

    barrier = pltpu.get_barrier_semaphore()

    for dev in (pa, pb, zp, zm, xp, xm, sib):
        pl.semaphore_signal(barrier, inc=1, device_id=dev, device_id_type=MESH)
    pl.semaphore_wait(barrier, 7)

    sent = []

    def send(src, dst, rsem, dev):
        c = pltpu.make_async_remote_copy(
            src_ref=src, dst_ref=dst, send_sem=ssem.at[len(sent)], recv_sem=rsem, device_id=dev, device_id_type=MESH
        )
        c.start()
        sent.append(c)
        return c

    def arrived(dst, rsem):
        pltpu.make_async_remote_copy(
            src_ref=dst, dst_ref=dst, send_sem=ssem.at[0], recv_sem=rsem, device_id=sib, device_id_type=MESH
        ).wait_recv()

    def send_y(s, k, dev):
        send(yb.at[s, core, k], yb.at[s, core, k], yr.at[s, k], dev)

    def cross_y(s, k):
        send(yb.at[s, core, k], yb.at[s, core, k], yr2.at[s, k], sib)

    def got_y(s, k):
        arrived(yb.at[s, core, k], yr.at[s, k])
        cross_y(s, k)

    def send_x(i, k, dev):
        send(xb.at[i, k], xb.at[i, k], xr.at[i, k], dev)

    def got_x(i, k):
        arrived(xb.at[i, k], xr.at[i, k])

    xa = (1 - ylo) * 4
    xo = ylo * 4

    def split_x(i):
        v = xb[i].reshape(OWN, HALF)
        hi, low = split(v)
        at = pl.ds(pl.multiple_of(i * OWN, OWN), OWN)
        xh[at, :] = hi
        xl[at, :] = low
        xs[at, :] = jnp.broadcast_to(jnp.sum(v * v, axis=1, keepdims=True), (OWN, 128))

    def split_xs(i, c):
        split_x(at_x(i))
        split_x(4 + at_x(i))
        return c

    def split_y(s):
        for k in range(2):
            arrived(yb.at[s, 1 - core, k], yr2.at[s, k])
        v = yb[s].reshape(BLK, HALF)
        hi, low = split(v)
        at = pl.ds(pl.multiple_of(s * BLK, BLK), BLK)
        yh_[at, :] = hi
        yl_[at, :] = low
        return hi, low, jnp.sum(v * v, axis=1, keepdims=True)

    for k in range(2):
        send(x_hbm.at[pl.ds(k * PIECE, PIECE), kother], xb.at[d, k], xr.at[d, k], pa)
    for k in range(2):
        mine = slot(0, "o")
        send(y_hbm.at[pl.ds(k * PIECE, PIECE), kother], yb.at[mine, core, k], yr.at[mine, k], pa)
    for k in range(2):
        cx_own[k].wait()
        send_x(d, k, xp)
        send_x(d, k, xm)
        cy_own[k].wait()
        send_y(mine, k, zp)
        send_y(mine, k, zm)
        send_y(mine, k, pb)
        cross_y(mine, k)

    for k in range(2):
        got_x(xa + x, k)
        send_x(xa + x, k, xp)
        send_x(xa + x, k, xm)
        got_y(slot(3, "o"), k)
        send_y(slot(3, "o"), k, zp)
        got_y(slot(0, "b"), k)
        send_y(slot(0, "b"), k, zm)
        got_y(slot(1, "o"), k)
        got_x(xo + at_x(1), k)
        got_x(xo + at_x(3), k)
        send_x(xo + at_x(3), k, xp)

    lax.fori_loop(0, 1, split_xs, 0)

    for k in range(2):
        got_y(slot(0, "a"), k)
        send_y(slot(0, "a"), k, zp)
        send_y(slot(0, "a"), k, zm)
        send_y(slot(0, "a"), k, pb)
        got_x(xa + at_x(1), k)
        send_x(xa + at_x(1), k, xm)
        got_x(xa + at_x(3), k)
        got_y(slot(2, "o"), k)
        got_y(slot(1, "b"), k)
    for k in range(2):
        send_y(slot(2, "o"), k, pb)
    lax.fori_loop(0, 2, lambda i, c: split_xs(1 + 2 * i, c), 0)

    for k in range(2):
        got_y(slot(0, "c"), k)
        send_y(slot(0, "c"), k, zp)
        got_y(slot(1, "a"), k)
        send_y(slot(1, "a"), k, zm)
        got_y(slot(3, "a"), k)
        got_x(xo + at_x(2), k)
        got_x(xa + at_x(2), k)
    for k in range(2):
        send_y(slot(0, "b"), k, zp)
        send_y(slot(0, "c"), k, zm)
    lax.fori_loop(2, 3, split_xs, 0)
    r = lax.broadcasted_iota(jnp.int32, (128, 128), 0)
    c = lax.broadcasted_iota(jnp.int32, (128, 128), 1)
    for i in range(3):
        piece = jnp.sum(jnp.where(r == c, xs[128 * i : 128 * i + 128, :], 0.0), axis=0, keepdims=True)
        rsq[:, 128 * i : 128 * i + 128] = jnp.broadcast_to(piece, (8, 128))

    def block(s):
        hi, low, csq = split_y(s)
        both = dot_nt(jnp.concatenate([hi, low], axis=0), xh[...])
        cross = both[:BLK] + both[BLK:] + dot_nt(hi, xl[...])
        return (2.0 * cross - csq - rsq[0:1, :]) * SCALE

    def pair_block(dz, is_c):
        k = (is_c * (1 - yhi) + (1 - is_c) * yhi) * 4 + at_z(dz)
        ps[k] = block((1 - h) * 8 + k)
        pltpu.make_async_remote_copy(
            src_ref=ps.at[k], dst_ref=pr.at[k], send_sem=prs.at[0, k], recv_sem=prs.at[1, k], device_id=pa, device_id_type=MESH
        ).start()

    def own_block(dz, is_b):
        k = (is_b * (1 - yhi) + (1 - is_b) * yhi) * 4 + at_z(dz)
        lg[pl.ds(pl.multiple_of(k * BLK, BLK), BLK), :] = block(h * 8 + k)

    def group1(i, c):
        pair_block(lax.rem(i, 2) + 2 * (i // 3), lax.rem(i // 2 + i // 3, 2))
        return c

    def group2(i, c):
        pair_block(2 + i, i)
        return c

    def group3(i, c):
        own_block(i, 0)
        return c

    def group4(i, c):
        pair_block(1 + i, 1)
        return c

    def group5(i, c):
        own_block(i, 1)
        return c

    lax.fori_loop(0, 4, group1, 0)
    for k in range(2):
        got_y(slot(2, "a"), k)
        send_y(slot(2, "a"), k, pb)
        got_y(slot(3, "c"), k)
        got_y(slot(2, "b"), k)
    lax.fori_loop(0, 2, group2, 0)
    lax.fori_loop(0, 4, group3, 0)
    for k in range(2):
        got_y(slot(1, "c"), k)
        got_y(slot(2, "c"), k)
        got_y(slot(3, "b"), k)
    lax.fori_loop(0, 2, group4, 0)
    lax.fori_loop(0, 4, group5, 0)

    def pair_wait(i, c):
        m8, s8 = c
        hi = (1 - i // 4) * yhi + (i // 4) * (1 - yhi)
        k = hi * 4 + at_z(lax.rem(3 * i, 4))
        cp = pltpu.make_async_remote_copy(
            src_ref=ps.at[k], dst_ref=pr.at[k], send_sem=prs.at[0, k], recv_sem=prs.at[1, k], device_id=pa, device_id_type=MESH
        )
        cp.wait_recv()
        cp.wait_send()
        at = pl.ds(pl.multiple_of(k * BLK, BLK), BLK)
        v = lg[at, :] + pr[k]
        lg[at, :] = v
        v = v.reshape(12, 8, ROWS)
        top = jnp.maximum(m8, jnp.max(v, axis=0))
        return top, s8 * jnp.exp(m8 - top) + jnp.sum(jnp.exp(v - top[None]), axis=0)

    m8, s8 = lax.fori_loop(0, NB, pair_wait, (jnp.full((8, ROWS), -1e30, F32), jnp.zeros((8, ROWS), F32)))

    def send_logits(k):
        at = pl.ds(LO_AT[k], LO_AT[k + 1] - LO_AT[k])
        send(lg.at[at], lo.at[at], lsem.at[k], pa)

    def got_logits(k):
        at = pl.ds(LO_AT[k], LO_AT[k + 1] - LO_AT[k])
        arrived(lo.at[at], lsem.at[k])

    def ex_rows(rnd, msg):
        rx[rnd, d] = msg

        def go_(k, c):
            p = lax.rem(d + k, 8)
            pltpu.make_async_remote_copy(
                src_ref=rx.at[rnd, d], dst_ref=rx.at[rnd, d], send_sem=rxs.at[0, rnd, p], recv_sem=rxs.at[1, rnd, d],
                device_id=(n, p), device_id_type=MESH,
            ).start()
            return c

        lax.fori_loop(1, 8, go_, 0, unroll=True)

        def done():
            def wt(k, c):
                p = lax.rem(d + k, 8)
                w = pltpu.make_async_remote_copy(
                    src_ref=rx.at[rnd, p], dst_ref=rx.at[rnd, p], send_sem=rxs.at[0, rnd, p], recv_sem=rxs.at[1, rnd, p],
                    device_id=(n, p), device_id_type=MESH,
                )
                w.wait_recv()
                return c

            lax.fori_loop(1, 8, wt, 0, unroll=True)
            return rx[rnd]

        return done

    def ex_cols(buf, sem, msg, rnd):
        buf[rnd, n] = msg

        def go_(k, c):
            p = lax.rem(n + k, 16)
            pltpu.make_async_remote_copy(
                src_ref=buf.at[rnd, n], dst_ref=buf.at[rnd, n], send_sem=sem.at[0, rnd, p], recv_sem=sem.at[1, rnd, n],
                device_id=col_dev(p), device_id_type=MESH,
            ).start()
            return c

        lax.fori_loop(1, 16, go_, 0, unroll=True)

        def done():
            def wt(k, c):
                p = lax.rem(n + k, 16)
                pltpu.make_async_remote_copy(
                    src_ref=buf.at[rnd, p], dst_ref=buf.at[rnd, p], send_sem=sem.at[0, rnd, p], recv_sem=sem.at[1, rnd, p],
                    device_id=col_dev(p), device_id_type=MESH,
                ).wait_recv()
                return c

            lax.fori_loop(1, 16, wt, 0, unroll=True)
            return buf[rnd]

        return done

    def row_msg(parts):
        parts = parts + [jnp.zeros((1, 128), F32)] * (8 - len(parts))
        return jnp.concatenate(parts, axis=0)

    def blk(k):
        return slice(BLK * k, BLK * k + BLK)

    m = jnp.max(m8, axis=0, keepdims=True)
    tot = jnp.sum(s8 * jnp.exp(m8 - m), axis=0, keepdims=True)
    done = ex_rows(0, row_msg(rows3(m) + rows3(tot)))
    send_logits(0)
    everyone = done()
    mm = everyone[:, 0:3, :]
    top = jnp.max(mm, axis=0)
    tt = jnp.sum(everyone[:, 3:6, :] * jnp.exp(mm - top[None]), axis=0)
    f1 = flat3(LOGN - top - jnp.log(tt))

    pm = jnp.zeros((8, 128), F32)
    pt = jnp.zeros((8, 128), F32)
    for k in range(NB):
        a = lg[blk(k), :] + f1
        cm = jnp.max(a, axis=1, keepdims=True)
        e = jnp.exp(a - cm)
        q_[blk(k), :] = e
        pm = pm + pack_block(k, cm)
        pt = pt + pack_block(k, jnp.sum(e, axis=1, keepdims=True))
    everyone = ex_cols(cx1, cx1s, jnp.concatenate([pm, pt], axis=0), 0)()
    mm = everyone[:, 0:8, :]
    top = jnp.max(mm, axis=0)
    tt = jnp.sum(everyone[:, 8:16, :] * jnp.exp(mm - top[None]), axis=0)
    used = lax.broadcasted_iota(jnp.int32, (8, 128), 1) < 96
    g1 = jnp.where(used, LOGN - top - jnp.log(jnp.where(used, tt, 1.0)), 0.0)
    go[0] = g1
    send(go.at[0], go.at[1], gs.at[0], pa)

    fac = jnp.exp(pm + g1)
    s8 = jnp.zeros((8, ROWS), F32)
    for k in range(NB):
        p = q_[blk(k), :] * unpack(fac, 12 * k, 12)
        q_[blk(k), :] = p
        s8 = s8 + jnp.sum(p.reshape(12, 8, ROWS), axis=0)

    def row_step(rnd, s8, between):
        done = ex_rows(rnd, row_msg(rows3(jnp.sum(s8, axis=0, keepdims=True))))
        between()
        return flat3(NSAMP / jnp.sum(done()[:, 0:3, :], axis=0))

    def col_step(rnd, u, between):
        pk = jnp.zeros((8, 128), F32)
        for k in range(NB):
            pk = pk + pack_block(k, jnp.sum(q_[blk(k), :] * u, axis=1, keepdims=True))
        done = ex_cols(cx, cxs, pk, rnd)
        between()
        tt = jnp.sum(done(), axis=0)
        return NSAMP / jnp.where(used, tt, 1.0)

    def row_sums(v):
        s8 = jnp.zeros((8, ROWS), F32)
        for k in range(NB):
            s8 = s8 + jnp.sum((q_[blk(k), :] * unpack(v, 12 * k, 12)).reshape(12, 8, ROWS), axis=0)
        return s8

    def turn(src, dst, some):
        for q in some:
            dst[:, 128 * q : 128 * q + 128] = src[128 * q : 128 * q + 128, :].T

    def far(some):
        for q in some:
            at = slice(128 * q, 128 * q + 128)
            po[:, at] = jnp.exp(lo[at, :] + f1 + unpack(go[1], 16 * q, 16)).T

    def in_row1():
        send_logits(1)
        turn(q_, pn, range(0, 3))

    def in_row2():
        send_logits(2)
        arrived(go.at[1], gs.at[0])
        got_logits(0)
        far(range(0, 2))

    def in_col2():
        got_logits(1)
        far(range(2, 4))
        got_logits(2)
        far(range(4, 6))

    u = row_step(1, s8, in_row1)
    v = col_step(0, u, lambda: turn(q_, pn, range(3, 6)))
    u = row_step(2, row_sums(v), in_row2)
    v = col_step(1, u, in_col2)
    vo[0] = v
    send(vo.at[0], vo.at[1], gs.at[1], pa)
    total = ex_rows(3, row_msg(rows3(jnp.sum(row_sums(v), axis=0, keepdims=True))))

    hi, low = split(pn[...] * packed_row(v))
    wh[0] = hi
    wl[0] = low

    own_rows = pl.ds(pl.multiple_of(h * COLS, COLS), COLS)
    far_rows = pl.ds(pl.multiple_of((1 - h) * COLS, COLS), COLS)

    def part(i, rows, cols):
        return (
            dot_nn(wh[i], yh_[rows, cols]) + dot_nn(wh[i], yl_[rows, cols]) + dot_nn(wl[i], yh_[rows, cols])
        )

    def cols_of(c):
        return pl.ds(CUTS[c], CUTS[c + 1] - CUTS[c])

    def cut(ref, i, c):
        return ref.at[i, :, cols_of(c)]

    def compute(c):
        t = part(0, own_rows, cols_of(c))
        if c == 0:
            arrived(vo.at[1], gs.at[1])
            hi, low = split(po[...] * packed_row(vo[1]))
            wh[1] = hi
            wl[1] = low
        t = t + part(1, far_rows, cols_of(c))
        tp[:, :, cols_of(c)] = t.reshape(8, OWN, CUTS[c + 1] - CUTS[c])

    def pass_on(i, to, k, c, dev):
        send(cut(tp, i, c), cut(to, k, c), (r1s if to is r1 else r2s).at[c, k], dev)

    def add(i, k, c):
        tp[i, :, cols_of(c)] = tp[i, :, cols_of(c)] + r1[k, :, cols_of(c)]

    def start_pair(c):
        pass_on(xa + at_x(2), r1, 0, c, xp)
        pass_on(xa + at_x(3), r2, 0, c, xm)

    def pass_pair(c):
        arrived(cut(r1, 0, c), r1s.at[c, 0])
        add(xa + at_x(1), 0, c)
        pass_on(xa + at_x(1), r2, 1, c, xp)

    def start_own(c):
        pass_on(xo + at_x(2), r1, 1, c, xm)

    def last_own(c):
        pass_on(xo + at_x(1), r2, 3, c, xp)

    def pass_own(c):
        arrived(cut(r1, 1, c), r1s.at[c, 1])
        add(xo + at_x(3), 1, c)
        pass_on(xo + at_x(3), r2, 2, c, xm)

    def both(i, c, k):
        for m in (k, k + 1):
            arrived(cut(r2, m, c), r2s.at[c, m])
        return tp[i, :, cols_of(c)] + r2[k, :, cols_of(c)] + r2[k + 1, :, cols_of(c)]

    def final_pair(c):
        tp[xa + x, :, cols_of(c)] = both(xa + x, c, 0)
        send(cut(tp, xa + x, c), pf.at[:, cols_of(c)], pfs.at[c], pa)

    for c in range(CH):
        compute(c)
        start_pair(c)
        start_own(c)
        if c:
            pass_pair(c - 1)
        else:
            last_own(c)
    pass_pair(CH - 1)
    for c in range(1, CH):
        last_own(c)

    fin = flat3(jnp.sum(total()[:, 0:3, :], axis=0))
    lane = lax.broadcasted_iota(jnp.int32, (OWN, ROWS), 1)
    row = lax.broadcasted_iota(jnp.int32, (OWN, ROWS), 0) + d * OWN
    norm = 1.0 / jnp.sum(jnp.where(lane == row, fin, 0.0), axis=1, keepdims=True)
    f_out[...] = EPS * (f1 + jnp.log(u))
    near = lax.broadcasted_iota(jnp.int32, (8, 128), 1) // 48 == yhi
    g_out[...] = EPS * packed_row(jnp.where(near, g1 + jnp.log(v), go[1] + jnp.log(vo[1])))

    for c in range(CH):
        final_pair(c)
        if c:
            pass_own(c - 1)
    pass_own(CH - 1)
    for c in range(CH):
        width = CUTS[c + 1] - CUTS[c]
        t_out[:, pl.ds(pl.multiple_of(h * HALF + CUTS[c], 256), width)] = both(xo + x, c, 2) * norm
    for c in range(CH):
        width = CUTS[c + 1] - CUTS[c]
        arrived(pf.at[:, cols_of(c)], pfs.at[c])
        t_out[:, pl.ds(pl.multiple_of((1 - h) * HALF + CUTS[c], 256), width)] = pf[:, cols_of(c)] * norm

    for cp in sent:
        cp.wait_send()

    def drain_rows(k, c):
        p = lax.rem(d + k, 8)
        for rnd in range(4):
            pltpu.make_async_remote_copy(
                src_ref=rx.at[rnd, d], dst_ref=rx.at[rnd, d], send_sem=rxs.at[0, rnd, p], recv_sem=rxs.at[1, rnd, d],
                device_id=(n, p), device_id_type=MESH,
            ).wait_send()
        return c

    def drain_cols(k, c):
        p = lax.rem(n + k, 16)
        for buf, sem, rnd in ((cx1, cx1s, 0), (cx, cxs, 0), (cx, cxs, 1)):
            pltpu.make_async_remote_copy(
                src_ref=buf.at[rnd, n], dst_ref=buf.at[rnd, n], send_sem=sem.at[0, rnd, p], recv_sem=sem.at[1, rnd, n],
                device_id=col_dev(p), device_id_type=MESH,
            ).wait_send()
        return c

    lax.fori_loop(1, 8, drain_rows, 0)
    lax.fori_loop(1, 16, drain_cols, 0)


def hand_out(t_in, f_in, g_in, t_out, f_out, g_out, sem):
    parts = [
        pltpu.make_async_copy(t_in.at[pl.ds(8 * k, 8)], t_out.at[pl.ds(8 * k, 8)], sem.at[k]) for k in range(OWN // 8)
    ]
    for cp in parts:
        cp.start()
    f_out[...] = f_in[...].reshape(ROWS)
    g_out[...] = g_in[...].reshape(COLS)
    for cp in parts:
        cp.wait()


def body(noise_latents, data_latents):
    dma = pltpu.SemaphoreType.DMA
    vm = pltpu.VMEM
    scratch = [
        vm((8, 2, PIECE, HALF), F32),
        vm((16, 2, 2, PIECE, HALF), F32),
        vm((ROWS, HALF), BF16),
        vm((ROWS, HALF), BF16),
        vm((2 * COLS, HALF), BF16),
        vm((2 * COLS, HALF), BF16),
        vm((ROWS, 128), F32),
        vm((8, ROWS), F32),
        vm((NB, BLK, ROWS), F32),
        vm((NB, BLK, ROWS), F32),
        vm((COLS, ROWS), F32),
        vm((COLS, ROWS), F32),
        vm((COLS, ROWS), F32),
        vm((ROWS, COLS), F32),
        vm((ROWS, COLS), F32),
        vm((2, ROWS, COLS), BF16),
        vm((2, ROWS, COLS), BF16),
        vm((8, OWN, HALF), F32),
        vm((2, OWN, HALF), F32),
        vm((4, OWN, HALF), F32),
        vm((OWN, HALF), F32),
        vm((4, 8, 8, 128), F32),
        vm((1, 16, 16, 128), F32),
        vm((2, 16, 8, 128), F32),
        vm((2, 8, 128), F32),
        vm((2, 8, 128), F32),
        dma((2, 2)),
        dma((8, 2)),
        dma((16, 2)),
        dma((16, 2)),
        dma((2, NB)),
        dma((3,)),
        dma((2, 4, 8)),
        dma((2, 1, 16)),
        dma((2, 2, 16)),
        dma((2,)),
        dma((CH, 2)),
        dma((CH, 4)),
        dma((CH,)),
        dma((192,)),
    ]
    t, f, g = pl.pallas_call(
        kernel,
        out_shape=(
            vm((OWN, WIDTH), F32),
            vm((1, ROWS), F32),
            vm((1, COLS), F32),
        ),
        in_specs=[pl.BlockSpec(memory_space=pl.ANY)] * 2,
        out_specs=(pl.BlockSpec(memory_space=pltpu.VMEM),) * 3,
        scratch_shapes=scratch,
        compiler_params=pltpu.CompilerParams(
            collective_id=0, has_side_effects=True, vmem_limit_bytes=60 * 2**20
        ),
        name="coupling",
    )(noise_latents, data_latents)
    return pl.pallas_call(
        hand_out,
        out_shape=(
            jax.ShapeDtypeStruct((OWN, WIDTH), F32),
            jax.ShapeDtypeStruct((ROWS,), F32),
            jax.ShapeDtypeStruct((COLS,), F32),
        ),
        in_specs=[pl.BlockSpec(memory_space=pltpu.VMEM)] * 3,
        out_specs=(pl.BlockSpec(memory_space=pl.ANY),) + (pl.BlockSpec(memory_space=pltpu.VMEM),) * 2,
        scratch_shapes=[pltpu.SemaphoreType.DMA((OWN // 8,))],
        compiler_params=pltpu.CompilerParams(vmem_limit_bytes=2 * 2**20),
        name="hand_out",
    )(t, f, g)


def solution(mesh):
    placed = (P(("noise", "dp"), None), P(("dp", "noise"), None))
    return jax.shard_map(
        body,
        mesh=mesh,
        in_specs=placed,
        out_specs=(P(("noise", "dp"), None), P("noise"), P("dp")),
        check_vma=False,
    )
```

```python
import functools
import math

import jax
import jax.numpy as jnp
from jax import lax
from jax.experimental import pallas as pl
from jax.experimental.pallas import tpu as pltpu
from jax.sharding import PartitionSpec as P

MESH = pl.DeviceIdType.MESH
F32 = jnp.float32
BF16 = jnp.bfloat16
EPS = 0.01

OWN = 48
WIDTH = 4096
HALF = WIDTH // 2
ROWS = 384
COLS = 768
BLK = 96
NB = COLS // BLK
PIECE = OWN // 2
LO_AT = (0, 256, 496, 672, 768)
NSAMP = 6144
LOGN = math.log(NSAMP)
SCALE = 1.0 / (WIDTH * EPS)
CUTS = (0, 256, 512, 1024, 1536, 2048)
CH = len(CUTS) - 1


def split(v):
    hi = v.astype(BF16)
    return hi, (v - hi.astype(F32)).astype(BF16)


def dot_nt(a, b):
    return lax.dot_general(a, b, (((1,), (1,)), ((), ())), preferred_element_type=F32)


def dot_nn(a, b):
    return lax.dot_general(a, b, (((1,), (0,)), ((), ())), preferred_element_type=F32)


def pack_block(k, val):
    v3 = val.reshape(12, 8, 1)
    lane = lax.broadcasted_iota(jnp.int32, (12, 8, 128), 2)
    lead = lax.broadcasted_iota(jnp.int32, (12, 8, 128), 0) + 12 * k
    return jnp.sum(jnp.where(lane == lead, v3, 0.0), axis=0)


def unpack(packed, first, count):
    lane = lax.broadcasted_iota(jnp.int32, (count, 8, 128), 2)
    lead = lax.broadcasted_iota(jnp.int32, (count, 8, 128), 0) + first
    v3 = jnp.sum(jnp.where(lane == lead, packed[None], 0.0), axis=2, keepdims=True)
    return v3.reshape(8 * count, 1)


def to_row(col):
    r = lax.broadcasted_iota(jnp.int32, (128, 128), 0)
    c = lax.broadcasted_iota(jnp.int32, (128, 128), 1)
    return jnp.sum(jnp.where(r == c, col, 0.0), axis=0, keepdims=True)


def packed_row(packed):
    return jnp.concatenate([to_row(unpack(packed, 16 * q, 16)) for q in range(6)], axis=1)


def rows3(v):
    return [v[:, 128 * q : 128 * q + 128] for q in range(3)]


def flat3(v):
    return jnp.concatenate([v[q : q + 1] for q in range(3)], axis=1)


def kernel(
    x_hbm, y_hbm, t_out, f_out, g_out,
    xb, yb, xh, xl, yh_, yl_, xs, rsq, ps, pr, lg, lo, q_, pn, po, wh, wl, tp, r1, r2, pf,
    rx, cx1, cx, go, vo,
    loc, xr, yr, yr2, prs, los, lsem, rxs, cx1s, cxs, gs, r1s, r2s, pfs, asem, tsem,
):
    n = lax.axis_index("noise")
    d = lax.axis_index("dp")
    core = lax.rem(n, 2)
    z = lax.rem(n // 2, 4)
    yhi = n // 8
    x = lax.rem(d, 4)
    ylo = d // 4
    h = lax.rem(yhi + ylo, 2)

    def at_z(k):
        return lax.rem(z + k, 4)

    def at_x(k):
        return lax.rem(x + k, 4)

    sib = (n + 1 - 2 * core, d)
    pa = (n, (1 - ylo) * 4 + x)
    pb = (((1 - yhi) * 4 + z) * 2 + core, (1 - ylo) * 4 + x)
    zp = ((yhi * 4 + at_z(1)) * 2 + core, d)
    zm = ((yhi * 4 + at_z(3)) * 2 + core, d)
    xp = (n, ylo * 4 + at_x(1))
    xm = (n, ylo * 4 + at_x(3))

    SRC = {"o": (yhi, h), "a": (yhi, 1 - h), "b": (1 - yhi, h), "c": (1 - yhi, 1 - h)}

    def slot(dz, who):
        hi, tile = SRC[who]
        return tile * 8 + hi * 4 + at_z(dz)

    def col_dev(p):
        return (p, lax.rem(p // 8 + h, 2) * 4 + x)

    kmine = pl.ds(pl.multiple_of(h * HALF, HALF), HALF)
    kother = pl.ds(pl.multiple_of((1 - h) * HALF, HALF), HALF)

    cx_own = [
        pltpu.make_async_copy(x_hbm.at[pl.ds(k * PIECE, PIECE), kmine], xb.at[d, k], loc.at[0, k]) for k in range(2)
    ]
    cy_own = [
        pltpu.make_async_copy(y_hbm.at[pl.ds(k * PIECE, PIECE), kmine], yb.at[slot(0, "o"), core, k], loc.at[1, k])
        for k in range(2)
    ]
    for cp in cx_own + cy_own:
        cp.start()

    barrier = pltpu.get_barrier_semaphore()

    for dev in (pa, pb, zp, zm, xp, xm, sib):
        pl.semaphore_signal(barrier, inc=1, device_id=dev, device_id_type=MESH)
    pl.semaphore_wait(barrier, 7)

    def send(src, dst, rsem, dev, ssend):
        pltpu.make_async_remote_copy(
            src_ref=src, dst_ref=dst, send_sem=ssend, recv_sem=rsem, device_id=dev, device_id_type=MESH
        ).start()

    def all_sent(ref, ssend):
        pltpu.make_async_remote_copy(
            src_ref=ref, dst_ref=ref, send_sem=ssend, recv_sem=lsem.at[0], device_id=sib, device_id_type=MESH
        ).wait_send()

    PA, PB, ZP, ZM, XP, XM, SIB = range(7)
    TO = [pa, pb, zp, zm, xp, xm, sib]

    def arrived(dst, rsem):
        pltpu.make_async_remote_copy(
            src_ref=dst, dst_ref=dst, send_sem=asem.at[0], recv_sem=rsem, device_id=sib, device_id_type=MESH
        ).wait_recv()

    def send_y(s, k, to):
        send(yb.at[s, core, k], yb.at[s, core, k], yr.at[s, k], TO[to], asem.at[to])

    def cross_y(s, k):
        send(yb.at[s, core, k], yb.at[s, core, k], yr2.at[s], sib, asem.at[SIB])

    def got_y(s, k):
        arrived(yb.at[s, core, k], yr.at[s, k])
        cross_y(s, k)

    def send_x(i, k, to):
        send(xb.at[i, k], xb.at[i, k], xr.at[i, k], TO[to], asem.at[to])

    def got_x(i, k):
        arrived(xb.at[i, k], xr.at[i, k])

    xa = (1 - ylo) * 4
    xo = ylo * 4

    def split_x(i):
        v = xb[i].reshape(OWN, HALF)
        hi, low = split(v)
        at = pl.ds(pl.multiple_of(i * OWN, OWN), OWN)
        xh[at, :] = hi
        xl[at, :] = low
        xs[at, :] = jnp.broadcast_to(jnp.sum(v * v, axis=1, keepdims=True), (OWN, 128))

    def split_xs(i, c):
        split_x(at_x(i))
        split_x(4 + at_x(i))
        return c

    def split_y(s):
        arrived(yb.at[s, 1 - core], yr2.at[s])
        v = yb[s].reshape(BLK, HALF)
        hi, low = split(v)
        at = pl.ds(pl.multiple_of(s * BLK, BLK), BLK)
        yh_[at, :] = hi
        yl_[at, :] = low
        return hi, low, jnp.sum(v * v, axis=1, keepdims=True)

    for k in range(2):
        send(x_hbm.at[pl.ds(k * PIECE, PIECE), kother], xb.at[d, k], xr.at[d, k], pa, asem.at[PA])
    for k in range(2):
        mine = slot(0, "o")
        send(y_hbm.at[pl.ds(k * PIECE, PIECE), kother], yb.at[mine, core, k], yr.at[mine, k], pa, asem.at[PA])
    for k in range(2):
        cx_own[k].wait()
        send_x(d, k, XP)
        send_x(d, k, XM)
        cy_own[k].wait()
        send_y(mine, k, ZP)
        send_y(mine, k, ZM)
        send_y(mine, k, PB)
        cross_y(mine, k)

    for k in range(2):
        got_x(xa + x, k)
        send_x(xa + x, k, XP)
        send_x(xa + x, k, XM)
        got_y(slot(3, "o"), k)
        send_y(slot(3, "o"), k, ZP)
        got_y(slot(0, "b"), k)
        send_y(slot(0, "b"), k, ZM)
        got_y(slot(1, "o"), k)
        got_x(xo + at_x(1), k)
        got_x(xo + at_x(3), k)
        send_x(xo + at_x(3), k, XP)

    lax.fori_loop(0, 1, split_xs, 0)

    for k in range(2):
        got_y(slot(0, "a"), k)
        send_y(slot(0, "a"), k, ZP)
        send_y(slot(0, "a"), k, ZM)
        send_y(slot(0, "a"), k, PB)
        got_x(xa + at_x(1), k)
        send_x(xa + at_x(1), k, XM)
        got_x(xa + at_x(3), k)
        got_y(slot(2, "o"), k)
        got_y(slot(1, "b"), k)
    for k in range(2):
        send_y(slot(2, "o"), k, PB)
    lax.fori_loop(0, 2, lambda i, c: split_xs(1 + 2 * i, c), 0)

    for k in range(2):
        got_y(slot(0, "c"), k)
        send_y(slot(0, "c"), k, ZP)
        got_y(slot(1, "a"), k)
        send_y(slot(1, "a"), k, ZM)
        got_y(slot(3, "a"), k)
        got_x(xo + at_x(2), k)
        got_x(xa + at_x(2), k)
    for k in range(2):
        send_y(slot(0, "b"), k, ZP)
        send_y(slot(0, "c"), k, ZM)
    lax.fori_loop(2, 3, split_xs, 0)
    r = lax.broadcasted_iota(jnp.int32, (128, 128), 0)
    c = lax.broadcasted_iota(jnp.int32, (128, 128), 1)
    for i in range(3):
        piece = jnp.sum(jnp.where(r == c, xs[128 * i : 128 * i + 128, :], 0.0), axis=0, keepdims=True)
        rsq[:, 128 * i : 128 * i + 128] = jnp.broadcast_to(piece, (8, 128))

    def block(s):
        hi, low, csq = split_y(s)
        both = dot_nt(jnp.concatenate([hi, low], axis=0), xh[...])
        cross = both[:BLK] + both[BLK:] + dot_nt(hi, xl[...])
        return (2.0 * cross - csq - rsq[0:1, :]) * SCALE

    def pair_block(dz, is_c):
        k = (is_c * (1 - yhi) + (1 - is_c) * yhi) * 4 + at_z(dz)
        ps[k] = block((1 - h) * 8 + k)
        pltpu.make_async_remote_copy(
            src_ref=ps.at[k], dst_ref=pr.at[k], send_sem=lsem.at[1], recv_sem=prs.at[k], device_id=pa, device_id_type=MESH
        ).start()

    def own_block(dz, is_b):
        k = (is_b * (1 - yhi) + (1 - is_b) * yhi) * 4 + at_z(dz)
        lg[pl.ds(pl.multiple_of(k * BLK, BLK), BLK), :] = block(h * 8 + k)

    def group1(i, c):
        pair_block(lax.rem(i, 2) + 2 * (i // 3), lax.rem(i // 2 + i // 3, 2))
        return c

    def group2(i, c):
        pair_block(2 + i, i)
        return c

    def group3(i, c):
        own_block(i, 0)
        return c

    def group4(i, c):
        pair_block(1 + i, 1)
        return c

    def group5(i, c):
        own_block(i, 1)
        return c

    lax.fori_loop(0, 4, group1, 0)
    for k in range(2):
        got_y(slot(2, "a"), k)
        send_y(slot(2, "a"), k, PB)
        got_y(slot(3, "c"), k)
        got_y(slot(2, "b"), k)
    lax.fori_loop(0, 2, group2, 0)
    lax.fori_loop(0, 4, group3, 0)
    for k in range(2):
        got_y(slot(1, "c"), k)
        got_y(slot(2, "c"), k)
        got_y(slot(3, "b"), k)
    lax.fori_loop(0, 2, group4, 0)
    lax.fori_loop(0, 4, group5, 0)

    def pair_wait(i, c):
        m8, s8 = c
        hi = (1 - i // 4) * yhi + (i // 4) * (1 - yhi)
        k = hi * 4 + at_z(lax.rem(3 * i, 4))
        arrived(pr.at[k], prs.at[k])
        at = pl.ds(pl.multiple_of(k * BLK, BLK), BLK)
        v = lg[at, :] + pr[k]
        lg[at, :] = v
        v = v.reshape(12, 8, ROWS)
        top = jnp.maximum(m8, jnp.max(v, axis=0))
        return top, s8 * jnp.exp(m8 - top) + jnp.sum(jnp.exp(v - top[None]), axis=0)

    m8, s8 = lax.fori_loop(0, NB, pair_wait, (jnp.full((8, ROWS), -1e30, F32), jnp.zeros((8, ROWS), F32)))

    def send_logits(k):
        at = pl.ds(LO_AT[k], LO_AT[k + 1] - LO_AT[k])
        send(lg.at[at], lo.at[at], los.at[k], pa, lsem.at[2])

    def got_logits(k):
        at = pl.ds(LO_AT[k], LO_AT[k + 1] - LO_AT[k])
        arrived(lo.at[at], los.at[k])

    def exchange(buf, sems, rnd, mine, peers, msg):
        buf[rnd, mine] = msg
        for dev in peers:
            pltpu.make_async_remote_copy(
                src_ref=buf.at[rnd, mine], dst_ref=buf.at[rnd, mine], send_sem=sems.at[0, rnd], recv_sem=sems.at[1, rnd],
                device_id=dev, device_id_type=MESH,
            ).start()
        every = buf.at[rnd, pl.ds(0, len(peers))]
        all_of = pltpu.make_async_remote_copy(
            src_ref=every, dst_ref=every, send_sem=sems.at[0, rnd], recv_sem=sems.at[1, rnd],
            device_id=peers[0], device_id_type=MESH,
        )
        small.append(all_of)

        def done():
            all_of.wait_recv()
            return buf[rnd]

        return done

    small = []
    row_peers = [(n, lax.rem(d + k, 8)) for k in range(1, 8)]
    col_peers = [col_dev(lax.rem(n + k, 16)) for k in range(1, 16)]

    def ex_rows(rnd, msg):
        return exchange(rx, rxs, rnd, d, row_peers, msg)

    def ex_cols(buf, sems, msg, rnd):
        return exchange(buf, sems, rnd, n, col_peers, msg)

    def row_msg(parts):
        parts = parts + [jnp.zeros((1, 128), F32)] * (8 - len(parts))
        return jnp.concatenate(parts, axis=0)

    def blk(k):
        return slice(BLK * k, BLK * k + BLK)

    m = jnp.max(m8, axis=0, keepdims=True)
    tot = jnp.sum(s8 * jnp.exp(m8 - m), axis=0, keepdims=True)
    done = ex_rows(0, row_msg(rows3(m) + rows3(tot)))
    send_logits(0)
    everyone = done()
    mm = everyone[:, 0:3, :]
    top = jnp.max(mm, axis=0)
    tt = jnp.sum(everyone[:, 3:6, :] * jnp.exp(mm - top[None]), axis=0)
    f1 = flat3(LOGN - top - jnp.log(tt))

    pm = jnp.zeros((8, 128), F32)
    pt = jnp.zeros((8, 128), F32)
    for k in range(NB):
        a = lg[blk(k), :] + f1
        cm = jnp.max(a, axis=1, keepdims=True)
        e = jnp.exp(a - cm)
        q_[blk(k), :] = e
        pm = pm + pack_block(k, cm)
        pt = pt + pack_block(k, jnp.sum(e, axis=1, keepdims=True))
    done = ex_cols(cx1, cx1s, jnp.concatenate([pm, pt], axis=0), 0)
    for ref, to in (
        (xb.at[pl.ds(0, 2)], PA),
        (yb.at[pl.ds(0, 4), core], PB),
        (yb.at[pl.ds(0, 5), core], ZP),
        (yb.at[pl.ds(0, 5), core], ZM),
        (xb.at[pl.ds(0, 3)], XP),
        (xb.at[pl.ds(0, 3)], XM),
        (yb.at[:, core], SIB),
    ):
        all_sent(ref, asem.at[to])
    all_sent(ps, lsem.at[1])
    everyone = done()
    mm = everyone[:, 0:8, :]
    top = jnp.max(mm, axis=0)
    tt = jnp.sum(everyone[:, 8:16, :] * jnp.exp(mm - top[None]), axis=0)
    used = lax.broadcasted_iota(jnp.int32, (8, 128), 1) < 96
    g1 = jnp.where(used, LOGN - top - jnp.log(jnp.where(used, tt, 1.0)), 0.0)
    go[0] = g1
    send(go.at[0], go.at[1], gs.at[0], pa, lsem.at[3])

    fac = jnp.exp(pm + g1)
    s8 = jnp.zeros((8, ROWS), F32)
    for k in range(NB):
        p = q_[blk(k), :] * unpack(fac, 12 * k, 12)
        q_[blk(k), :] = p
        s8 = s8 + jnp.sum(p.reshape(12, 8, ROWS), axis=0)

    def row_step(rnd, s8, between):
        done = ex_rows(rnd, row_msg(rows3(jnp.sum(s8, axis=0, keepdims=True))))
        between()
        return flat3(NSAMP / jnp.sum(done()[:, 0:3, :], axis=0))

    def col_step(rnd, u, between):
        pk = jnp.zeros((8, 128), F32)
        for k in range(NB):
            pk = pk + pack_block(k, jnp.sum(q_[blk(k), :] * u, axis=1, keepdims=True))
        done = ex_cols(cx, cxs, pk, rnd)
        between()
        tt = jnp.sum(done(), axis=0)
        return NSAMP / jnp.where(used, tt, 1.0)

    def row_sums(v):
        s8 = jnp.zeros((8, ROWS), F32)
        for k in range(NB):
            s8 = s8 + jnp.sum((q_[blk(k), :] * unpack(v, 12 * k, 12)).reshape(12, 8, ROWS), axis=0)
        return s8

    def turn(src, dst, some):
        for q in some:
            dst[:, 128 * q : 128 * q + 128] = src[128 * q : 128 * q + 128, :].T

    def far(some):
        for q in some:
            at = slice(128 * q, 128 * q + 128)
            po[:, at] = jnp.exp(lo[at, :] + f1 + unpack(go[1], 16 * q, 16)).T

    def in_row1():
        send_logits(1)
        turn(q_, pn, range(0, 3))

    def in_row2():
        send_logits(2)
        arrived(go.at[1], gs.at[0])
        got_logits(0)
        far(range(0, 2))

    def in_col2():
        send_logits(3)
        got_logits(1)
        far(range(2, 3))
        got_logits(2)
        far(range(3, 5))
        got_logits(3)
        far(range(5, 6))

    u = row_step(1, s8, in_row1)
    v = col_step(0, u, lambda: turn(q_, pn, range(3, 6)))
    u = row_step(2, row_sums(v), in_row2)
    v = col_step(1, u, in_col2)
    vo[0] = v
    send(vo.at[0], vo.at[1], gs.at[1], pa, lsem.at[4])
    total = ex_rows(3, row_msg(rows3(jnp.sum(row_sums(v), axis=0, keepdims=True))))

    hi, low = split(pn[...] * packed_row(v))
    wh[0] = hi
    wl[0] = low

    own_rows = pl.ds(pl.multiple_of(h * COLS, COLS), COLS)
    far_rows = pl.ds(pl.multiple_of((1 - h) * COLS, COLS), COLS)

    def part(i, rows, cols):
        return (
            dot_nn(wh[i], yh_[rows, cols]) + dot_nn(wh[i], yl_[rows, cols]) + dot_nn(wl[i], yh_[rows, cols])
        )

    def cols_of(c):
        return pl.ds(CUTS[c], CUTS[c + 1] - CUTS[c])

    def cut(ref, i, c):
        return ref.at[i, :, cols_of(c)]

    def compute(c):
        t = part(0, own_rows, cols_of(c))
        if c == 0:
            arrived(vo.at[1], gs.at[1])
            hi, low = split(po[...] * packed_row(vo[1]))
            wh[1] = hi
            wl[1] = low
        t = t + part(1, far_rows, cols_of(c))
        tp[:, :, cols_of(c)] = t.reshape(8, OWN, CUTS[c + 1] - CUTS[c])

    def pass_on(i, buf, k, c, to):
        sem = r1s.at[c, k] if buf is r1 else r2s.at[c, k // 2]
        send(cut(tp, i, c), cut(buf, k, c), sem, TO[to], tsem.at[to])

    def add(i, k, c):
        tp[i, :, cols_of(c)] = tp[i, :, cols_of(c)] + r1[k, :, cols_of(c)]

    def start_pair(c):
        pass_on(xa + at_x(2), r1, 0, c, XP)
        pass_on(xa + at_x(3), r2, 0, c, XM)

    def pass_pair(c):
        arrived(cut(r1, 0, c), r1s.at[c, 0])
        add(xa + at_x(1), 0, c)
        pass_on(xa + at_x(1), r2, 1, c, XP)

    def start_own(c):
        pass_on(xo + at_x(2), r1, 1, c, XM)

    def last_own(c):
        pass_on(xo + at_x(1), r2, 3, c, XP)

    def pass_own(c):
        arrived(cut(r1, 1, c), r1s.at[c, 1])
        add(xo + at_x(3), 1, c)
        pass_on(xo + at_x(3), r2, 2, c, XM)

    def both(i, c, k):
        arrived(r2.at[pl.ds(k, 2), :, cols_of(c)], r2s.at[c, k // 2])
        return tp[i, :, cols_of(c)] + r2[k, :, cols_of(c)] + r2[k + 1, :, cols_of(c)]

    def final_pair(c):
        tp[xa + x, :, cols_of(c)] = both(xa + x, c, 0)
        send(cut(tp, xa + x, c), pf.at[:, cols_of(c)], pfs, pa, tsem.at[PA])

    for c in range(CH):
        compute(c)
        start_pair(c)
        start_own(c)
        if c:
            pass_pair(c - 1)
        else:
            last_own(c)
    pass_pair(CH - 1)
    for c in range(1, CH):
        last_own(c)

    fin = flat3(jnp.sum(total()[:, 0:3, :], axis=0))
    lane = lax.broadcasted_iota(jnp.int32, (OWN, ROWS), 1)
    row = lax.broadcasted_iota(jnp.int32, (OWN, ROWS), 0) + d * OWN
    norm = 1.0 / jnp.sum(jnp.where(lane == row, fin, 0.0), axis=1, keepdims=True)
    f_out[...] = EPS * (f1 + jnp.log(u))
    near = lax.broadcasted_iota(jnp.int32, (8, 128), 1) // 48 == yhi
    g_out[...] = EPS * packed_row(jnp.where(near, g1 + jnp.log(v), go[1] + jnp.log(vo[1])))

    for c in range(CH):
        final_pair(c)
        if c:
            pass_own(c - 1)
    pass_own(CH - 1)
    for c in range(CH):
        width = CUTS[c + 1] - CUTS[c]
        t_out[:, pl.ds(pl.multiple_of(h * HALF + CUTS[c], 256), width)] = both(xo + x, c, 2) * norm
    arrived(pf, pfs)
    t_out[:, kother] = pf[...] * norm

    all_sent(lg, lsem.at[2])
    all_sent(go.at[0], lsem.at[3])
    all_sent(vo.at[0], lsem.at[4])
    all_sent(pf, tsem.at[PA])
    for to in (XP, XM):
        all_sent(tp.at[pl.ds(0, 3)], tsem.at[to])
    for cp in small:
        cp.wait_send()


def hand_out(t_in, f_in, g_in, t_out, f_out, g_out, sem):
    parts = [
        pltpu.make_async_copy(t_in.at[pl.ds(8 * k, 8)], t_out.at[pl.ds(8 * k, 8)], sem.at[k]) for k in range(OWN // 8)
    ]
    for cp in parts:
        cp.start()
    f_out[...] = f_in[...].reshape(ROWS)
    g_out[...] = g_in[...].reshape(COLS)
    for cp in parts:
        cp.wait()


def body(noise_latents, data_latents):
    dma = pltpu.SemaphoreType.DMA
    vm = pltpu.VMEM
    scratch = [
        vm((8, 2, PIECE, HALF), F32),
        vm((16, 2, 2, PIECE, HALF), F32),
        vm((ROWS, HALF), BF16),
        vm((ROWS, HALF), BF16),
        vm((2 * COLS, HALF), BF16),
        vm((2 * COLS, HALF), BF16),
        vm((ROWS, 128), F32),
        vm((8, ROWS), F32),
        vm((NB, BLK, ROWS), F32),
        vm((NB, BLK, ROWS), F32),
        vm((COLS, ROWS), F32),
        vm((COLS, ROWS), F32),
        vm((COLS, ROWS), F32),
        vm((ROWS, COLS), F32),
        vm((ROWS, COLS), F32),
        vm((2, ROWS, COLS), BF16),
        vm((2, ROWS, COLS), BF16),
        vm((8, OWN, HALF), F32),
        vm((2, OWN, HALF), F32),
        vm((4, OWN, HALF), F32),
        vm((OWN, HALF), F32),
        vm((4, 8, 8, 128), F32),
        vm((1, 16, 16, 128), F32),
        vm((2, 16, 8, 128), F32),
        vm((2, 8, 128), F32),
        vm((2, 8, 128), F32),
        dma((2, 2)),
        dma((8, 2)),
        dma((16, 2)),
        dma((16,)),
        dma((NB,)),
        dma((4,)),
        dma((5,)),
        dma((2, 4)),
        dma((2, 1)),
        dma((2, 2)),
        dma((2,)),
        dma((CH, 2)),
        dma((CH, 2)),
        dma,
        dma((7,)),
        dma((7,)),
    ]
    t, f, g = pl.pallas_call(
        kernel,
        out_shape=(
            vm((OWN, WIDTH), F32),
            vm((1, ROWS), F32),
            vm((1, COLS), F32),
        ),
        in_specs=[pl.BlockSpec(memory_space=pl.ANY)] * 2,
        out_specs=(pl.BlockSpec(memory_space=pltpu.VMEM),) * 3,
        scratch_shapes=scratch,
        compiler_params=pltpu.CompilerParams(
            collective_id=0, has_side_effects=True, vmem_limit_bytes=60 * 2**20
        ),
        name="coupling",
    )(noise_latents, data_latents)
    return pl.pallas_call(
        hand_out,
        out_shape=(
            jax.ShapeDtypeStruct((OWN, WIDTH), F32),
            jax.ShapeDtypeStruct((ROWS,), F32),
            jax.ShapeDtypeStruct((COLS,), F32),
        ),
        in_specs=[pl.BlockSpec(memory_space=pltpu.VMEM)] * 3,
        out_specs=(pl.BlockSpec(memory_space=pl.ANY),) + (pl.BlockSpec(memory_space=pltpu.VMEM),) * 2,
        scratch_shapes=[pltpu.SemaphoreType.DMA((OWN // 8,))],
        compiler_params=pltpu.CompilerParams(vmem_limit_bytes=2 * 2**20),
        name="hand_out",
    )(t, f, g)


def solution(mesh):
    placed = (P(("noise", "dp"), None), P(("dp", "noise"), None))
    return jax.shard_map(
        body,
        mesh=mesh,
        in_specs=placed,
        out_specs=(P(("noise", "dp"), None), P("noise"), P("dp")),
        check_vma=False,
    )
```

```python
import functools
import math

import jax
import jax.numpy as jnp
from jax import lax
from jax.experimental import pallas as pl
from jax.experimental.pallas import tpu as pltpu
from jax.sharding import PartitionSpec as P

MESH = pl.DeviceIdType.MESH
F32 = jnp.float32
BF16 = jnp.bfloat16
EPS = 0.01

OWN = 48
WIDTH = 4096
HALF = WIDTH // 2
ROWS = 384
COLS = 768
BLK = 96
NB = COLS // BLK
PIECE = OWN // 2
LO_AT = (0, 256, 496, 672, 768)
NSAMP = 6144
LOGN = math.log(NSAMP)
SCALE = 1.0 / (WIDTH * EPS)
CUTS = (0, 256, 512, 1024, 1536, 2048)
CH = len(CUTS) - 1


def split(v):
    hi = v.astype(BF16)
    return hi, (v - hi.astype(F32)).astype(BF16)


def dot_nt(a, b):
    return lax.dot_general(a, b, (((1,), (1,)), ((), ())), preferred_element_type=F32)


def dot_nn(a, b):
    return lax.dot_general(a, b, (((1,), (0,)), ((), ())), preferred_element_type=F32)


def pack_block(k, val):
    v3 = val.reshape(12, 8, 1)
    lane = lax.broadcasted_iota(jnp.int32, (12, 8, 128), 2)
    lead = lax.broadcasted_iota(jnp.int32, (12, 8, 128), 0) + 12 * k
    return jnp.sum(jnp.where(lane == lead, v3, 0.0), axis=0)


def unpack(packed, first, count):
    lane = lax.broadcasted_iota(jnp.int32, (count, 8, 128), 2)
    lead = lax.broadcasted_iota(jnp.int32, (count, 8, 128), 0) + first
    v3 = jnp.sum(jnp.where(lane == lead, packed[None], 0.0), axis=2, keepdims=True)
    return v3.reshape(8 * count, 1)


def to_row(col):
    r = lax.broadcasted_iota(jnp.int32, (128, 128), 0)
    c = lax.broadcasted_iota(jnp.int32, (128, 128), 1)
    return jnp.sum(jnp.where(r == c, col, 0.0), axis=0, keepdims=True)


def packed_row(packed):
    return jnp.concatenate([to_row(unpack(packed, 16 * q, 16)) for q in range(6)], axis=1)


def rows3(v):
    return [v[:, 128 * q : 128 * q + 128] for q in range(3)]


def flat3(v):
    return jnp.concatenate([v[q : q + 1] for q in range(3)], axis=1)


def kernel(
    x_hbm, y_hbm, t_out, f_out, g_out,
    xb, yb, xh, xl, yh_, yl_, xs, cse, rsq, ps, pr, lg, lo, q_, pn, po, wh, wl, tp, r1, r2, pf,
    rx, cx1, cx, go, vo,
    loc, xr, yr, yr2, prs, los, lsem, rxs, cx1s, cxs, gs, r1s, r2s, pfs, asem, tsem,
):
    n = lax.axis_index("noise")
    d = lax.axis_index("dp")
    core = lax.rem(n, 2)
    z = lax.rem(n // 2, 4)
    yhi = n // 8
    x = lax.rem(d, 4)
    ylo = d // 4
    h = lax.rem(yhi + ylo, 2)

    def at_z(k):
        return lax.rem(z + k, 4)

    def at_x(k):
        return lax.rem(x + k, 4)

    sib = (n + 1 - 2 * core, d)
    pa = (n, (1 - ylo) * 4 + x)
    pb = (((1 - yhi) * 4 + z) * 2 + core, (1 - ylo) * 4 + x)
    zp = ((yhi * 4 + at_z(1)) * 2 + core, d)
    zm = ((yhi * 4 + at_z(3)) * 2 + core, d)
    xp = (n, ylo * 4 + at_x(1))
    xm = (n, ylo * 4 + at_x(3))

    SRC = {"o": (yhi, h), "a": (yhi, 1 - h), "b": (1 - yhi, h), "c": (1 - yhi, 1 - h)}

    def slot(dz, who):
        hi, tile = SRC[who]
        return tile * 8 + hi * 4 + at_z(dz)

    def col_dev(p):
        return (p, lax.rem(p // 8 + h, 2) * 4 + x)

    kmine = pl.ds(pl.multiple_of(h * HALF, HALF), HALF)
    kother = pl.ds(pl.multiple_of((1 - h) * HALF, HALF), HALF)

    cx_own = [
        pltpu.make_async_copy(x_hbm.at[pl.ds(k * PIECE, PIECE), kmine], xb.at[d, k], loc.at[0, k]) for k in range(2)
    ]
    cy_own = [
        pltpu.make_async_copy(y_hbm.at[pl.ds(k * PIECE, PIECE), kmine], yb.at[slot(0, "o"), core, k], loc.at[1, k])
        for k in range(2)
    ]
    for cp in cx_own + cy_own:
        cp.start()

    barrier = pltpu.get_barrier_semaphore()

    for dev in (pa, pb, zp, zm, xp, xm, sib):
        pl.semaphore_signal(barrier, inc=1, device_id=dev, device_id_type=MESH)
    pl.semaphore_wait(barrier, 7)

    def send(src, dst, rsem, dev, ssend):
        pltpu.make_async_remote_copy(
            src_ref=src, dst_ref=dst, send_sem=ssend, recv_sem=rsem, device_id=dev, device_id_type=MESH
        ).start()

    def all_sent(ref, ssend):
        pltpu.make_async_remote_copy(
            src_ref=ref, dst_ref=ref, send_sem=ssend, recv_sem=lsem.at[0], device_id=sib, device_id_type=MESH
        ).wait_send()

    PA, PB, ZP, ZM, XP, XM, SIB = range(7)
    TO = [pa, pb, zp, zm, xp, xm, sib]

    def arrived(dst, rsem):
        pltpu.make_async_remote_copy(
            src_ref=dst, dst_ref=dst, send_sem=asem.at[0], recv_sem=rsem, device_id=sib, device_id_type=MESH
        ).wait_recv()

    def send_y(s, k, to):
        send(yb.at[s, core, k], yb.at[s, core, k], yr.at[s, k], TO[to], asem.at[to])

    def cross_y(s, k):
        send(yb.at[s, core, k], yb.at[s, core, k], yr2.at[s], sib, asem.at[SIB])

    def got_y(s, k):
        arrived(yb.at[s, core, k], yr.at[s, k])
        cross_y(s, k)

    def send_x(i, k, to):
        send(xb.at[i, k], xb.at[i, k], xr.at[i, k], TO[to], asem.at[to])

    def got_x(i, k):
        arrived(xb.at[i, k], xr.at[i, k])

    xa = (1 - ylo) * 4
    xo = ylo * 4

    def split_x(i):
        v = xb[i].reshape(OWN, HALF)
        hi, low = split(v)
        at = pl.ds(pl.multiple_of(i * OWN, OWN), OWN)
        xh[at, :] = hi
        xl[at, :] = low
        xs[at, :] = jnp.broadcast_to(jnp.sum(v * v, axis=1, keepdims=True), (OWN, 128))

    def fill_rsq(at):
        r = lax.broadcasted_iota(jnp.int32, (128, 128), 0)
        c = lax.broadcasted_iota(jnp.int32, (128, 128), 1)
        piece = jnp.sum(jnp.where(r == c, xs[at, :], 0.0), axis=0, keepdims=True)
        rsq[:, at] = jnp.broadcast_to(piece, (8, 128))

    def split_y(s):
        arrived(yb.at[s, 1 - core], yr2.at[s])
        v = yb[s].reshape(BLK, HALF)
        hi, low = split(v)
        at = pl.ds(pl.multiple_of(s * BLK, BLK), BLK)
        yh_[at, :] = hi
        yl_[at, :] = low
        return hi, low, jnp.sum(v * v, axis=1, keepdims=True)

    for k in range(2):
        send(x_hbm.at[pl.ds(k * PIECE, PIECE), kother], xb.at[d, k], xr.at[d, k], pa, asem.at[PA])
    for k in range(2):
        mine = slot(0, "o")
        send(y_hbm.at[pl.ds(k * PIECE, PIECE), kother], yb.at[mine, core, k], yr.at[mine, k], pa, asem.at[PA])
    for k in range(2):
        cx_own[k].wait()
        send_x(d, k, XP)
        send_x(d, k, XM)
        cy_own[k].wait()
        send_y(mine, k, ZP)
        send_y(mine, k, ZM)
        send_y(mine, k, PB)
        cross_y(mine, k)

    for k in range(2):
        got_x(xa + x, k)
        send_x(xa + x, k, XM)
        got_x(xo + at_x(3), k)
        send_x(xo + at_x(3), k, XP)
        got_y(slot(3, "o"), k)
        send_y(slot(3, "o"), k, ZP)
        got_y(slot(0, "b"), k)
        send_y(slot(0, "b"), k, ZM)
        got_y(slot(1, "o"), k)
        got_x(xo + at_x(1), k)
    for k in range(2):
        send_x(xa + x, k, XP)

    def split_first(i, c):
        split_x(lax.rem(i // 3 + ylo, 2) * 4 + at_x(lax.rem(i + i // 2, 4) * (1 - i // 3)))
        return c

    lax.fori_loop(0, 4, split_first, 0)

    for k in range(2):
        got_y(slot(0, "a"), k)
        send_y(slot(0, "a"), k, ZP)
        send_y(slot(0, "a"), k, ZM)
        send_y(slot(0, "a"), k, PB)
        got_x(xa + at_x(1), k)
        send_x(xa + at_x(1), k, XM)
        got_x(xo + at_x(2), k)
        got_y(slot(2, "o"), k)
        got_y(slot(1, "b"), k)
    for k in range(2):
        send_y(slot(2, "o"), k, PB)

    def split_second(i, c):
        split_x(lax.rem(i + ylo, 2) * 4 + at_x(2 - i))
        return c

    lax.fori_loop(0, 2, split_second, 0)

    first = pl.ds(pl.multiple_of(256 * ylo, 128), 128)
    rest = pl.ds(pl.multiple_of(128 * (1 - ylo), 128), 256)
    fill_rsq(first)

    def pair_send(k, lanes):
        at = (k,) if lanes is None else (k, slice(None), lanes)
        pltpu.make_async_remote_copy(
            src_ref=ps.at[at], dst_ref=pr.at[at], send_sem=lsem.at[1], recv_sem=prs.at[k], device_id=pa, device_id_type=MESH
        ).start()

    def cross_part(hi, low, csq, lanes):
        both = dot_nt(jnp.concatenate([hi, low], axis=0), xh[lanes, :])
        cross = both[:BLK] + both[BLK:] + dot_nt(hi, xl[lanes, :])
        return (2.0 * cross - csq - rsq[0:1, lanes]) * SCALE

    def pair_first(e, k):
        hi, low, csq = split_y((1 - h) * 8 + k)
        cse[e] = jnp.broadcast_to(csq, (BLK, 128))
        ps[k, :, first] = cross_part(hi, low, csq, first)
        pair_send(k, first)

    def pair_rest(e, k):
        at = pl.ds(pl.multiple_of(((1 - h) * 8 + k) * BLK, BLK), BLK)
        ps[k, :, rest] = cross_part(yh_[at, :], yl_[at, :], cse[e, :, 0:1], rest)
        pair_send(k, rest)

    ka = yhi * 4 + z
    kc = (1 - yhi) * 4 + z
    pair_first(0, ka)

    for k in range(2):
        got_y(slot(0, "c"), k)
        send_y(slot(0, "c"), k, ZP)
        if k:
            pair_first(1, kc)
        got_y(slot(1, "a"), k)
        send_y(slot(1, "a"), k, ZM)
        got_y(slot(3, "a"), k)
        got_x(xa + at_x(3), k)
        got_x(xa + at_x(2), k)
    for k in range(2):
        send_y(slot(0, "b"), k, ZP)
        send_y(slot(0, "c"), k, ZM)

    def split_third(i, c):
        split_x(xa + at_x(2 + i))
        return c

    lax.fori_loop(0, 2, split_third, 0)
    for i in range(3):
        fill_rsq(pl.ds(128 * i, 128))

    def block(s):
        hi, low, csq = split_y(s)
        return cross_part(hi, low, csq, slice(None))

    def pair_block(dz, is_c):
        k = (is_c * (1 - yhi) + (1 - is_c) * yhi) * 4 + at_z(dz)
        ps[k] = block((1 - h) * 8 + k)
        pair_send(k, None)

    def own_block(dz, is_b):
        k = (is_b * (1 - yhi) + (1 - is_b) * yhi) * 4 + at_z(dz)
        lg[pl.ds(pl.multiple_of(k * BLK, BLK), BLK), :] = block(h * 8 + k)

    def group1(i, c):
        pair_block(1 + 2 * i, 0)
        return c

    def group2(i, c):
        pair_block(2 + i, i)
        return c

    def group3(i, c):
        own_block(i, 0)
        return c

    def group4(i, c):
        pair_block(1 + i, 1)
        return c

    def group5(i, c):
        own_block(i, 1)
        return c

    pair_rest(0, ka)
    pair_rest(1, kc)
    lax.fori_loop(0, 2, group1, 0)
    for k in range(2):
        got_y(slot(2, "a"), k)
        send_y(slot(2, "a"), k, PB)
        got_y(slot(3, "c"), k)
        got_y(slot(2, "b"), k)
    lax.fori_loop(0, 2, group2, 0)
    lax.fori_loop(0, 4, group3, 0)
    for k in range(2):
        got_y(slot(1, "c"), k)
        got_y(slot(2, "c"), k)
        got_y(slot(3, "b"), k)
    lax.fori_loop(0, 2, group4, 0)
    lax.fori_loop(0, 4, group5, 0)

    def pair_wait(i, c):
        m8, s8 = c
        hi = (1 - i // 4) * yhi + (i // 4) * (1 - yhi)
        k = hi * 4 + at_z(lax.rem(3 * i, 4))
        arrived(pr.at[k], prs.at[k])
        at = pl.ds(pl.multiple_of(k * BLK, BLK), BLK)
        v = lg[at, :] + pr[k]
        lg[at, :] = v
        v = v.reshape(12, 8, ROWS)
        top = jnp.maximum(m8, jnp.max(v, axis=0))
        return top, s8 * jnp.exp(m8 - top) + jnp.sum(jnp.exp(v - top[None]), axis=0)

    m8, s8 = lax.fori_loop(0, NB, pair_wait, (jnp.full((8, ROWS), -1e30, F32), jnp.zeros((8, ROWS), F32)))

    def send_logits(k):
        at = pl.ds(LO_AT[k], LO_AT[k + 1] - LO_AT[k])
        send(lg.at[at], lo.at[at], los.at[k], pa, lsem.at[2])

    def got_logits(k):
        at = pl.ds(LO_AT[k], LO_AT[k + 1] - LO_AT[k])
        arrived(lo.at[at], los.at[k])

    def exchange(buf, sems, rnd, mine, peers, msg):
        buf[rnd, mine] = msg
        for dev in peers:
            pltpu.make_async_remote_copy(
                src_ref=buf.at[rnd, mine], dst_ref=buf.at[rnd, mine], send_sem=sems.at[0, rnd], recv_sem=sems.at[1, rnd],
                device_id=dev, device_id_type=MESH,
            ).start()
        every = buf.at[rnd, pl.ds(0, len(peers))]
        all_of = pltpu.make_async_remote_copy(
            src_ref=every, dst_ref=every, send_sem=sems.at[0, rnd], recv_sem=sems.at[1, rnd],
            device_id=peers[0], device_id_type=MESH,
        )
        small.append(all_of)

        def done():
            all_of.wait_recv()
            return buf[rnd]

        return done

    small = []
    row_peers = [(n, lax.rem(d + k, 8)) for k in range(1, 8)]
    col_peers = [col_dev(lax.rem(n + k, 16)) for k in range(1, 16)]

    def ex_rows(rnd, msg):
        return exchange(rx, rxs, rnd, d, row_peers, msg)

    def ex_cols(buf, sems, msg, rnd):
        return exchange(buf, sems, rnd, n, col_peers, msg)

    def row_msg(parts):
        parts = parts + [jnp.zeros((1, 128), F32)] * (8 - len(parts))
        return jnp.concatenate(parts, axis=0)

    def blk(k):
        return slice(BLK * k, BLK * k + BLK)

    m = jnp.max(m8, axis=0, keepdims=True)
    tot = jnp.sum(s8 * jnp.exp(m8 - m), axis=0, keepdims=True)
    done = ex_rows(0, row_msg(rows3(m) + rows3(tot)))
    send_logits(0)
    everyone = done()
    mm = everyone[:, 0:3, :]
    top = jnp.max(mm, axis=0)
    tt = jnp.sum(everyone[:, 3:6, :] * jnp.exp(mm - top[None]), axis=0)
    f1 = flat3(LOGN - top - jnp.log(tt))

    pm = jnp.zeros((8, 128), F32)
    pt = jnp.zeros((8, 128), F32)
    for k in range(NB):
        a = lg[blk(k), :] + f1
        cm = jnp.max(a, axis=1, keepdims=True)
        e = jnp.exp(a - cm)
        q_[blk(k), :] = e
        pm = pm + pack_block(k, cm)
        pt = pt + pack_block(k, jnp.sum(e, axis=1, keepdims=True))
    done = ex_cols(cx1, cx1s, jnp.concatenate([pm, pt], axis=0), 0)
    for ref, to in (
        (xb.at[pl.ds(0, 2)], PA),
        (yb.at[pl.ds(0, 4), core], PB),
        (yb.at[pl.ds(0, 5), core], ZP),
        (yb.at[pl.ds(0, 5), core], ZM),
        (xb.at[pl.ds(0, 3)], XP),
        (xb.at[pl.ds(0, 3)], XM),
        (yb.at[:, core], SIB),
    ):
        all_sent(ref, asem.at[to])
    all_sent(ps, lsem.at[1])
    everyone = done()
    mm = everyone[:, 0:8, :]
    top = jnp.max(mm, axis=0)
    tt = jnp.sum(everyone[:, 8:16, :] * jnp.exp(mm - top[None]), axis=0)
    used = lax.broadcasted_iota(jnp.int32, (8, 128), 1) < 96
    g1 = jnp.where(used, LOGN - top - jnp.log(jnp.where(used, tt, 1.0)), 0.0)
    go[0] = g1
    send(go.at[0], go.at[1], gs.at[0], pa, lsem.at[3])

    fac = jnp.exp(pm + g1)
    s8 = jnp.zeros((8, ROWS), F32)
    for k in range(NB):
        p = q_[blk(k), :] * unpack(fac, 12 * k, 12)
        q_[blk(k), :] = p
        s8 = s8 + jnp.sum(p.reshape(12, 8, ROWS), axis=0)

    def row_step(rnd, s8, between):
        done = ex_rows(rnd, row_msg(rows3(jnp.sum(s8, axis=0, keepdims=True))))
        between()
        return flat3(NSAMP / jnp.sum(done()[:, 0:3, :], axis=0))

    def col_step(rnd, u, between):
        pk = jnp.zeros((8, 128), F32)
        for k in range(NB):
            pk = pk + pack_block(k, jnp.sum(q_[blk(k), :] * u, axis=1, keepdims=True))
        done = ex_cols(cx, cxs, pk, rnd)
        between()
        tt = jnp.sum(done(), axis=0)
        return NSAMP / jnp.where(used, tt, 1.0)

    def row_sums(v):
        s8 = jnp.zeros((8, ROWS), F32)
        for k in range(NB):
            s8 = s8 + jnp.sum((q_[blk(k), :] * unpack(v, 12 * k, 12)).reshape(12, 8, ROWS), axis=0)
        return s8

    def turn(src, dst, some):
        for q in some:
            dst[:, 128 * q : 128 * q + 128] = src[128 * q : 128 * q + 128, :].T

    def far(some):
        for q in some:
            at = slice(128 * q, 128 * q + 128)
            po[:, at] = jnp.exp(lo[at, :] + f1 + unpack(go[1], 16 * q, 16)).T

    def in_row1():
        send_logits(1)
        turn(q_, pn, range(0, 3))

    def in_row2():
        send_logits(2)
        arrived(go.at[1], gs.at[0])
        got_logits(0)
        far(range(0, 2))

    def in_col2():
        send_logits(3)
        got_logits(1)
        far(range(2, 3))
        got_logits(2)
        far(range(3, 5))
        got_logits(3)
        far(range(5, 6))

    u = row_step(1, s8, in_row1)
    v = col_step(0, u, lambda: turn(q_, pn, range(3, 6)))
    u = row_step(2, row_sums(v), in_row2)
    v = col_step(1, u, in_col2)
    vo[0] = v
    send(vo.at[0], vo.at[1], gs.at[1], pa, lsem.at[4])
    total = ex_rows(3, row_msg(rows3(jnp.sum(row_sums(v), axis=0, keepdims=True))))

    hi, low = split(pn[...] * packed_row(v))
    wh[0] = hi
    wl[0] = low

    own_rows = pl.ds(pl.multiple_of(h * COLS, COLS), COLS)
    far_rows = pl.ds(pl.multiple_of((1 - h) * COLS, COLS), COLS)

    def part(i, rows, cols):
        return (
            dot_nn(wh[i], yh_[rows, cols]) + dot_nn(wh[i], yl_[rows, cols]) + dot_nn(wl[i], yh_[rows, cols])
        )

    def cols_of(c):
        return pl.ds(CUTS[c], CUTS[c + 1] - CUTS[c])

    def cut(ref, i, c):
        return ref.at[i, :, cols_of(c)]

    def compute(c):
        t = part(0, own_rows, cols_of(c))
        if c == 0:
            arrived(vo.at[1], gs.at[1])
            hi, low = split(po[...] * packed_row(vo[1]))
            wh[1] = hi
            wl[1] = low
        t = t + part(1, far_rows, cols_of(c))
        tp[:, :, cols_of(c)] = t.reshape(8, OWN, CUTS[c + 1] - CUTS[c])

    def pass_on(i, buf, k, c, to):
        sem = r1s.at[c, k] if buf is r1 else r2s.at[c, k // 2]
        send(cut(tp, i, c), cut(buf, k, c), sem, TO[to], tsem.at[to])

    def add(i, k, c):
        tp[i, :, cols_of(c)] = tp[i, :, cols_of(c)] + r1[k, :, cols_of(c)]

    def start_pair(c):
        pass_on(xa + at_x(2), r1, 0, c, XP)
        pass_on(xa + at_x(3), r2, 0, c, XM)

    def pass_pair(c):
        arrived(cut(r1, 0, c), r1s.at[c, 0])
        add(xa + at_x(1), 0, c)
        pass_on(xa + at_x(1), r2, 1, c, XP)

    def start_own(c):
        pass_on(xo + at_x(2), r1, 1, c, XM)

    def last_own(c):
        pass_on(xo + at_x(1), r2, 3, c, XP)

    def pass_own(c):
        arrived(cut(r1, 1, c), r1s.at[c, 1])
        add(xo + at_x(3), 1, c)
        pass_on(xo + at_x(3), r2, 2, c, XM)

    def both(i, c, k):
        arrived(r2.at[pl.ds(k, 2), :, cols_of(c)], r2s.at[c, k // 2])
        return tp[i, :, cols_of(c)] + r2[k, :, cols_of(c)] + r2[k + 1, :, cols_of(c)]

    def final_pair(c):
        tp[xa + x, :, cols_of(c)] = both(xa + x, c, 0)
        send(cut(tp, xa + x, c), pf.at[:, cols_of(c)], pfs, pa, tsem.at[PA])

    for c in range(CH):
        compute(c)
        start_pair(c)
        start_own(c)
        if c:
            pass_pair(c - 1)
        else:
            last_own(c)
    pass_pair(CH - 1)
    for c in range(1, CH):
        last_own(c)

    fin = flat3(jnp.sum(total()[:, 0:3, :], axis=0))
    lane = lax.broadcasted_iota(jnp.int32, (OWN, ROWS), 1)
    row = lax.broadcasted_iota(jnp.int32, (OWN, ROWS), 0) + d * OWN
    norm = 1.0 / jnp.sum(jnp.where(lane == row, fin, 0.0), axis=1, keepdims=True)
    f_out[...] = EPS * (f1 + jnp.log(u))
    near = lax.broadcasted_iota(jnp.int32, (8, 128), 1) // 48 == yhi
    g_out[...] = EPS * packed_row(jnp.where(near, g1 + jnp.log(v), go[1] + jnp.log(vo[1])))

    for c in range(CH):
        final_pair(c)
        if c:
            pass_own(c - 1)
    pass_own(CH - 1)
    for c in range(CH):
        width = CUTS[c + 1] - CUTS[c]
        t_out[:, pl.ds(pl.multiple_of(h * HALF + CUTS[c], 256), width)] = both(xo + x, c, 2) * norm
    arrived(pf, pfs)
    t_out[:, kother] = pf[...] * norm

    all_sent(lg, lsem.at[2])
    all_sent(go.at[0], lsem.at[3])
    all_sent(vo.at[0], lsem.at[4])
    all_sent(pf, tsem.at[PA])
    for to in (XP, XM):
        all_sent(tp.at[pl.ds(0, 3)], tsem.at[to])
    for cp in small:
        cp.wait_send()


def hand_out(t_in, f_in, g_in, t_out, f_out, g_out, sem):
    parts = [
        pltpu.make_async_copy(t_in.at[pl.ds(8 * k, 8)], t_out.at[pl.ds(8 * k, 8)], sem.at[k]) for k in range(OWN // 8)
    ]
    for cp in parts:
        cp.start()
    f_out[...] = f_in[...].reshape(ROWS)
    g_out[...] = g_in[...].reshape(COLS)
    for cp in parts:
        cp.wait()


def body(noise_latents, data_latents):
    dma = pltpu.SemaphoreType.DMA
    vm = pltpu.VMEM
    scratch = [
        vm((8, 2, PIECE, HALF), F32),
        vm((16, 2, 2, PIECE, HALF), F32),
        vm((ROWS, HALF), BF16),
        vm((ROWS, HALF), BF16),
        vm((2 * COLS, HALF), BF16),
        vm((2 * COLS, HALF), BF16),
        vm((ROWS, 128), F32),
        vm((2, BLK, 128), F32),
        vm((8, ROWS), F32),
        vm((NB, BLK, ROWS), F32),
        vm((NB, BLK, ROWS), F32),
        vm((COLS, ROWS), F32),
        vm((COLS, ROWS), F32),
        vm((COLS, ROWS), F32),
        vm((ROWS, COLS), F32),
        vm((ROWS, COLS), F32),
        vm((2, ROWS, COLS), BF16),
        vm((2, ROWS, COLS), BF16),
        vm((8, OWN, HALF), F32),
        vm((2, OWN, HALF), F32),
        vm((4, OWN, HALF), F32),
        vm((OWN, HALF), F32),
        vm((4, 8, 8, 128), F32),
        vm((1, 16, 16, 128), F32),
        vm((2, 16, 8, 128), F32),
        vm((2, 8, 128), F32),
        vm((2, 8, 128), F32),
        dma((2, 2)),
        dma((8, 2)),
        dma((16, 2)),
        dma((16,)),
        dma((NB,)),
        dma((4,)),
        dma((5,)),
        dma((2, 4)),
        dma((2, 1)),
        dma((2, 2)),
        dma((2,)),
        dma((CH, 2)),
        dma((CH, 2)),
        dma,
        dma((7,)),
        dma((7,)),
    ]
    t, f, g = pl.pallas_call(
        kernel,
        out_shape=(
            vm((OWN, WIDTH), F32),
            vm((1, ROWS), F32),
            vm((1, COLS), F32),
        ),
        in_specs=[pl.BlockSpec(memory_space=pl.ANY)] * 2,
        out_specs=(pl.BlockSpec(memory_space=pltpu.VMEM),) * 3,
        scratch_shapes=scratch,
        compiler_params=pltpu.CompilerParams(
            collective_id=0, has_side_effects=True, vmem_limit_bytes=60 * 2**20
        ),
        name="coupling",
    )(noise_latents, data_latents)
    return pl.pallas_call(
        hand_out,
        out_shape=(
            jax.ShapeDtypeStruct((OWN, WIDTH), F32),
            jax.ShapeDtypeStruct((ROWS,), F32),
            jax.ShapeDtypeStruct((COLS,), F32),
        ),
        in_specs=[pl.BlockSpec(memory_space=pltpu.VMEM)] * 3,
        out_specs=(pl.BlockSpec(memory_space=pl.ANY),) + (pl.BlockSpec(memory_space=pltpu.VMEM),) * 2,
        scratch_shapes=[pltpu.SemaphoreType.DMA((OWN // 8,))],
        compiler_params=pltpu.CompilerParams(vmem_limit_bytes=2 * 2**20),
        name="hand_out",
    )(t, f, g)


def solution(mesh):
    placed = (P(("noise", "dp"), None), P(("dp", "noise"), None))
    return jax.shard_map(
        body,
        mesh=mesh,
        in_specs=placed,
        out_specs=(P(("noise", "dp"), None), P("noise"), P("dp")),
        check_vma=False,
    )
```

```python
import functools
import math

import jax
import jax.numpy as jnp
from jax import lax
from jax.experimental import pallas as pl
from jax.experimental.pallas import tpu as pltpu
from jax.sharding import PartitionSpec as P

MESH = pl.DeviceIdType.MESH
F32 = jnp.float32
BF16 = jnp.bfloat16
EPS = 0.01

OWN = 48
WIDTH = 4096
HALF = WIDTH // 2
ROWS = 384
COLS = 768
BLK = 96
NB = COLS // BLK
PIECE = OWN // 2
LO_AT = (0, 64, 320, 384, 560, 768)
NSAMP = 6144
LOGN = math.log(NSAMP)
SCALE = 1.0 / (WIDTH * EPS)
CUTS = (0, 256, 512, 1024, 1536, 2048)
CH = len(CUTS) - 1


def split(v):
    hi = v.astype(BF16)
    return hi, (v - hi.astype(F32)).astype(BF16)


def dot_nt(a, b):
    return lax.dot_general(a, b, (((1,), (1,)), ((), ())), preferred_element_type=F32)


def dot_nn(a, b):
    return lax.dot_general(a, b, (((1,), (0,)), ((), ())), preferred_element_type=F32)


def pack_block(k, val):
    v3 = val.reshape(12, 8, 1)
    lane = lax.broadcasted_iota(jnp.int32, (12, 8, 128), 2)
    lead = lax.broadcasted_iota(jnp.int32, (12, 8, 128), 0) + 12 * k
    return jnp.sum(jnp.where(lane == lead, v3, 0.0), axis=0)


def unpack(packed, first, count):
    lane = lax.broadcasted_iota(jnp.int32, (count, 8, 128), 2)
    lead = lax.broadcasted_iota(jnp.int32, (count, 8, 128), 0) + first
    v3 = jnp.sum(jnp.where(lane == lead, packed[None], 0.0), axis=2, keepdims=True)
    return v3.reshape(8 * count, 1)


def to_row(col):
    r = lax.broadcasted_iota(jnp.int32, (128, 128), 0)
    c = lax.broadcasted_iota(jnp.int32, (128, 128), 1)
    return jnp.sum(jnp.where(r == c, col, 0.0), axis=0, keepdims=True)


def packed_row(packed):
    return jnp.concatenate([to_row(unpack(packed, 16 * q, 16)) for q in range(6)], axis=1)


def rows3(v):
    return [v[:, 128 * q : 128 * q + 128] for q in range(3)]


def flat3(v):
    return jnp.concatenate([v[q : q + 1] for q in range(3)], axis=1)


def kernel(
    x_hbm, y_hbm, t_out, f_out, g_out,
    xb, yb, xh, xl, yh_, yl_, xs, cse, rsq, ps, pr, lg, lo, q_, pn, po, wh, wl, tp, r1, r2, pf,
    rx, cx1, cx, go, vo,
    loc, xr, yr, yr2, prs, los, lsem, rxs, cx1s, cxs, gs, r1s, r2s, pfs, asem, tsem,
):
    n = lax.axis_index("noise")
    d = lax.axis_index("dp")
    core = lax.rem(n, 2)
    z = lax.rem(n // 2, 4)
    yhi = n // 8
    x = lax.rem(d, 4)
    ylo = d // 4
    h = lax.rem(yhi + ylo, 2)

    def at_z(k):
        return lax.rem(z + k, 4)

    def at_x(k):
        return lax.rem(x + k, 4)

    sib = (n + 1 - 2 * core, d)
    pa = (n, (1 - ylo) * 4 + x)
    pb = (((1 - yhi) * 4 + z) * 2 + core, (1 - ylo) * 4 + x)
    zp = ((yhi * 4 + at_z(1)) * 2 + core, d)
    zm = ((yhi * 4 + at_z(3)) * 2 + core, d)
    xp = (n, ylo * 4 + at_x(1))
    xm = (n, ylo * 4 + at_x(3))

    SRC = {"o": (yhi, h), "a": (yhi, 1 - h), "b": (1 - yhi, h), "c": (1 - yhi, 1 - h)}

    def slot(dz, who):
        hi, tile = SRC[who]
        return tile * 8 + hi * 4 + at_z(dz)

    def col_dev(p):
        return (p, lax.rem(p // 8 + h, 2) * 4 + x)

    kmine = pl.ds(pl.multiple_of(h * HALF, HALF), HALF)
    kother = pl.ds(pl.multiple_of((1 - h) * HALF, HALF), HALF)

    cx_own = [
        pltpu.make_async_copy(x_hbm.at[pl.ds(k * PIECE, PIECE), kmine], xb.at[d, k], loc.at[0, k]) for k in range(2)
    ]
    cy_own = [
        pltpu.make_async_copy(y_hbm.at[pl.ds(k * PIECE, PIECE), kmine], yb.at[slot(0, "o"), core, k], loc.at[1, k])
        for k in range(2)
    ]
    for cp in cx_own + cy_own:
        cp.start()

    barrier = pltpu.get_barrier_semaphore()

    for dev in (pa, pb, zp, zm, xp, xm, sib):
        pl.semaphore_signal(barrier, inc=1, device_id=dev, device_id_type=MESH)
    pl.semaphore_wait(barrier, 7)

    def send(src, dst, rsem, dev, ssend):
        pltpu.make_async_remote_copy(
            src_ref=src, dst_ref=dst, send_sem=ssend, recv_sem=rsem, device_id=dev, device_id_type=MESH
        ).start()

    def all_sent(ref, ssend):
        pltpu.make_async_remote_copy(
            src_ref=ref, dst_ref=ref, send_sem=ssend, recv_sem=lsem.at[0], device_id=sib, device_id_type=MESH
        ).wait_send()

    PA, PB, ZP, ZM, XP, XM, SIB = range(7)
    TO = [pa, pb, zp, zm, xp, xm, sib]

    def arrived(dst, rsem):
        pltpu.make_async_remote_copy(
            src_ref=dst, dst_ref=dst, send_sem=asem.at[0], recv_sem=rsem, device_id=sib, device_id_type=MESH
        ).wait_recv()

    def send_y(s, k, to):
        send(yb.at[s, core, k], yb.at[s, core, k], yr.at[s, k], TO[to], asem.at[to])

    def cross_y(s, k):
        send(yb.at[s, core, k], yb.at[s, core, k], yr2.at[s], sib, asem.at[SIB])

    def got_y(s, k):
        arrived(yb.at[s, core, k], yr.at[s, k])
        cross_y(s, k)

    def send_x(i, k, to):
        send(xb.at[i, k], xb.at[i, k], xr.at[i, k], TO[to], asem.at[to])

    def got_x(i, k):
        arrived(xb.at[i, k], xr.at[i, k])

    xa = (1 - ylo) * 4
    xo = ylo * 4

    def split_x(i):
        v = xb[i].reshape(OWN, HALF)
        hi, low = split(v)
        at = pl.ds(pl.multiple_of(i * OWN, OWN), OWN)
        xh[at, :] = hi
        xl[at, :] = low
        xs[at, :] = jnp.broadcast_to(jnp.sum(v * v, axis=1, keepdims=True), (OWN, 128))

    def fill_rsq(at):
        r = lax.broadcasted_iota(jnp.int32, (128, 128), 0)
        c = lax.broadcasted_iota(jnp.int32, (128, 128), 1)
        piece = jnp.sum(jnp.where(r == c, xs[at, :], 0.0), axis=0, keepdims=True)
        rsq[:, at] = jnp.broadcast_to(piece, (8, 128))

    def split_y(s):
        arrived(yb.at[s, 1 - core], yr2.at[s])
        v = yb[s].reshape(BLK, HALF)
        hi, low = split(v)
        at = pl.ds(pl.multiple_of(s * BLK, BLK), BLK)
        yh_[at, :] = hi
        yl_[at, :] = low
        return hi, low, jnp.sum(v * v, axis=1, keepdims=True)

    for k in range(2):
        send(x_hbm.at[pl.ds(k * PIECE, PIECE), kother], xb.at[d, k], xr.at[d, k], pa, asem.at[PA])
    for k in range(2):
        mine = slot(0, "o")
        send(y_hbm.at[pl.ds(k * PIECE, PIECE), kother], yb.at[mine, core, k], yr.at[mine, k], pa, asem.at[PA])
    for k in range(2):
        cx_own[k].wait()
        send_x(d, k, XP)
        send_x(d, k, XM)
        cy_own[k].wait()
        send_y(mine, k, ZP)
        send_y(mine, k, ZM)
        send_y(mine, k, PB)
        cross_y(mine, k)

    for k in range(2):
        got_x(xa + x, k)
        send_x(xa + x, k, XM)
        got_x(xo + at_x(3), k)
        send_x(xo + at_x(3), k, XP)
        got_y(slot(3, "o"), k)
        if k == 0:
            send_y(slot(3, "o"), 0, ZP)
        got_y(slot(0, "b"), k)
        if k == 0:
            send_y(slot(0, "b"), 0, ZM)
            send_y(slot(0, "b"), 0, ZP)
        got_y(slot(1, "o"), k)
        if k == 1:
            send_y(slot(1, "o"), 1, ZM)
        got_x(xo + at_x(1), k)
    for k in range(2):
        send_x(xa + x, k, XP)

    def split_first(i, c):
        split_x(lax.rem(i // 3 + ylo, 2) * 4 + at_x(lax.rem(i + i // 2, 4) * (1 - i // 3)))
        return c

    lax.fori_loop(0, 4, split_first, 0)

    for k in range(2):
        got_y(slot(0, "a"), k)
        send_y(slot(0, "a"), k, ZP)
        send_y(slot(0, "a"), k, ZM)
        send_y(slot(0, "a"), k, PB)
        got_x(xa + at_x(1), k)
        send_x(xa + at_x(1), k, XM)
        got_x(xo + at_x(2), k)
        got_y(slot(2, "o"), k)
    got_y(slot(1, "b"), 0)
    got_y(slot(3, "b"), 0)
    for k in range(2):
        send_y(slot(2, "o"), k, PB)

    def split_second(i, c):
        split_x(lax.rem(i + ylo, 2) * 4 + at_x(2 - i))
        return c

    lax.fori_loop(0, 2, split_second, 0)

    first = pl.ds(pl.multiple_of(256 * ylo, 128), 128)
    rest = pl.ds(pl.multiple_of(128 * (1 - ylo), 128), 256)
    fill_rsq(first)

    def pair_send(k, lanes):
        at = (k,) if lanes is None else (k, slice(None), lanes)
        pltpu.make_async_remote_copy(
            src_ref=ps.at[at], dst_ref=pr.at[at], send_sem=lsem.at[1], recv_sem=prs.at[k], device_id=pa, device_id_type=MESH
        ).start()

    def cross_part(hi, low, csq, lanes):
        both = dot_nt(jnp.concatenate([hi, low], axis=0), xh[lanes, :])
        cross = both[:BLK] + both[BLK:] + dot_nt(hi, xl[lanes, :])
        return (2.0 * cross - csq - rsq[0:1, lanes]) * SCALE

    def pair_first(e, k):
        hi, low, csq = split_y((1 - h) * 8 + k)
        cse[e] = jnp.broadcast_to(csq, (BLK, 128))
        ps[k, :, first] = cross_part(hi, low, csq, first)
        pair_send(k, first)

    def pair_rest(e, k):
        at = pl.ds(pl.multiple_of(((1 - h) * 8 + k) * BLK, BLK), BLK)
        ps[k, :, rest] = cross_part(yh_[at, :], yl_[at, :], cse[e, :, 0:1], rest)
        pair_send(k, rest)

    ka = yhi * 4 + z
    kc = (1 - yhi) * 4 + z
    pair_first(0, ka)

    for k in range(2):
        got_y(slot(0, "c"), k)
        if k == 0:
            send_y(slot(0, "c"), 0, ZM)
        else:
            pair_first(1, kc)
        got_y(slot(3, "a"), k)
        if k == 0:
            send_y(slot(3, "a"), 0, ZP)
            send_y(slot(0, "c"), 0, ZP)
        got_y(slot(1, "a"), k)
        if k == 1:
            send_y(slot(1, "a"), 1, ZM)
        got_x(xa + at_x(3), k)
        got_x(xa + at_x(2), k)
    for to in (ZP, ZM):
        send_y(slot(0, "c"), 1, to)
        send_y(slot(0, "b"), 1, to)

    def split_third(i, c):
        split_x(xa + at_x(2 + i))
        return c

    lax.fori_loop(0, 2, split_third, 0)
    for i in range(3):
        fill_rsq(pl.ds(128 * i, 128))

    def block(s):
        hi, low, csq = split_y(s)
        return cross_part(hi, low, csq, slice(None))

    def pair_block(dz, is_c):
        k = (is_c * (1 - yhi) + (1 - is_c) * yhi) * 4 + at_z(dz)
        ps[k] = block((1 - h) * 8 + k)
        pair_send(k, None)

    def own_block(dz, is_b):
        k = (is_b * (1 - yhi) + (1 - is_b) * yhi) * 4 + at_z(dz)
        lg[pl.ds(pl.multiple_of(k * BLK, BLK), BLK), :] = block(h * 8 + k)

    def group1(i, c):
        pair_block(1 + 2 * i, 0)
        return c

    def group3(i, c):
        own_block(i, 0)
        return c

    def group4(i, c):
        pair_block(1 + 2 * i, 1)
        return c

    def group5(i, c):
        own_block(i, 1)
        return c

    pair_rest(0, ka)
    pair_rest(1, kc)
    lax.fori_loop(0, 2, group1, 0)
    for k in range(2):
        got_y(slot(2, "a"), k)
        send_y(slot(2, "a"), k, PB)
    for k in range(2):
        got_y(slot(2, "b"), k)
    pair_block(2, 0)
    lax.fori_loop(0, 4, group3, 0)
    for k in range(2):
        got_y(slot(1, "c"), k)
        got_y(slot(3, "c"), k)
    lax.fori_loop(0, 2, group4, 0)
    for k in range(2):
        got_y(slot(2, "c"), k)
    pair_block(2, 1)
    got_y(slot(1, "b"), 1)
    got_y(slot(3, "b"), 1)
    lax.fori_loop(0, 4, group5, 0)

    def rows_from(k, count):
        half = k // 384
        return pl.ds(pl.multiple_of(((1 - half) * yhi + half * (1 - yhi)) * 384 + k - half * 384, 16), count)

    def send_logits(k):
        at = rows_from(LO_AT[k], LO_AT[k + 1] - LO_AT[k])
        send(lg.at[at], lo.at[at], los.at[k], pa, lsem.at[2])

    def got_logits(k):
        at = rows_from(LO_AT[k], LO_AT[k + 1] - LO_AT[k])
        arrived(lo.at[at], los.at[k])

    def pair_wait(i, c):
        m8, s8 = c
        hi = (1 - i // 4) * yhi + (i // 4) * (1 - yhi)
        k = hi * 4 + at_z(lax.rem(3 * i, 4))
        arrived(pr.at[k], prs.at[k])
        at = pl.ds(pl.multiple_of(k * BLK, BLK), BLK)
        v = lg[at, :] + pr[k]
        lg[at, :] = v
        v = v.reshape(12, 8, ROWS)
        top = jnp.maximum(m8, jnp.max(v, axis=0))
        return top, s8 * jnp.exp(m8 - top) + jnp.sum(jnp.exp(v - top[None]), axis=0)

    stats = lax.fori_loop(0, NB // 2, pair_wait, (jnp.full((8, ROWS), -1e30, F32), jnp.zeros((8, ROWS), F32)))
    send_logits(0)
    m8, s8 = lax.fori_loop(NB // 2, NB, pair_wait, stats)

    def exchange(buf, sems, rnd, mine, peers, msg):
        buf[rnd, mine] = msg
        for dev in peers:
            pltpu.make_async_remote_copy(
                src_ref=buf.at[rnd, mine], dst_ref=buf.at[rnd, mine], send_sem=sems.at[0, rnd], recv_sem=sems.at[1, rnd],
                device_id=dev, device_id_type=MESH,
            ).start()
        every = buf.at[rnd, pl.ds(0, len(peers))]
        all_of = pltpu.make_async_remote_copy(
            src_ref=every, dst_ref=every, send_sem=sems.at[0, rnd], recv_sem=sems.at[1, rnd],
            device_id=peers[0], device_id_type=MESH,
        )
        small.append(all_of)

        def done():
            all_of.wait_recv()
            return buf[rnd]

        return done

    small = []
    row_peers = [(n, lax.rem(d + k, 8)) for k in range(1, 8)]
    col_peers = [col_dev(lax.rem(n + k, 16)) for k in range(1, 16)]

    def ex_rows(rnd, msg):
        return exchange(rx, rxs, rnd, d, row_peers, msg)

    def ex_cols(buf, sems, msg, rnd):
        return exchange(buf, sems, rnd, n, col_peers, msg)

    def row_msg(parts):
        parts = parts + [jnp.zeros((1, 128), F32)] * (8 - len(parts))
        return jnp.concatenate(parts, axis=0)

    def blk(k):
        return slice(BLK * k, BLK * k + BLK)

    m = jnp.max(m8, axis=0, keepdims=True)
    tot = jnp.sum(s8 * jnp.exp(m8 - m), axis=0, keepdims=True)
    done = ex_rows(0, row_msg(rows3(m) + rows3(tot)))
    send_logits(1)
    everyone = done()
    mm = everyone[:, 0:3, :]
    top = jnp.max(mm, axis=0)
    tt = jnp.sum(everyone[:, 3:6, :] * jnp.exp(mm - top[None]), axis=0)
    f1 = flat3(LOGN - top - jnp.log(tt))

    pm = jnp.zeros((8, 128), F32)
    pt = jnp.zeros((8, 128), F32)
    for k in range(NB):
        a = lg[blk(k), :] + f1
        cm = jnp.max(a, axis=1, keepdims=True)
        e = jnp.exp(a - cm)
        q_[blk(k), :] = e
        pm = pm + pack_block(k, cm)
        pt = pt + pack_block(k, jnp.sum(e, axis=1, keepdims=True))
    done = ex_cols(cx1, cx1s, jnp.concatenate([pm, pt], axis=0), 0)
    for ref, to in (
        (xb.at[pl.ds(0, 2)], PA),
        (yb.at[pl.ds(0, 4), core], PB),
        (yb.at[pl.ds(0, 5), core], ZP),
        (yb.at[pl.ds(0, 5), core], ZM),
        (xb.at[pl.ds(0, 3)], XP),
        (xb.at[pl.ds(0, 3)], XM),
        (yb.at[:, core], SIB),
    ):
        all_sent(ref, asem.at[to])
    all_sent(ps, lsem.at[1])
    everyone = done()
    mm = everyone[:, 0:8, :]
    top = jnp.max(mm, axis=0)
    tt = jnp.sum(everyone[:, 8:16, :] * jnp.exp(mm - top[None]), axis=0)
    used = lax.broadcasted_iota(jnp.int32, (8, 128), 1) < 96
    g1 = jnp.where(used, LOGN - top - jnp.log(jnp.where(used, tt, 1.0)), 0.0)
    go[0] = g1
    send(go.at[0], go.at[1], gs.at[0], pa, lsem.at[3])

    fac = jnp.exp(pm + g1)
    s8 = jnp.zeros((8, ROWS), F32)
    for k in range(NB):
        p = q_[blk(k), :] * unpack(fac, 12 * k, 12)
        q_[blk(k), :] = p
        s8 = s8 + jnp.sum(p.reshape(12, 8, ROWS), axis=0)

    def row_step(rnd, s8, between):
        done = ex_rows(rnd, row_msg(rows3(jnp.sum(s8, axis=0, keepdims=True))))
        between()
        return flat3(NSAMP / jnp.sum(done()[:, 0:3, :], axis=0))

    def col_step(rnd, u, between):
        pk = jnp.zeros((8, 128), F32)
        for k in range(NB):
            pk = pk + pack_block(k, jnp.sum(q_[blk(k), :] * u, axis=1, keepdims=True))
        done = ex_cols(cx, cxs, pk, rnd)
        between()
        tt = jnp.sum(done(), axis=0)
        return NSAMP / jnp.where(used, tt, 1.0)

    def row_sums(v):
        s8 = jnp.zeros((8, ROWS), F32)
        for k in range(NB):
            s8 = s8 + jnp.sum((q_[blk(k), :] * unpack(v, 12 * k, 12)).reshape(12, 8, ROWS), axis=0)
        return s8

    def turn(src, dst, some):
        for q in some:
            dst[:, 128 * q : 128 * q + 128] = src[128 * q : 128 * q + 128, :].T

    def far(some):
        for q in some:
            at = rows_from(128 * q, 128)
            lane = lax.broadcasted_iota(jnp.int32, (16, 8, 128), 2)
            lead = lax.broadcasted_iota(jnp.int32, (16, 8, 128), 0) + at.start // 8
            g = jnp.sum(jnp.where(lane == lead, go[1][None], 0.0), axis=2, keepdims=True).reshape(128, 1)
            po[:, pl.ds(pl.multiple_of(at.start, 128), 128)] = jnp.exp(lo[at, :] + f1 + g).T

    def in_row1():
        send_logits(2)
        send_logits(3)
        turn(q_, pn, range(0, 3))

    def in_row2():
        send_logits(4)
        arrived(go.at[1], gs.at[0])
        got_logits(0)
        got_logits(1)
        far(range(0, 2))

    def in_col2():
        got_logits(2)
        got_logits(3)
        far(range(2, 4))
        got_logits(4)
        far(range(4, 6))

    u = row_step(1, s8, in_row1)
    v = col_step(0, u, lambda: turn(q_, pn, range(3, 6)))
    u = row_step(2, row_sums(v), in_row2)
    v = col_step(1, u, in_col2)
    vo[0] = v
    send(vo.at[0], vo.at[1], gs.at[1], pa, lsem.at[4])
    total = ex_rows(3, row_msg(rows3(jnp.sum(row_sums(v), axis=0, keepdims=True))))

    hi, low = split(pn[...] * packed_row(v))
    wh[0] = hi
    wl[0] = low

    own_rows = pl.ds(pl.multiple_of(h * COLS, COLS), COLS)
    far_rows = pl.ds(pl.multiple_of((1 - h) * COLS, COLS), COLS)

    def part(i, rows, cols):
        return (
            dot_nn(wh[i], yh_[rows, cols]) + dot_nn(wh[i], yl_[rows, cols]) + dot_nn(wl[i], yh_[rows, cols])
        )

    def cols_of(c):
        return pl.ds(CUTS[c], CUTS[c + 1] - CUTS[c])

    def cut(ref, i, c):
        return ref.at[i, :, cols_of(c)]

    def compute(c):
        t = part(0, own_rows, cols_of(c))
        if c == 0:
            arrived(vo.at[1], gs.at[1])
            hi, low = split(po[...] * packed_row(vo[1]))
            wh[1] = hi
            wl[1] = low
        t = t + part(1, far_rows, cols_of(c))
        tp[:, :, cols_of(c)] = t.reshape(8, OWN, CUTS[c + 1] - CUTS[c])

    def pass_on(i, buf, k, c, to):
        sem = r1s.at[c, k] if buf is r1 else r2s.at[c, k // 2]
        send(cut(tp, i, c), cut(buf, k, c), sem, TO[to], tsem.at[to])

    def add(i, k, c):
        tp[i, :, cols_of(c)] = tp[i, :, cols_of(c)] + r1[k, :, cols_of(c)]

    def start_pair(c):
        pass_on(xa + at_x(2), r1, 0, c, XP)
        pass_on(xa + at_x(3), r2, 0, c, XM)

    def pass_pair(c):
        arrived(cut(r1, 0, c), r1s.at[c, 0])
        add(xa + at_x(1), 0, c)
        pass_on(xa + at_x(1), r2, 1, c, XP)

    def start_own(c):
        pass_on(xo + at_x(2), r1, 1, c, XM)

    def last_own(c):
        pass_on(xo + at_x(1), r2, 3, c, XP)

    def pass_own(c):
        arrived(cut(r1, 1, c), r1s.at[c, 1])
        add(xo + at_x(3), 1, c)
        pass_on(xo + at_x(3), r2, 2, c, XM)

    def both(i, c, k):
        arrived(r2.at[pl.ds(k, 2), :, cols_of(c)], r2s.at[c, k // 2])
        return tp[i, :, cols_of(c)] + r2[k, :, cols_of(c)] + r2[k + 1, :, cols_of(c)]

    def final_pair(c):
        tp[xa + x, :, cols_of(c)] = both(xa + x, c, 0)
        send(cut(tp, xa + x, c), pf.at[:, cols_of(c)], pfs, pa, tsem.at[PA])

    for c in range(CH):
        compute(c)
        start_pair(c)
        start_own(c)
        if c:
            pass_pair(c - 1)
        else:
            last_own(c)
    pass_pair(CH - 1)
    for c in range(1, CH):
        last_own(c)

    fin = flat3(jnp.sum(total()[:, 0:3, :], axis=0))
    lane = lax.broadcasted_iota(jnp.int32, (OWN, ROWS), 1)
    row = lax.broadcasted_iota(jnp.int32, (OWN, ROWS), 0) + d * OWN
    norm = 1.0 / jnp.sum(jnp.where(lane == row, fin, 0.0), axis=1, keepdims=True)
    f_out[...] = EPS * (f1 + jnp.log(u))
    near = lax.broadcasted_iota(jnp.int32, (8, 128), 1) // 48 == yhi
    g_out[...] = EPS * packed_row(jnp.where(near, g1 + jnp.log(v), go[1] + jnp.log(vo[1])))

    for c in range(CH):
        final_pair(c)
        if c:
            pass_own(c - 1)
    pass_own(CH - 1)
    for c in range(CH):
        width = CUTS[c + 1] - CUTS[c]
        t_out[:, pl.ds(pl.multiple_of(h * HALF + CUTS[c], 256), width)] = both(xo + x, c, 2) * norm
    arrived(pf, pfs)
    t_out[:, kother] = pf[...] * norm

    all_sent(lg, lsem.at[2])
    all_sent(go.at[0], lsem.at[3])
    all_sent(vo.at[0], lsem.at[4])
    all_sent(pf, tsem.at[PA])
    for to in (XP, XM):
        all_sent(tp.at[pl.ds(0, 3)], tsem.at[to])
    for cp in small:
        cp.wait_send()


def hand_out(t_in, f_in, g_in, t_out, f_out, g_out, sem):
    parts = [
        pltpu.make_async_copy(t_in.at[pl.ds(8 * k, 8)], t_out.at[pl.ds(8 * k, 8)], sem.at[k]) for k in range(OWN // 8)
    ]
    for cp in parts:
        cp.start()
    f_out[...] = f_in[...].reshape(ROWS)
    g_out[...] = g_in[...].reshape(COLS)
    for cp in parts:
        cp.wait()


def body(noise_latents, data_latents):
    dma = pltpu.SemaphoreType.DMA
    vm = pltpu.VMEM
    scratch = [
        vm((8, 2, PIECE, HALF), F32),
        vm((16, 2, 2, PIECE, HALF), F32),
        vm((ROWS, HALF), BF16),
        vm((ROWS, HALF), BF16),
        vm((2 * COLS, HALF), BF16),
        vm((2 * COLS, HALF), BF16),
        vm((ROWS, 128), F32),
        vm((2, BLK, 128), F32),
        vm((8, ROWS), F32),
        vm((NB, BLK, ROWS), F32),
        vm((NB, BLK, ROWS), F32),
        vm((COLS, ROWS), F32),
        vm((COLS, ROWS), F32),
        vm((COLS, ROWS), F32),
        vm((ROWS, COLS), F32),
        vm((ROWS, COLS), F32),
        vm((2, ROWS, COLS), BF16),
        vm((2, ROWS, COLS), BF16),
        vm((8, OWN, HALF), F32),
        vm((2, OWN, HALF), F32),
        vm((4, OWN, HALF), F32),
        vm((OWN, HALF), F32),
        vm((4, 8, 8, 128), F32),
        vm((1, 16, 16, 128), F32),
        vm((2, 16, 8, 128), F32),
        vm((2, 8, 128), F32),
        vm((2, 8, 128), F32),
        dma((2, 2)),
        dma((8, 2)),
        dma((16, 2)),
        dma((16,)),
        dma((NB,)),
        dma((5,)),
        dma((5,)),
        dma((2, 4)),
        dma((2, 1)),
        dma((2, 2)),
        dma((2,)),
        dma((CH, 2)),
        dma((CH, 2)),
        dma,
        dma((7,)),
        dma((7,)),
    ]
    t, f, g = pl.pallas_call(
        kernel,
        out_shape=(
            vm((OWN, WIDTH), F32),
            vm((1, ROWS), F32),
            vm((1, COLS), F32),
        ),
        in_specs=[pl.BlockSpec(memory_space=pl.ANY)] * 2,
        out_specs=(pl.BlockSpec(memory_space=pltpu.VMEM),) * 3,
        scratch_shapes=scratch,
        compiler_params=pltpu.CompilerParams(
            collective_id=0, has_side_effects=True, vmem_limit_bytes=60 * 2**20
        ),
        name="coupling",
    )(noise_latents, data_latents)
    return pl.pallas_call(
        hand_out,
        out_shape=(
            jax.ShapeDtypeStruct((OWN, WIDTH), F32),
            jax.ShapeDtypeStruct((ROWS,), F32),
            jax.ShapeDtypeStruct((COLS,), F32),
        ),
        in_specs=[pl.BlockSpec(memory_space=pltpu.VMEM)] * 3,
        out_specs=(pl.BlockSpec(memory_space=pl.ANY),) + (pl.BlockSpec(memory_space=pltpu.VMEM),) * 2,
        scratch_shapes=[pltpu.SemaphoreType.DMA((OWN // 8,))],
        compiler_params=pltpu.CompilerParams(vmem_limit_bytes=2 * 2**20),
        name="hand_out",
    )(t, f, g)


def solution(mesh):
    placed = (P(("noise", "dp"), None), P(("dp", "noise"), None))
    return jax.shard_map(
        body,
        mesh=mesh,
        in_specs=placed,
        out_specs=(P(("noise", "dp"), None), P("noise"), P("dp")),
        check_vma=False,
    )
```

```python
import functools
import math

import jax
import jax.numpy as jnp
from jax import lax
from jax.experimental import pallas as pl
from jax.experimental.pallas import tpu as pltpu
from jax.sharding import PartitionSpec as P

MESH = pl.DeviceIdType.MESH
F32 = jnp.float32
BF16 = jnp.bfloat16
EPS = 0.01

OWN = 48
WIDTH = 4096
HALF = WIDTH // 2
ROWS = 384
COLS = 768
BLK = 96
NB = COLS // BLK
PIECE = OWN // 2
LO_AT = (0, 64, 320, 384, 560, 768)
NSAMP = 6144
LOGN = math.log(NSAMP)
SCALE = 1.0 / (WIDTH * EPS)
CUTS = (0, 256, 512, 1024, 1536, 2048)
CH = len(CUTS) - 1


def split(v):
    hi = v.astype(BF16)
    return hi, (v - hi.astype(F32)).astype(BF16)


def dot_nt(a, b):
    return lax.dot_general(a, b, (((1,), (1,)), ((), ())), preferred_element_type=F32)


def dot_nn(a, b):
    return lax.dot_general(a, b, (((1,), (0,)), ((), ())), preferred_element_type=F32)


def pack_block(k, val):
    v3 = val.reshape(12, 8, 1)
    lane = lax.broadcasted_iota(jnp.int32, (12, 8, 128), 2)
    lead = lax.broadcasted_iota(jnp.int32, (12, 8, 128), 0) + 12 * k
    return jnp.sum(jnp.where(lane == lead, v3, 0.0), axis=0)


def unpack(packed, first, count):
    lane = lax.broadcasted_iota(jnp.int32, (count, 8, 128), 2)
    lead = lax.broadcasted_iota(jnp.int32, (count, 8, 128), 0) + first
    v3 = jnp.sum(jnp.where(lane == lead, packed[None], 0.0), axis=2, keepdims=True)
    return v3.reshape(8 * count, 1)


def to_row(col):
    r = lax.broadcasted_iota(jnp.int32, (128, 128), 0)
    c = lax.broadcasted_iota(jnp.int32, (128, 128), 1)
    return jnp.sum(jnp.where(r == c, col, 0.0), axis=0, keepdims=True)


def packed_row(packed):
    return jnp.concatenate([to_row(unpack(packed, 16 * q, 16)) for q in range(6)], axis=1)


def rows3(v):
    return [v[:, 128 * q : 128 * q + 128] for q in range(3)]


def flat3(v):
    return jnp.concatenate([v[q : q + 1] for q in range(3)], axis=1)


def kernel(
    x_hbm, y_hbm, t_out, f_out, g_out,
    xb, yb, xh, xl, yh_, yl_, xs, cse, rsq, ps, pr, lg, lo, q_, pn, po, wh, wl, tp, r1, r2, pf,
    rx, cx1, cx, go, vo,
    loc, xr, yr, yr2, prs, los, lsem, rxs, cx1s, cxs, gs, r1s, r2s, pfs, asem, tsem,
):
    n = lax.axis_index("noise")
    d = lax.axis_index("dp")
    core = lax.rem(n, 2)
    z = lax.rem(n // 2, 4)
    yhi = n // 8
    x = lax.rem(d, 4)
    ylo = d // 4
    h = lax.rem(yhi + ylo, 2)

    def at_z(k):
        return lax.rem(z + k, 4)

    def at_x(k):
        return lax.rem(x + k, 4)

    sib = (n + 1 - 2 * core, d)
    pa = (n, (1 - ylo) * 4 + x)
    pb = (((1 - yhi) * 4 + z) * 2 + core, (1 - ylo) * 4 + x)
    zp = ((yhi * 4 + at_z(1)) * 2 + core, d)
    zm = ((yhi * 4 + at_z(3)) * 2 + core, d)
    xp = (n, ylo * 4 + at_x(1))
    xm = (n, ylo * 4 + at_x(3))

    SRC = {"o": (yhi, h), "a": (yhi, 1 - h), "b": (1 - yhi, h), "c": (1 - yhi, 1 - h)}

    def slot(dz, who):
        hi, tile = SRC[who]
        return tile * 8 + hi * 4 + at_z(dz)

    def col_dev(p):
        return (p, lax.rem(p // 8 + h, 2) * 4 + x)

    kmine = pl.ds(pl.multiple_of(h * HALF, HALF), HALF)
    kother = pl.ds(pl.multiple_of((1 - h) * HALF, HALF), HALF)

    cx_own = [
        pltpu.make_async_copy(x_hbm.at[pl.ds(k * PIECE, PIECE), kmine], xb.at[d, k], loc.at[0, k]) for k in range(2)
    ]
    cy_own = [
        pltpu.make_async_copy(y_hbm.at[pl.ds(k * PIECE, PIECE), kmine], yb.at[slot(0, "o"), core, k], loc.at[1, k])
        for k in range(2)
    ]
    for cp in cx_own + cy_own:
        cp.start()

    barrier = pltpu.get_barrier_semaphore()

    for dev in (pa, pb, zp, zm, xp, xm, sib):
        pl.semaphore_signal(barrier, inc=1, device_id=dev, device_id_type=MESH)
    pl.semaphore_wait(barrier, 7)

    def send(src, dst, rsem, dev, ssend):
        pltpu.make_async_remote_copy(
            src_ref=src, dst_ref=dst, send_sem=ssend, recv_sem=rsem, device_id=dev, device_id_type=MESH
        ).start()

    def all_sent(ref, ssend):
        pltpu.make_async_remote_copy(
            src_ref=ref, dst_ref=ref, send_sem=ssend, recv_sem=lsem.at[0], device_id=sib, device_id_type=MESH
        ).wait_send()

    PA, PB, ZP, ZM, XP, XM, SIB = range(7)
    TO = [pa, pb, zp, zm, xp, xm, sib]

    def arrived(dst, rsem):
        pltpu.make_async_remote_copy(
            src_ref=dst, dst_ref=dst, send_sem=asem.at[0], recv_sem=rsem, device_id=sib, device_id_type=MESH
        ).wait_recv()

    def send_y(s, k, to):
        send(yb.at[s, core, k], yb.at[s, core, k], yr.at[s, k], TO[to], asem.at[to])

    def cross_y(s, k):
        send(yb.at[s, core, k], yb.at[s, core, k], yr2.at[s], sib, asem.at[SIB])

    def got_y(s, k):
        arrived(yb.at[s, core, k], yr.at[s, k])
        cross_y(s, k)

    def send_x(i, k, to):
        send(xb.at[i, k], xb.at[i, k], xr.at[i, k], TO[to], asem.at[to])

    def got_x(i, k):
        arrived(xb.at[i, k], xr.at[i, k])

    xa = (1 - ylo) * 4
    xo = ylo * 4

    def split_x(i):
        v = xb[i].reshape(OWN, HALF)
        hi, low = split(v)
        at = pl.ds(pl.multiple_of(i * OWN, OWN), OWN)
        xh[at, :] = hi
        xl[at, :] = low
        xs[at, :] = jnp.broadcast_to(jnp.sum(v * v, axis=1, keepdims=True), (OWN, 128))

    def fill_rsq(at):
        r = lax.broadcasted_iota(jnp.int32, (128, 128), 0)
        c = lax.broadcasted_iota(jnp.int32, (128, 128), 1)
        piece = jnp.sum(jnp.where(r == c, xs[at, :], 0.0), axis=0, keepdims=True)
        rsq[:, at] = jnp.broadcast_to(piece, (8, 128))

    def split_y(s):
        arrived(yb.at[s, 1 - core], yr2.at[s])
        v = yb[s].reshape(BLK, HALF)
        hi, low = split(v)
        at = pl.ds(pl.multiple_of(s * BLK, BLK), BLK)
        yh_[at, :] = hi
        yl_[at, :] = low
        return hi, low, jnp.sum(v * v, axis=1, keepdims=True)

    for k in range(2):
        send(x_hbm.at[pl.ds(k * PIECE, PIECE), kother], xb.at[d, k], xr.at[d, k], pa, asem.at[PA])
    for k in range(2):
        mine = slot(0, "o")
        send(y_hbm.at[pl.ds(k * PIECE, PIECE), kother], yb.at[mine, core, k], yr.at[mine, k], pa, asem.at[PA])
    for k in range(2):
        cx_own[k].wait()
        send_x(d, k, XP)
        send_x(d, k, XM)
        cy_own[k].wait()
        send_y(mine, k, ZP)
        send_y(mine, k, ZM)
        send_y(mine, k, PB)
        cross_y(mine, k)

    for k in range(2):
        got_x(xa + x, k)
        send_x(xa + x, k, XM)
        got_x(xo + at_x(3), k)
        send_x(xo + at_x(3), k, XP)
        got_y(slot(3, "o"), k)
        if k == 0:
            send_y(slot(3, "o"), 0, ZP)
        got_y(slot(0, "b"), k)
        if k == 0:
            send_y(slot(0, "b"), 0, ZM)
            send_y(slot(0, "b"), 0, ZP)
        got_y(slot(1, "o"), k)
        if k == 1:
            send_y(slot(1, "o"), 1, ZM)
        got_x(xo + at_x(1), k)
    for k in range(2):
        send_x(xa + x, k, XP)

    def split_first(i, c):
        split_x(lax.rem(i // 3 + ylo, 2) * 4 + at_x(lax.rem(i + i // 2, 4) * (1 - i // 3)))
        return c

    lax.fori_loop(0, 4, split_first, 0)

    for k in range(2):
        got_y(slot(0, "a"), k)
        send_y(slot(0, "a"), k, ZP)
        send_y(slot(0, "a"), k, ZM)
        send_y(slot(0, "a"), k, PB)
        got_x(xa + at_x(1), k)
        send_x(xa + at_x(1), k, XM)
        got_x(xo + at_x(2), k)
        got_y(slot(2, "o"), k)
    got_y(slot(1, "b"), 0)
    got_y(slot(3, "b"), 0)
    for k in range(2):
        send_y(slot(2, "o"), k, PB)

    def split_second(i, c):
        split_x(lax.rem(i + ylo, 2) * 4 + at_x(2 - i))
        return c

    lax.fori_loop(0, 2, split_second, 0)

    first = pl.ds(pl.multiple_of(256 * ylo, 128), 128)
    rest = pl.ds(pl.multiple_of(128 * (1 - ylo), 128), 256)
    fill_rsq(first)

    def pair_send(k, lanes):
        at = (k,) if lanes is None else (k, slice(None), lanes)
        pltpu.make_async_remote_copy(
            src_ref=ps.at[at], dst_ref=pr.at[at], send_sem=lsem.at[1], recv_sem=prs.at[k], device_id=pa, device_id_type=MESH
        ).start()

    def cross_part(hi, low, csq, lanes):
        both = dot_nt(jnp.concatenate([hi, low], axis=0), xh[lanes, :])
        cross = both[:BLK] + both[BLK:] + dot_nt(hi, xl[lanes, :])
        return (2.0 * cross - csq - rsq[0:1, lanes]) * SCALE

    def pair_first(e, k):
        hi, low, csq = split_y((1 - h) * 8 + k)
        cse[e] = jnp.broadcast_to(csq, (BLK, 128))
        ps[k, :, first] = cross_part(hi, low, csq, first)
        pair_send(k, first)

    def pair_rest(e, k):
        at = pl.ds(pl.multiple_of(((1 - h) * 8 + k) * BLK, BLK), BLK)
        ps[k, :, rest] = cross_part(yh_[at, :], yl_[at, :], cse[e, :, 0:1], rest)
        pair_send(k, rest)

    ka = yhi * 4 + z
    kc = (1 - yhi) * 4 + z
    pair_first(0, ka)

    for k in range(2):
        got_y(slot(0, "c"), k)
        if k == 0:
            send_y(slot(0, "c"), 0, ZM)
        else:
            pair_first(1, kc)
        got_y(slot(3, "a"), k)
        if k == 0:
            send_y(slot(3, "a"), 0, ZP)
            send_y(slot(0, "c"), 0, ZP)
        got_y(slot(1, "a"), k)
        if k == 1:
            send_y(slot(1, "a"), 1, ZM)
        got_x(xa + at_x(3), k)
        got_x(xa + at_x(2), k)
    for to in (ZP, ZM):
        send_y(slot(0, "c"), 1, to)
        send_y(slot(0, "b"), 1, to)

    def split_third(i, c):
        split_x(xa + at_x(2 + i))
        return c

    lax.fori_loop(0, 2, split_third, 0)
    for i in range(3):
        fill_rsq(pl.ds(128 * i, 128))

    def block(s):
        hi, low, csq = split_y(s)
        return cross_part(hi, low, csq, slice(None))

    def pair_block(dz, is_c):
        k = (is_c * (1 - yhi) + (1 - is_c) * yhi) * 4 + at_z(dz)
        ps[k] = block((1 - h) * 8 + k)
        pair_send(k, None)

    def own_block(dz, is_b):
        k = (is_b * (1 - yhi) + (1 - is_b) * yhi) * 4 + at_z(dz)
        lg[pl.ds(pl.multiple_of(k * BLK, BLK), BLK), :] = block(h * 8 + k)

    def group1(i, c):
        pair_block(1 + 2 * i, 0)
        return c

    def group3(i, c):
        own_block(i, 0)
        return c

    def group4(i, c):
        pair_block(1 + 2 * i, 1)
        return c

    def group5(i, c):
        own_block(lax.rem(i + 2, 4), (i + 2) // 4)
        return c

    pair_rest(0, ka)
    pair_rest(1, kc)
    lax.fori_loop(0, 2, group1, 0)
    for k in range(2):
        got_y(slot(2, "a"), k)
        send_y(slot(2, "a"), k, PB)
    for k in range(2):
        got_y(slot(2, "b"), k)
    pair_block(2, 0)
    lax.fori_loop(0, 2, group3, 0)
    for k in range(2):
        got_y(slot(1, "c"), k)
        got_y(slot(3, "c"), k)
    lax.fori_loop(0, 2, group4, 0)
    for k in range(2):
        got_y(slot(2, "c"), k)
    pair_block(2, 1)
    got_y(slot(1, "b"), 1)
    got_y(slot(3, "b"), 1)
    lax.fori_loop(0, 6, group5, 0)

    def rows_from(k, count):
        half = k // 384
        return pl.ds(pl.multiple_of(((1 - half) * yhi + half * (1 - yhi)) * 384 + k - half * 384, 16), count)

    def send_logits(k):
        at = rows_from(LO_AT[k], LO_AT[k + 1] - LO_AT[k])
        send(lg.at[at], lo.at[at], los.at[k], pa, lsem.at[2])

    def got_logits(k):
        at = rows_from(LO_AT[k], LO_AT[k + 1] - LO_AT[k])
        arrived(lo.at[at], los.at[k])

    def pair_wait(i, c):
        m8, s8 = c
        hi = (1 - i // 4) * yhi + (i // 4) * (1 - yhi)
        k = hi * 4 + at_z(lax.rem(3 * i, 4))
        arrived(pr.at[k], prs.at[k])
        at = pl.ds(pl.multiple_of(k * BLK, BLK), BLK)
        v = lg[at, :] + pr[k]
        lg[at, :] = v
        v = v.reshape(12, 8, ROWS)
        top = jnp.maximum(m8, jnp.max(v, axis=0))
        return top, s8 * jnp.exp(m8 - top) + jnp.sum(jnp.exp(v - top[None]), axis=0)

    stats = lax.fori_loop(0, NB // 2, pair_wait, (jnp.full((8, ROWS), -1e30, F32), jnp.zeros((8, ROWS), F32)))
    send_logits(0)
    m8, s8 = lax.fori_loop(NB // 2, NB, pair_wait, stats)

    def exchange(buf, sems, rnd, mine, peers, msg):
        buf[rnd, mine] = msg
        for dev in peers:
            pltpu.make_async_remote_copy(
                src_ref=buf.at[rnd, mine], dst_ref=buf.at[rnd, mine], send_sem=sems.at[0, rnd], recv_sem=sems.at[1, rnd],
                device_id=dev, device_id_type=MESH,
            ).start()
        every = buf.at[rnd, pl.ds(0, len(peers))]
        all_of = pltpu.make_async_remote_copy(
            src_ref=every, dst_ref=every, send_sem=sems.at[0, rnd], recv_sem=sems.at[1, rnd],
            device_id=peers[0], device_id_type=MESH,
        )
        small.append(all_of)

        def done():
            all_of.wait_recv()
            return buf[rnd]

        return done

    small = []
    row_peers = [(n, lax.rem(d + k, 8)) for k in range(1, 8)]
    col_peers = [col_dev(lax.rem(n + k, 16)) for k in range(1, 16)]

    def ex_rows(rnd, msg):
        return exchange(rx, rxs, rnd, d, row_peers, msg)

    def ex_cols(buf, sems, msg, rnd):
        return exchange(buf, sems, rnd, n, col_peers, msg)

    def row_msg(parts):
        parts = parts + [jnp.zeros((1, 128), F32)] * (8 - len(parts))
        return jnp.concatenate(parts, axis=0)

    def blk(k):
        return slice(BLK * k, BLK * k + BLK)

    m = jnp.max(m8, axis=0, keepdims=True)
    tot = jnp.sum(s8 * jnp.exp(m8 - m), axis=0, keepdims=True)
    done = ex_rows(0, row_msg(rows3(m) + rows3(tot)))
    send_logits(1)
    everyone = done()
    mm = everyone[:, 0:3, :]
    top = jnp.max(mm, axis=0)
    tt = jnp.sum(everyone[:, 3:6, :] * jnp.exp(mm - top[None]), axis=0)
    f1 = flat3(LOGN - top - jnp.log(tt))

    pm = jnp.zeros((8, 128), F32)
    pt = jnp.zeros((8, 128), F32)
    for k in range(NB):
        a = lg[blk(k), :] + f1
        cm = jnp.max(a, axis=1, keepdims=True)
        e = jnp.exp(a - cm)
        q_[blk(k), :] = e
        pm = pm + pack_block(k, cm)
        pt = pt + pack_block(k, jnp.sum(e, axis=1, keepdims=True))
    done = ex_cols(cx1, cx1s, jnp.concatenate([pm, pt], axis=0), 0)
    for ref, to in (
        (xb.at[pl.ds(0, 2)], PA),
        (yb.at[pl.ds(0, 4), core], PB),
        (yb.at[pl.ds(0, 5), core], ZP),
        (yb.at[pl.ds(0, 5), core], ZM),
        (xb.at[pl.ds(0, 3)], XP),
        (xb.at[pl.ds(0, 3)], XM),
        (yb.at[:, core], SIB),
    ):
        all_sent(ref, asem.at[to])
    all_sent(ps, lsem.at[1])
    everyone = done()
    mm = everyone[:, 0:8, :]
    top = jnp.max(mm, axis=0)
    tt = jnp.sum(everyone[:, 8:16, :] * jnp.exp(mm - top[None]), axis=0)
    used = lax.broadcasted_iota(jnp.int32, (8, 128), 1) < 96
    g1 = jnp.where(used, LOGN - top - jnp.log(jnp.where(used, tt, 1.0)), 0.0)
    go[0] = g1
    send(go.at[0], go.at[1], gs.at[0], pa, lsem.at[3])

    fac = jnp.exp(pm + g1)
    s8 = jnp.zeros((8, ROWS), F32)
    for k in range(NB):
        p = q_[blk(k), :] * unpack(fac, 12 * k, 12)
        q_[blk(k), :] = p
        s8 = s8 + jnp.sum(p.reshape(12, 8, ROWS), axis=0)

    def row_step(rnd, s8, between):
        done = ex_rows(rnd, row_msg(rows3(jnp.sum(s8, axis=0, keepdims=True))))
        between()
        return flat3(NSAMP / jnp.sum(done()[:, 0:3, :], axis=0))

    def col_step(rnd, u, between):
        pk = jnp.zeros((8, 128), F32)
        for k in range(NB):
            pk = pk + pack_block(k, jnp.sum(q_[blk(k), :] * u, axis=1, keepdims=True))
        done = ex_cols(cx, cxs, pk, rnd)
        between()
        tt = jnp.sum(done(), axis=0)
        return NSAMP / jnp.where(used, tt, 1.0)

    def row_sums(v):
        s8 = jnp.zeros((8, ROWS), F32)
        for k in range(NB):
            s8 = s8 + jnp.sum((q_[blk(k), :] * unpack(v, 12 * k, 12)).reshape(12, 8, ROWS), axis=0)
        return s8

    def turn(src, dst, some):
        for q in some:
            dst[:, 128 * q : 128 * q + 128] = src[128 * q : 128 * q + 128, :].T

    def far(some):
        for q in some:
            at = rows_from(128 * q, 128)
            lane = lax.broadcasted_iota(jnp.int32, (16, 8, 128), 2)
            lead = lax.broadcasted_iota(jnp.int32, (16, 8, 128), 0) + at.start // 8
            g = jnp.sum(jnp.where(lane == lead, go[1][None], 0.0), axis=2, keepdims=True).reshape(128, 1)
            po[:, pl.ds(pl.multiple_of(at.start, 128), 128)] = jnp.exp(lo[at, :] + f1 + g).T

    def in_row1():
        send_logits(2)
        send_logits(3)
        turn(q_, pn, range(0, 3))

    def in_row2():
        send_logits(4)
        arrived(go.at[1], gs.at[0])
        got_logits(0)
        got_logits(1)
        far(range(0, 2))

    def in_col2():
        got_logits(2)
        got_logits(3)
        far(range(2, 4))
        got_logits(4)
        far(range(4, 6))

    u = row_step(1, s8, in_row1)
    v = col_step(0, u, lambda: turn(q_, pn, range(3, 6)))
    u = row_step(2, row_sums(v), in_row2)
    v = col_step(1, u, in_col2)
    vo[0] = v
    send(vo.at[0], vo.at[1], gs.at[1], pa, lsem.at[4])
    total = ex_rows(3, row_msg(rows3(jnp.sum(row_sums(v), axis=0, keepdims=True))))

    hi, low = split(pn[...] * packed_row(v))
    wh[0] = hi
    wl[0] = low

    own_rows = pl.ds(pl.multiple_of(h * COLS, COLS), COLS)
    far_rows = pl.ds(pl.multiple_of((1 - h) * COLS, COLS), COLS)

    def part(i, rows, cols):
        return (
            dot_nn(wh[i], yh_[rows, cols]) + dot_nn(wh[i], yl_[rows, cols]) + dot_nn(wl[i], yh_[rows, cols])
        )

    def cols_of(c):
        return pl.ds(CUTS[c], CUTS[c + 1] - CUTS[c])

    def cut(ref, i, c):
        return ref.at[i, :, cols_of(c)]

    def compute(c):
        t = part(0, own_rows, cols_of(c))
        if c == 0:
            arrived(vo.at[1], gs.at[1])
            hi, low = split(po[...] * packed_row(vo[1]))
            wh[1] = hi
            wl[1] = low
        t = t + part(1, far_rows, cols_of(c))
        tp[:, :, cols_of(c)] = t.reshape(8, OWN, CUTS[c + 1] - CUTS[c])

    def pass_on(i, buf, k, c, to):
        sem = r1s.at[c, k] if buf is r1 else r2s.at[c, k // 2]
        send(cut(tp, i, c), cut(buf, k, c), sem, TO[to], tsem.at[to])

    def add(i, k, c):
        tp[i, :, cols_of(c)] = tp[i, :, cols_of(c)] + r1[k, :, cols_of(c)]

    def start_pair(c):
        pass_on(xa + at_x(2), r1, 0, c, XP)
        pass_on(xa + at_x(3), r2, 0, c, XM)

    def pass_pair(c):
        arrived(cut(r1, 0, c), r1s.at[c, 0])
        add(xa + at_x(1), 0, c)
        pass_on(xa + at_x(1), r2, 1, c, XP)

    def start_own(c):
        pass_on(xo + at_x(2), r1, 1, c, XM)

    def last_own(c):
        pass_on(xo + at_x(1), r2, 3, c, XP)

    def pass_own(c):
        arrived(cut(r1, 1, c), r1s.at[c, 1])
        add(xo + at_x(3), 1, c)
        pass_on(xo + at_x(3), r2, 2, c, XM)

    def both(i, c, k):
        arrived(r2.at[pl.ds(k, 2), :, cols_of(c)], r2s.at[c, k // 2])
        return tp[i, :, cols_of(c)] + r2[k, :, cols_of(c)] + r2[k + 1, :, cols_of(c)]

    def final_pair(c):
        tp[xa + x, :, cols_of(c)] = both(xa + x, c, 0)
        send(cut(tp, xa + x, c), pf.at[:, cols_of(c)], pfs, pa, tsem.at[PA])

    for c in range(CH):
        compute(c)
        start_pair(c)
        start_own(c)
        if c:
            pass_pair(c - 1)
        else:
            last_own(c)
    pass_pair(CH - 1)
    for c in range(1, CH):
        last_own(c)

    fin = flat3(jnp.sum(total()[:, 0:3, :], axis=0))
    lane = lax.broadcasted_iota(jnp.int32, (OWN, ROWS), 1)
    row = lax.broadcasted_iota(jnp.int32, (OWN, ROWS), 0) + d * OWN
    norm = 1.0 / jnp.sum(jnp.where(lane == row, fin, 0.0), axis=1, keepdims=True)
    f_out[...] = EPS * (f1 + jnp.log(u))
    near = lax.broadcasted_iota(jnp.int32, (8, 128), 1) // 48 == yhi
    g_out[...] = EPS * packed_row(jnp.where(near, g1 + jnp.log(v), go[1] + jnp.log(vo[1])))

    for c in range(CH):
        final_pair(c)
        if c:
            pass_own(c - 1)
    pass_own(CH - 1)
    for c in range(CH):
        width = CUTS[c + 1] - CUTS[c]
        t_out[:, pl.ds(pl.multiple_of(h * HALF + CUTS[c], 256), width)] = both(xo + x, c, 2) * norm
    arrived(pf, pfs)
    t_out[:, kother] = pf[...] * norm

    all_sent(lg, lsem.at[2])
    all_sent(go.at[0], lsem.at[3])
    all_sent(vo.at[0], lsem.at[4])
    all_sent(pf, tsem.at[PA])
    for to in (XP, XM):
        all_sent(tp.at[pl.ds(0, 3)], tsem.at[to])
    for cp in small:
        cp.wait_send()


def hand_out(t_in, f_in, g_in, t_out, f_out, g_out, sem):
    parts = [
        pltpu.make_async_copy(t_in.at[pl.ds(8 * k, 8)], t_out.at[pl.ds(8 * k, 8)], sem.at[k]) for k in range(OWN // 8)
    ]
    for cp in parts:
        cp.start()
    f_out[...] = f_in[...].reshape(ROWS)
    g_out[...] = g_in[...].reshape(COLS)
    for cp in parts:
        cp.wait()


def body(noise_latents, data_latents):
    dma = pltpu.SemaphoreType.DMA
    vm = pltpu.VMEM
    scratch = [
        vm((8, 2, PIECE, HALF), F32),
        vm((16, 2, 2, PIECE, HALF), F32),
        vm((ROWS, HALF), BF16),
        vm((ROWS, HALF), BF16),
        vm((2 * COLS, HALF), BF16),
        vm((2 * COLS, HALF), BF16),
        vm((ROWS, 128), F32),
        vm((2, BLK, 128), F32),
        vm((8, ROWS), F32),
        vm((NB, BLK, ROWS), F32),
        vm((NB, BLK, ROWS), F32),
        vm((COLS, ROWS), F32),
        vm((COLS, ROWS), F32),
        vm((COLS, ROWS), F32),
        vm((ROWS, COLS), F32),
        vm((ROWS, COLS), F32),
        vm((2, ROWS, COLS), BF16),
        vm((2, ROWS, COLS), BF16),
        vm((8, OWN, HALF), F32),
        vm((2, OWN, HALF), F32),
        vm((4, OWN, HALF), F32),
        vm((OWN, HALF), F32),
        vm((4, 8, 8, 128), F32),
        vm((1, 16, 16, 128), F32),
        vm((2, 16, 8, 128), F32),
        vm((2, 8, 128), F32),
        vm((2, 8, 128), F32),
        dma((2, 2)),
        dma((8, 2)),
        dma((16, 2)),
        dma((16,)),
        dma((NB,)),
        dma((5,)),
        dma((5,)),
        dma((2, 4)),
        dma((2, 1)),
        dma((2, 2)),
        dma((2,)),
        dma((CH, 2)),
        dma((CH, 2)),
        dma,
        dma((7,)),
        dma((7,)),
    ]
    t, f, g = pl.pallas_call(
        kernel,
        out_shape=(
            vm((OWN, WIDTH), F32),
            vm((1, ROWS), F32),
            vm((1, COLS), F32),
        ),
        in_specs=[pl.BlockSpec(memory_space=pl.ANY)] * 2,
        out_specs=(pl.BlockSpec(memory_space=pltpu.VMEM),) * 3,
        scratch_shapes=scratch,
        compiler_params=pltpu.CompilerParams(
            collective_id=0, has_side_effects=True, vmem_limit_bytes=60 * 2**20
        ),
        name="coupling",
    )(noise_latents, data_latents)
    return pl.pallas_call(
        hand_out,
        out_shape=(
            jax.ShapeDtypeStruct((OWN, WIDTH), F32),
            jax.ShapeDtypeStruct((ROWS,), F32),
            jax.ShapeDtypeStruct((COLS,), F32),
        ),
        in_specs=[pl.BlockSpec(memory_space=pltpu.VMEM)] * 3,
        out_specs=(pl.BlockSpec(memory_space=pl.ANY),) + (pl.BlockSpec(memory_space=pltpu.VMEM),) * 2,
        scratch_shapes=[pltpu.SemaphoreType.DMA((OWN // 8,))],
        compiler_params=pltpu.CompilerParams(vmem_limit_bytes=2 * 2**20),
        name="hand_out",
    )(t, f, g)


def solution(mesh):
    placed = (P(("noise", "dp"), None), P(("dp", "noise"), None))
    return jax.shard_map(
        body,
        mesh=mesh,
        in_specs=placed,
        out_specs=(P(("noise", "dp"), None), P("noise"), P("dp")),
        check_vma=False,
    )
```

```python
import functools
import math

import jax
import jax.numpy as jnp
from jax import lax
from jax.experimental import pallas as pl
from jax.experimental.pallas import tpu as pltpu
from jax.sharding import PartitionSpec as P

MESH = pl.DeviceIdType.MESH
F32 = jnp.float32
BF16 = jnp.bfloat16
EPS = 0.01

OWN = 48
WIDTH = 4096
HALF = WIDTH // 2
ROWS = 384
COLS = 768
BLK = 96
NB = COLS // BLK
PIECE = OWN // 2
LO_AT = (0, 64, 320, 384, 560, 768)
NSAMP = 6144
LOGN = math.log(NSAMP)
SCALE = 1.0 / (WIDTH * EPS)
CUTS = (0, 256, 512, 1024, 1536, 2048)
CH = len(CUTS) - 1


def split(v):
    hi = v.astype(BF16)
    return hi, (v - hi.astype(F32)).astype(BF16)


def dot_nt(a, b):
    return lax.dot_general(a, b, (((1,), (1,)), ((), ())), preferred_element_type=F32)


def dot_nn(a, b):
    return lax.dot_general(a, b, (((1,), (0,)), ((), ())), preferred_element_type=F32)


def pack_block(k, val):
    v3 = val.reshape(12, 8, 1)
    lane = lax.broadcasted_iota(jnp.int32, (12, 8, 128), 2)
    lead = lax.broadcasted_iota(jnp.int32, (12, 8, 128), 0) + 12 * k
    return jnp.sum(jnp.where(lane == lead, v3, 0.0), axis=0)


def unpack(packed, first, count):
    lane = lax.broadcasted_iota(jnp.int32, (count, 8, 128), 2)
    lead = lax.broadcasted_iota(jnp.int32, (count, 8, 128), 0) + first
    v3 = jnp.sum(jnp.where(lane == lead, packed[None], 0.0), axis=2, keepdims=True)
    return v3.reshape(8 * count, 1)


def to_row(col):
    r = lax.broadcasted_iota(jnp.int32, (128, 128), 0)
    c = lax.broadcasted_iota(jnp.int32, (128, 128), 1)
    return jnp.sum(jnp.where(r == c, col, 0.0), axis=0, keepdims=True)


def packed_row(packed):
    return jnp.concatenate([to_row(unpack(packed, 16 * q, 16)) for q in range(6)], axis=1)


def rows3(v):
    return [v[:, 128 * q : 128 * q + 128] for q in range(3)]


def flat3(v):
    return jnp.concatenate([v[q : q + 1] for q in range(3)], axis=1)


def kernel(
    x_hbm, y_hbm, t_out, f_out, g_out,
    xb, yb, xh, xl, yh_, yl_, xs, cse, rsq, ps, pr, lg, lo, q_, pn, po, wh, wl, tp, r1, r2, pf,
    rx, cx1, cx, go, vo,
    loc, xr, yr, yr2, prs, los, lsem, rxs, cx1s, cxs, gs, r1s, r2s, pfs, asem, tsem,
):
    n = lax.axis_index("noise")
    d = lax.axis_index("dp")
    core = lax.rem(n, 2)
    z = lax.rem(n // 2, 4)
    yhi = n // 8
    x = lax.rem(d, 4)
    ylo = d // 4
    h = lax.rem(yhi + ylo, 2)

    def at_z(k):
        return lax.rem(z + k, 4)

    def at_x(k):
        return lax.rem(x + k, 4)

    sib = (n + 1 - 2 * core, d)
    pa = (n, (1 - ylo) * 4 + x)
    pb = (((1 - yhi) * 4 + z) * 2 + core, (1 - ylo) * 4 + x)
    zp = ((yhi * 4 + at_z(1)) * 2 + core, d)
    zm = ((yhi * 4 + at_z(3)) * 2 + core, d)
    xp = (n, ylo * 4 + at_x(1))
    xm = (n, ylo * 4 + at_x(3))

    SRC = {"o": (yhi, h), "a": (yhi, 1 - h), "b": (1 - yhi, h), "c": (1 - yhi, 1 - h)}

    def slot(dz, who):
        hi, tile = SRC[who]
        return tile * 8 + hi * 4 + at_z(dz)

    def col_dev(p):
        return (p, lax.rem(p // 8 + h, 2) * 4 + x)

    kmine = pl.ds(pl.multiple_of(h * HALF, HALF), HALF)
    kother = pl.ds(pl.multiple_of((1 - h) * HALF, HALF), HALF)

    cx_own = [
        pltpu.make_async_copy(x_hbm.at[pl.ds(k * PIECE, PIECE), kmine], xb.at[d, k], loc.at[0, k]) for k in range(2)
    ]
    cy_own = [
        pltpu.make_async_copy(y_hbm.at[pl.ds(k * PIECE, PIECE), kmine], yb.at[slot(0, "o"), core, k], loc.at[1, k])
        for k in range(2)
    ]
    for cp in cx_own + cy_own:
        cp.start()

    barrier = pltpu.get_barrier_semaphore()

    for dev in (pa, pb, zp, zm, xp, xm, sib):
        pl.semaphore_signal(barrier, inc=1, device_id=dev, device_id_type=MESH)
    pl.semaphore_wait(barrier, 7)

    def send(src, dst, rsem, dev, ssend):
        pltpu.make_async_remote_copy(
            src_ref=src, dst_ref=dst, send_sem=ssend, recv_sem=rsem, device_id=dev, device_id_type=MESH
        ).start()

    def all_sent(ref, ssend):
        pltpu.make_async_remote_copy(
            src_ref=ref, dst_ref=ref, send_sem=ssend, recv_sem=lsem.at[0], device_id=sib, device_id_type=MESH
        ).wait_send()

    PA, PB, ZP, ZM, XP, XM, SIB = range(7)
    TO = [pa, pb, zp, zm, xp, xm, sib]

    def arrived(dst, rsem):
        pltpu.make_async_remote_copy(
            src_ref=dst, dst_ref=dst, send_sem=asem.at[0], recv_sem=rsem, device_id=sib, device_id_type=MESH
        ).wait_recv()

    def send_y(s, k, to):
        send(yb.at[s, core, k], yb.at[s, core, k], yr.at[s, k], TO[to], asem.at[to])

    def cross_y(s, k):
        send(yb.at[s, core, k], yb.at[s, core, k], yr2.at[s], sib, asem.at[SIB])

    def got_y(s, k):
        arrived(yb.at[s, core, k], yr.at[s, k])
        cross_y(s, k)

    def send_x(i, k, to):
        send(xb.at[i, k], xb.at[i, k], xr.at[i, k], TO[to], asem.at[to])

    def got_x(i, k):
        arrived(xb.at[i, k], xr.at[i, k])

    xa = (1 - ylo) * 4
    xo = ylo * 4

    def split_x(i):
        v = xb[i].reshape(OWN, HALF)
        hi, low = split(v)
        at = pl.ds(pl.multiple_of(i * OWN, OWN), OWN)
        xh[at, :] = hi
        xl[at, :] = low
        xs[at, :] = jnp.broadcast_to(jnp.sum(v * v, axis=1, keepdims=True), (OWN, 128))

    def fill_rsq(at):
        r = lax.broadcasted_iota(jnp.int32, (128, 128), 0)
        c = lax.broadcasted_iota(jnp.int32, (128, 128), 1)
        piece = jnp.sum(jnp.where(r == c, xs[at, :], 0.0), axis=0, keepdims=True)
        rsq[:, at] = jnp.broadcast_to(piece, (8, 128))

    def split_y(s):
        arrived(yb.at[s, 1 - core], yr2.at[s])
        v = yb[s].reshape(BLK, HALF)
        hi, low = split(v)
        at = pl.ds(pl.multiple_of(s * BLK, BLK), BLK)
        yh_[at, :] = hi
        yl_[at, :] = low
        return hi, low, jnp.sum(v * v, axis=1, keepdims=True)

    for k in range(2):
        send(x_hbm.at[pl.ds(k * PIECE, PIECE), kother], xb.at[d, k], xr.at[d, k], pa, asem.at[PA])
    for k in range(2):
        mine = slot(0, "o")
        send(y_hbm.at[pl.ds(k * PIECE, PIECE), kother], yb.at[mine, core, k], yr.at[mine, k], pa, asem.at[PA])
    for k in range(2):
        cx_own[k].wait()
        send_x(d, k, XP)
        send_x(d, k, XM)
        cy_own[k].wait()
        send_y(mine, k, ZP)
        send_y(mine, k, ZM)
        send_y(mine, k, PB)
        cross_y(mine, k)

    for k in range(2):
        got_x(xa + x, k)
        send_x(xa + x, k, XM)
        got_x(xo + at_x(3), k)
        send_x(xo + at_x(3), k, XP)
        got_y(slot(3, "o"), k)
        if k == 0:
            send_y(slot(3, "o"), 0, ZP)
        got_y(slot(0, "b"), k)
        if k == 0:
            send_y(slot(0, "b"), 0, ZM)
            send_y(slot(0, "b"), 0, ZP)
        got_y(slot(1, "o"), k)
        if k == 1:
            send_y(slot(1, "o"), 1, ZM)
        got_x(xo + at_x(1), k)
    for k in range(2):
        send_x(xa + x, k, XP)

    def split_first(i, c):
        split_x(lax.rem(i // 3 + ylo, 2) * 4 + at_x(lax.rem(i + i // 2, 4) * (1 - i // 3)))
        return c

    lax.fori_loop(0, 4, split_first, 0)

    for k in range(2):
        got_y(slot(0, "a"), k)
        send_y(slot(0, "a"), k, ZP)
        send_y(slot(0, "a"), k, ZM)
        send_y(slot(0, "a"), k, PB)
        got_x(xa + at_x(1), k)
        send_x(xa + at_x(1), k, XM)
        got_x(xo + at_x(2), k)
        got_y(slot(2, "o"), k)
    got_y(slot(1, "b"), 0)
    got_y(slot(3, "b"), 0)
    for k in range(2):
        send_y(slot(2, "o"), k, PB)

    def split_second(i, c):
        split_x(lax.rem(i + ylo, 2) * 4 + at_x(2 - i))
        return c

    lax.fori_loop(0, 2, split_second, 0)

    first = pl.ds(pl.multiple_of(256 * ylo, 128), 128)
    rest = pl.ds(pl.multiple_of(128 * (1 - ylo), 128), 256)
    fill_rsq(first)

    def pair_send(k, lanes):
        at = (k,) if lanes is None else (k, slice(None), lanes)
        pltpu.make_async_remote_copy(
            src_ref=ps.at[at], dst_ref=pr.at[at], send_sem=lsem.at[1], recv_sem=prs.at[k], device_id=pa, device_id_type=MESH
        ).start()

    def cross_part(hi, low, csq, lanes):
        both = dot_nt(jnp.concatenate([hi, low], axis=0), xh[lanes, :])
        cross = both[:BLK] + both[BLK:] + dot_nt(hi, xl[lanes, :])
        return (2.0 * cross - csq - rsq[0:1, lanes]) * SCALE

    def pair_first(e, k):
        hi, low, csq = split_y((1 - h) * 8 + k)
        cse[e] = jnp.broadcast_to(csq, (BLK, 128))
        ps[k, :, first] = cross_part(hi, low, csq, first)
        pair_send(k, first)

    def pair_rest(e, k):
        at = pl.ds(pl.multiple_of(((1 - h) * 8 + k) * BLK, BLK), BLK)
        ps[k, :, rest] = cross_part(yh_[at, :], yl_[at, :], cse[e, :, 0:1], rest)
        pair_send(k, rest)

    ka = yhi * 4 + z
    kc = (1 - yhi) * 4 + z
    pair_first(0, ka)

    for k in range(2):
        got_y(slot(0, "c"), k)
        if k == 0:
            send_y(slot(0, "c"), 0, ZM)
        else:
            pair_first(1, kc)
        got_y(slot(3, "a"), k)
        if k == 0:
            send_y(slot(3, "a"), 0, ZP)
            send_y(slot(0, "c"), 0, ZP)
        got_y(slot(1, "a"), k)
        if k == 1:
            send_y(slot(1, "a"), 1, ZM)
        got_x(xa + at_x(3), k)
        got_x(xa + at_x(2), k)
    for to in (ZP, ZM):
        send_y(slot(0, "c"), 1, to)
        send_y(slot(0, "b"), 1, to)

    def split_third(i, c):
        split_x(xa + at_x(2 + i))
        return c

    lax.fori_loop(0, 2, split_third, 0)
    for i in range(3):
        fill_rsq(pl.ds(128 * i, 128))

    def block(s):
        hi, low, csq = split_y(s)
        return cross_part(hi, low, csq, slice(None))

    def pair_block(dz, is_c):
        k = (is_c * (1 - yhi) + (1 - is_c) * yhi) * 4 + at_z(dz)
        ps[k] = block((1 - h) * 8 + k)
        pair_send(k, None)

    def own_block(dz, is_b):
        k = (is_b * (1 - yhi) + (1 - is_b) * yhi) * 4 + at_z(dz)
        lg[pl.ds(pl.multiple_of(k * BLK, BLK), BLK), :] = block(h * 8 + k)

    def group1(i, c):
        pair_block(1 + 2 * i, 0)
        return c

    def group3(i, c):
        own_block(i, 0)
        return c

    def group4(i, c):
        pair_block(1 + 2 * i, 1)
        return c

    def group5(i, c):
        own_block(lax.rem(i + 2, 4), (i + 2) // 4)
        return c

    pair_rest(0, ka)
    pair_rest(1, kc)
    lax.fori_loop(0, 2, group1, 0)
    for k in range(2):
        got_y(slot(2, "a"), k)
        send_y(slot(2, "a"), k, PB)
    for k in range(2):
        got_y(slot(2, "b"), k)
    pair_block(2, 0)
    lax.fori_loop(0, 2, group3, 0)
    for k in range(2):
        got_y(slot(1, "c"), k)
        got_y(slot(3, "c"), k)
    lax.fori_loop(0, 2, group4, 0)
    for k in range(2):
        got_y(slot(2, "c"), k)
    pair_block(2, 1)
    got_y(slot(1, "b"), 1)
    got_y(slot(3, "b"), 1)
    lax.fori_loop(0, 6, group5, 0)

    def rows_from(k, count):
        half = k // 384
        return pl.ds(pl.multiple_of(((1 - half) * yhi + half * (1 - yhi)) * 384 + k - half * 384, 16), count)

    def send_logits(k):
        at = rows_from(LO_AT[k], LO_AT[k + 1] - LO_AT[k])
        send(lg.at[at], lo.at[at], los.at[k], pa, lsem.at[2])

    def got_logits(k):
        at = rows_from(LO_AT[k], LO_AT[k + 1] - LO_AT[k])
        arrived(lo.at[at], los.at[k])

    def pair_wait(i, c):
        m8, s8 = c
        hi = (1 - i // 4) * yhi + (i // 4) * (1 - yhi)
        k = hi * 4 + at_z(lax.rem(3 * i, 4))
        arrived(pr.at[k], prs.at[k])
        at = pl.ds(pl.multiple_of(k * BLK, BLK), BLK)
        v = lg[at, :] + pr[k]
        lg[at, :] = v
        v = v.reshape(12, 8, ROWS)
        top = jnp.maximum(m8, jnp.max(v, axis=0))
        return top, s8 * jnp.exp(m8 - top) + jnp.sum(jnp.exp(v - top[None]), axis=0)

    stats = lax.fori_loop(0, NB // 2, pair_wait, (jnp.full((8, ROWS), -1e30, F32), jnp.zeros((8, ROWS), F32)))
    send_logits(0)
    m8, s8 = lax.fori_loop(NB // 2, NB, pair_wait, stats)

    def exchange(buf, sems, rnd, mine, peers, msg):
        buf[rnd, mine] = msg
        for dev in peers:
            pltpu.make_async_remote_copy(
                src_ref=buf.at[rnd, mine], dst_ref=buf.at[rnd, mine], send_sem=sems.at[0, rnd], recv_sem=sems.at[1, rnd],
                device_id=dev, device_id_type=MESH,
            ).start()
        every = buf.at[rnd, pl.ds(0, len(peers))]
        all_of = pltpu.make_async_remote_copy(
            src_ref=every, dst_ref=every, send_sem=sems.at[0, rnd], recv_sem=sems.at[1, rnd],
            device_id=peers[0], device_id_type=MESH,
        )
        small.append(all_of)

        def done():
            all_of.wait_recv()
            return buf[rnd]

        return done

    small = []
    row_peers = [(n, lax.rem(d + k, 8)) for k in range(1, 8)]
    col_peers = [col_dev(lax.rem(n + k, 16)) for k in range(1, 16)]

    def ex_rows(rnd, msg):
        return exchange(rx, rxs, rnd, d, row_peers, msg)

    def ex_cols(buf, sems, msg, rnd):
        return exchange(buf, sems, rnd, n, col_peers, msg)

    def row_msg(parts):
        parts = parts + [jnp.zeros((1, 128), F32)] * (8 - len(parts))
        return jnp.concatenate(parts, axis=0)

    def blk(k):
        return slice(BLK * k, BLK * k + BLK)

    m = jnp.max(m8, axis=0, keepdims=True)
    tot = jnp.sum(s8 * jnp.exp(m8 - m), axis=0, keepdims=True)
    done = ex_rows(0, row_msg(rows3(m) + rows3(tot)))
    send_logits(1)
    everyone = done()
    mm = everyone[:, 0:3, :]
    top = jnp.max(mm, axis=0)
    tt = jnp.sum(everyone[:, 3:6, :] * jnp.exp(mm - top[None]), axis=0)
    f1 = flat3(LOGN - top - jnp.log(tt))

    pm = jnp.zeros((8, 128), F32)
    pt = jnp.zeros((8, 128), F32)
    for k in range(NB):
        a = lg[blk(k), :] + f1
        cm = jnp.max(a, axis=1, keepdims=True)
        e = jnp.exp(a - cm)
        q_[blk(k), :] = e
        pm = pm + pack_block(k, cm)
        pt = pt + pack_block(k, jnp.sum(e, axis=1, keepdims=True))
    done = ex_cols(cx1, cx1s, jnp.concatenate([pm, pt], axis=0), 0)
    for ref, to in (
        (xb.at[pl.ds(0, 2)], PA),
        (yb.at[pl.ds(0, 4), core], PB),
        (yb.at[pl.ds(0, 5), core], ZP),
        (yb.at[pl.ds(0, 5), core], ZM),
        (xb.at[pl.ds(0, 3)], XP),
        (xb.at[pl.ds(0, 3)], XM),
        (yb.at[:, core], SIB),
    ):
        all_sent(ref, asem.at[to])
    all_sent(ps, lsem.at[1])
    everyone = done()
    mm = everyone[:, 0:8, :]
    top = jnp.max(mm, axis=0)
    tt = jnp.sum(everyone[:, 8:16, :] * jnp.exp(mm - top[None]), axis=0)
    used = lax.broadcasted_iota(jnp.int32, (8, 128), 1) < 96
    g1 = jnp.where(used, LOGN - top - jnp.log(jnp.where(used, tt, 1.0)), 0.0)
    go[0] = g1
    send(go.at[0], go.at[1], gs.at[0], pa, lsem.at[3])

    fac = jnp.exp(pm + g1)
    s8 = jnp.zeros((8, ROWS), F32)
    for k in range(NB):
        p = q_[blk(k), :] * unpack(fac, 12 * k, 12)
        q_[blk(k), :] = p
        s8 = s8 + jnp.sum(p.reshape(12, 8, ROWS), axis=0)

    def row_step(rnd, s8, between):
        done = ex_rows(rnd, row_msg(rows3(jnp.sum(s8, axis=0, keepdims=True))))
        between()
        return flat3(NSAMP / jnp.sum(done()[:, 0:3, :], axis=0))

    def col_step(rnd, u, between):
        pk = jnp.zeros((8, 128), F32)
        for k in range(NB):
            pk = pk + pack_block(k, jnp.sum(q_[blk(k), :] * u, axis=1, keepdims=True))
        done = ex_cols(cx, cxs, pk, rnd)
        between()
        tt = jnp.sum(done(), axis=0)
        return NSAMP / jnp.where(used, tt, 1.0)

    def row_sums(v):
        s8 = jnp.zeros((8, ROWS), F32)
        for k in range(NB):
            s8 = s8 + jnp.sum((q_[blk(k), :] * unpack(v, 12 * k, 12)).reshape(12, 8, ROWS), axis=0)
        return s8

    def turn(src, dst, some):
        for q in some:
            dst[:, 128 * q : 128 * q + 128] = src[128 * q : 128 * q + 128, :].T

    def far(some):
        for q in some:
            at = rows_from(128 * q, 128)
            lane = lax.broadcasted_iota(jnp.int32, (16, 8, 128), 2)
            lead = lax.broadcasted_iota(jnp.int32, (16, 8, 128), 0) + at.start // 8
            g = jnp.sum(jnp.where(lane == lead, go[1][None], 0.0), axis=2, keepdims=True).reshape(128, 1)
            po[:, pl.ds(pl.multiple_of(at.start, 128), 128)] = jnp.exp(lo[at, :] + f1 + g).T

    def in_row1():
        send_logits(2)
        send_logits(3)
        turn(q_, pn, range(0, 3))

    def in_row2():
        send_logits(4)
        arrived(go.at[1], gs.at[0])
        got_logits(0)
        got_logits(1)
        far(range(0, 2))

    def in_col2():
        got_logits(2)
        got_logits(3)
        far(range(2, 4))
        got_logits(4)
        far(range(4, 6))

    u = row_step(1, s8, in_row1)
    v = col_step(0, u, lambda: turn(q_, pn, range(3, 6)))
    u = row_step(2, row_sums(v), in_row2)
    v = col_step(1, u, in_col2)
    vo[0] = v
    send(vo.at[0], vo.at[1], gs.at[1], pa, lsem.at[4])
    total = ex_rows(3, row_msg(rows3(jnp.sum(row_sums(v), axis=0, keepdims=True))))

    hi, low = split(pn[...] * packed_row(v))
    wh[0] = hi
    wl[0] = low

    own_rows = pl.ds(pl.multiple_of(h * COLS, COLS), COLS)
    far_rows = pl.ds(pl.multiple_of((1 - h) * COLS, COLS), COLS)

    def part(i, rows, cols):
        return (
            dot_nn(wh[i], yh_[rows, cols]) + dot_nn(wh[i], yl_[rows, cols]) + dot_nn(wl[i], yh_[rows, cols])
        )

    def cols_of(c):
        return pl.ds(CUTS[c], CUTS[c + 1] - CUTS[c])

    def cut(ref, i, c):
        return ref.at[i, :, cols_of(c)]

    def compute(c):
        t = part(0, own_rows, cols_of(c))
        if c == 0:
            arrived(vo.at[1], gs.at[1])
            hi, low = split(po[...] * packed_row(vo[1]))
            wh[1] = hi
            wl[1] = low
        t = t + part(1, far_rows, cols_of(c))
        tp[:, :, cols_of(c)] = t.reshape(8, OWN, CUTS[c + 1] - CUTS[c])

    def pass_on(i, buf, k, c, to):
        sem = r1s.at[c, k] if buf is r1 else r2s.at[c, k // 2]
        send(cut(tp, i, c), cut(buf, k, c), sem, TO[to], tsem.at[to])

    def add(i, k, c):
        tp[i, :, cols_of(c)] = tp[i, :, cols_of(c)] + r1[k, :, cols_of(c)]

    def start_pair(c):
        pass_on(xa + at_x(2), r1, 0, c, XP)
        pass_on(xa + at_x(3), r2, 0, c, XM)

    def pass_pair(c):
        arrived(cut(r1, 0, c), r1s.at[c, 0])
        add(xa + at_x(1), 0, c)
        pass_on(xa + at_x(1), r2, 1, c, XP)

    def start_own(c):
        pass_on(xo + at_x(2), r1, 1, c, XM)

    def last_own(c):
        pass_on(xo + at_x(1), r2, 3, c, XP)

    def pass_own(c):
        arrived(cut(r1, 1, c), r1s.at[c, 1])
        add(xo + at_x(3), 1, c)
        pass_on(xo + at_x(3), r2, 2, c, XM)

    def both(i, c, k):
        arrived(r2.at[pl.ds(k, 2), :, cols_of(c)], r2s.at[c, k // 2])
        return tp[i, :, cols_of(c)] + r2[k, :, cols_of(c)] + r2[k + 1, :, cols_of(c)]

    def final_pair(c):
        tp[xa + x, :, cols_of(c)] = both(xa + x, c, 0)
        send(cut(tp, xa + x, c), pf.at[:, cols_of(c)], pfs, pa, tsem.at[PA])

    for c in range(CH):
        compute(c)
        start_pair(c)
        start_own(c)
        if c < 2:
            last_own(c)
        else:
            pass_pair(c - 2)
    for c in range(CH - 2, CH):
        pass_pair(c)
    for c in range(2, CH):
        last_own(c)

    fin = flat3(jnp.sum(total()[:, 0:3, :], axis=0))
    lane = lax.broadcasted_iota(jnp.int32, (OWN, ROWS), 1)
    row = lax.broadcasted_iota(jnp.int32, (OWN, ROWS), 0) + d * OWN
    norm = 1.0 / jnp.sum(jnp.where(lane == row, fin, 0.0), axis=1, keepdims=True)
    f_out[...] = EPS * (f1 + jnp.log(u))
    near = lax.broadcasted_iota(jnp.int32, (8, 128), 1) // 48 == yhi
    g_out[...] = EPS * packed_row(jnp.where(near, g1 + jnp.log(v), go[1] + jnp.log(vo[1])))

    for c in range(CH):
        final_pair(c)
        if c:
            pass_own(c - 1)
    pass_own(CH - 1)
    for c in range(CH):
        width = CUTS[c + 1] - CUTS[c]
        t_out[:, pl.ds(pl.multiple_of(h * HALF + CUTS[c], 256), width)] = both(xo + x, c, 2) * norm
    arrived(pf, pfs)
    t_out[:, kother] = pf[...] * norm

    all_sent(lg, lsem.at[2])
    all_sent(go.at[0], lsem.at[3])
    all_sent(vo.at[0], lsem.at[4])
    all_sent(pf, tsem.at[PA])
    for to in (XP, XM):
        all_sent(tp.at[pl.ds(0, 3)], tsem.at[to])
    for cp in small:
        cp.wait_send()


def hand_out(t_in, f_in, g_in, t_out, f_out, g_out, sem):
    parts = [
        pltpu.make_async_copy(t_in.at[pl.ds(8 * k, 8)], t_out.at[pl.ds(8 * k, 8)], sem.at[k]) for k in range(OWN // 8)
    ]
    for cp in parts:
        cp.start()
    f_out[...] = f_in[...].reshape(ROWS)
    g_out[...] = g_in[...].reshape(COLS)
    for cp in parts:
        cp.wait()


def body(noise_latents, data_latents):
    dma = pltpu.SemaphoreType.DMA
    vm = pltpu.VMEM
    scratch = [
        vm((8, 2, PIECE, HALF), F32),
        vm((16, 2, 2, PIECE, HALF), F32),
        vm((ROWS, HALF), BF16),
        vm((ROWS, HALF), BF16),
        vm((2 * COLS, HALF), BF16),
        vm((2 * COLS, HALF), BF16),
        vm((ROWS, 128), F32),
        vm((2, BLK, 128), F32),
        vm((8, ROWS), F32),
        vm((NB, BLK, ROWS), F32),
        vm((NB, BLK, ROWS), F32),
        vm((COLS, ROWS), F32),
        vm((COLS, ROWS), F32),
        vm((COLS, ROWS), F32),
        vm((ROWS, COLS), F32),
        vm((ROWS, COLS), F32),
        vm((2, ROWS, COLS), BF16),
        vm((2, ROWS, COLS), BF16),
        vm((8, OWN, HALF), F32),
        vm((2, OWN, HALF), F32),
        vm((4, OWN, HALF), F32),
        vm((OWN, HALF), F32),
        vm((4, 8, 8, 128), F32),
        vm((1, 16, 16, 128), F32),
        vm((2, 16, 8, 128), F32),
        vm((2, 8, 128), F32),
        vm((2, 8, 128), F32),
        dma((2, 2)),
        dma((8, 2)),
        dma((16, 2)),
        dma((16,)),
        dma((NB,)),
        dma((5,)),
        dma((5,)),
        dma((2, 4)),
        dma((2, 1)),
        dma((2, 2)),
        dma((2,)),
        dma((CH, 2)),
        dma((CH, 2)),
        dma,
        dma((7,)),
        dma((7,)),
    ]
    t, f, g = pl.pallas_call(
        kernel,
        out_shape=(
            vm((OWN, WIDTH), F32),
            vm((1, ROWS), F32),
            vm((1, COLS), F32),
        ),
        in_specs=[pl.BlockSpec(memory_space=pl.ANY)] * 2,
        out_specs=(pl.BlockSpec(memory_space=pltpu.VMEM),) * 3,
        scratch_shapes=scratch,
        compiler_params=pltpu.CompilerParams(
            collective_id=0, has_side_effects=True, vmem_limit_bytes=60 * 2**20
        ),
        name="coupling",
    )(noise_latents, data_latents)
    return pl.pallas_call(
        hand_out,
        out_shape=(
            jax.ShapeDtypeStruct((OWN, WIDTH), F32),
            jax.ShapeDtypeStruct((ROWS,), F32),
            jax.ShapeDtypeStruct((COLS,), F32),
        ),
        in_specs=[pl.BlockSpec(memory_space=pltpu.VMEM)] * 3,
        out_specs=(pl.BlockSpec(memory_space=pl.ANY),) + (pl.BlockSpec(memory_space=pltpu.VMEM),) * 2,
        scratch_shapes=[pltpu.SemaphoreType.DMA((OWN // 8,))],
        compiler_params=pltpu.CompilerParams(vmem_limit_bytes=2 * 2**20),
        name="hand_out",
    )(t, f, g)


def solution(mesh):
    placed = (P(("noise", "dp"), None), P(("dp", "noise"), None))
    return jax.shard_map(
        body,
        mesh=mesh,
        in_specs=placed,
        out_specs=(P(("noise", "dp"), None), P("noise"), P("dp")),
        check_vma=False,
    )
```

```python
import functools
import math

import jax
import jax.numpy as jnp
from jax import lax
from jax.experimental import pallas as pl
from jax.experimental.pallas import tpu as pltpu
from jax.sharding import PartitionSpec as P

MESH = pl.DeviceIdType.MESH
F32 = jnp.float32
BF16 = jnp.bfloat16
EPS = 0.01

OWN = 48
WIDTH = 4096
HALF = WIDTH // 2
ROWS = 384
COLS = 768
BLK = 96
NB = COLS // BLK
PIECE = OWN // 2
LO_AT = (0, 64, 320, 384, 560, 768)
NSAMP = 6144
LOGN = math.log(NSAMP)
SCALE = 1.0 / (WIDTH * EPS)
CUTS = (0, 256, 512, 1024, 1536, 2048)
CH = len(CUTS) - 1


def split(v):
    hi = v.astype(BF16)
    return hi, (v - hi.astype(F32)).astype(BF16)


def dot_nt(a, b):
    return lax.dot_general(a, b, (((1,), (1,)), ((), ())), preferred_element_type=F32)


def dot_nn(a, b):
    return lax.dot_general(a, b, (((1,), (0,)), ((), ())), preferred_element_type=F32)


def pack_block(k, val):
    v3 = val.reshape(12, 8, 1)
    lane = lax.broadcasted_iota(jnp.int32, (12, 8, 128), 2)
    lead = lax.broadcasted_iota(jnp.int32, (12, 8, 128), 0) + 12 * k
    return jnp.sum(jnp.where(lane == lead, v3, 0.0), axis=0)


def unpack(packed, first, count):
    lane = lax.broadcasted_iota(jnp.int32, (count, 8, 128), 2)
    lead = lax.broadcasted_iota(jnp.int32, (count, 8, 128), 0) + first
    v3 = jnp.sum(jnp.where(lane == lead, packed[None], 0.0), axis=2, keepdims=True)
    return v3.reshape(8 * count, 1)


def to_row(col):
    r = lax.broadcasted_iota(jnp.int32, (128, 128), 0)
    c = lax.broadcasted_iota(jnp.int32, (128, 128), 1)
    return jnp.sum(jnp.where(r == c, col, 0.0), axis=0, keepdims=True)


def packed_row(packed):
    return jnp.concatenate([to_row(unpack(packed, 16 * q, 16)) for q in range(6)], axis=1)


def rows3(v):
    return [v[:, 128 * q : 128 * q + 128] for q in range(3)]


def flat3(v):
    return jnp.concatenate([v[q : q + 1] for q in range(3)], axis=1)


def kernel(
    x_hbm, y_hbm, t_out, f_out, g_out,
    xb, yb, xh, xl, yh_, yl_, xs, cse, rsq, ps, pr, lg, lo, q_, pn, po, wh, wl, tp, r1, r2, pf,
    rx, cx1, cx, go, vo,
    loc, xr, yr, yr2, prs, los, lsem, rxs, cx1s, cxs, gs, r1s, r2s, pfs, asem, tsem,
):
    n = lax.axis_index("noise")
    d = lax.axis_index("dp")
    core = lax.rem(n, 2)
    z = lax.rem(n // 2, 4)
    yhi = n // 8
    x = lax.rem(d, 4)
    ylo = d // 4
    h = lax.rem(yhi + ylo, 2)

    def at_z(k):
        return lax.rem(z + k, 4)

    def at_x(k):
        return lax.rem(x + k, 4)

    sib = (n + 1 - 2 * core, d)
    pa = (n, (1 - ylo) * 4 + x)
    pb = (((1 - yhi) * 4 + z) * 2 + core, (1 - ylo) * 4 + x)
    zp = ((yhi * 4 + at_z(1)) * 2 + core, d)
    zm = ((yhi * 4 + at_z(3)) * 2 + core, d)
    xp = (n, ylo * 4 + at_x(1))
    xm = (n, ylo * 4 + at_x(3))

    SRC = {"o": (yhi, h), "a": (yhi, 1 - h), "b": (1 - yhi, h), "c": (1 - yhi, 1 - h)}

    def slot(dz, who):
        hi, tile = SRC[who]
        return tile * 8 + hi * 4 + at_z(dz)

    def col_dev(p):
        return (p, lax.rem(p // 8 + h, 2) * 4 + x)

    kmine = pl.ds(pl.multiple_of(h * HALF, HALF), HALF)
    kother = pl.ds(pl.multiple_of((1 - h) * HALF, HALF), HALF)

    cx_own = [
        pltpu.make_async_copy(x_hbm.at[pl.ds(k * PIECE, PIECE), kmine], xb.at[d, k], loc.at[0, k]) for k in range(2)
    ]
    cy_own = [
        pltpu.make_async_copy(y_hbm.at[pl.ds(k * PIECE, PIECE), kmine], yb.at[slot(0, "o"), core, k], loc.at[1, k])
        for k in range(2)
    ]
    for cp in cx_own + cy_own:
        cp.start()

    barrier = pltpu.get_barrier_semaphore()

    for dev in (pa, pb, zp, zm, xp, xm, sib):
        pl.semaphore_signal(barrier, inc=1, device_id=dev, device_id_type=MESH)
    pl.semaphore_wait(barrier, 7)

    def send(src, dst, rsem, dev, ssend):
        pltpu.make_async_remote_copy(
            src_ref=src, dst_ref=dst, send_sem=ssend, recv_sem=rsem, device_id=dev, device_id_type=MESH
        ).start()

    def all_sent(ref, ssend):
        pltpu.make_async_remote_copy(
            src_ref=ref, dst_ref=ref, send_sem=ssend, recv_sem=lsem.at[0], device_id=sib, device_id_type=MESH
        ).wait_send()

    PA, PB, ZP, ZM, XP, XM, SIB = range(7)
    TO = [pa, pb, zp, zm, xp, xm, sib]

    def arrived(dst, rsem):
        pltpu.make_async_remote_copy(
            src_ref=dst, dst_ref=dst, send_sem=asem.at[0], recv_sem=rsem, device_id=sib, device_id_type=MESH
        ).wait_recv()

    def send_y(s, k, to):
        send(yb.at[s, core, k], yb.at[s, core, k], yr.at[s, k], TO[to], asem.at[to])

    def cross_y(s, k):
        send(yb.at[s, core, k], yb.at[s, core, k], yr2.at[s], sib, asem.at[SIB])

    def got_y(s, k):
        arrived(yb.at[s, core, k], yr.at[s, k])
        cross_y(s, k)

    def send_x(i, k, to):
        send(xb.at[i, k], xb.at[i, k], xr.at[i, k], TO[to], asem.at[to])

    def got_x(i, k):
        arrived(xb.at[i, k], xr.at[i, k])

    xa = (1 - ylo) * 4
    xo = ylo * 4

    def split_x(i):
        v = xb[i].reshape(OWN, HALF)
        hi, low = split(v)
        at = pl.ds(pl.multiple_of(i * OWN, OWN), OWN)
        xh[at, :] = hi
        xl[at, :] = low
        xs[at, :] = jnp.broadcast_to(jnp.sum(v * v, axis=1, keepdims=True), (OWN, 128))

    def fill_rsq(at):
        r = lax.broadcasted_iota(jnp.int32, (128, 128), 0)
        c = lax.broadcasted_iota(jnp.int32, (128, 128), 1)
        piece = jnp.sum(jnp.where(r == c, xs[at, :], 0.0), axis=0, keepdims=True)
        rsq[:, at] = jnp.broadcast_to(piece, (8, 128))

    def split_y(s):
        arrived(yb.at[s, 1 - core], yr2.at[s])
        v = yb[s].reshape(BLK, HALF)
        hi, low = split(v)
        at = pl.ds(pl.multiple_of(s * BLK, BLK), BLK)
        yh_[at, :] = hi
        yl_[at, :] = low
        return hi, low, jnp.sum(v * v, axis=1, keepdims=True)

    for k in range(2):
        send(x_hbm.at[pl.ds(k * PIECE, PIECE), kother], xb.at[d, k], xr.at[d, k], pa, asem.at[PA])
    for k in range(2):
        mine = slot(0, "o")
        send(y_hbm.at[pl.ds(k * PIECE, PIECE), kother], yb.at[mine, core, k], yr.at[mine, k], pa, asem.at[PA])
    for k in range(2):
        cx_own[k].wait()
        send_x(d, k, XP)
        send_x(d, k, XM)
        cy_own[k].wait()
        send_y(mine, k, ZP)
        send_y(mine, k, ZM)
        send_y(mine, k, PB)
        cross_y(mine, k)

    for k in range(2):
        got_x(xa + x, k)
        send_x(xa + x, k, XM)
        got_x(xo + at_x(3), k)
        send_x(xo + at_x(3), k, XP)
        got_y(slot(3, "o"), k)
        if k == 0:
            send_y(slot(3, "o"), 0, ZP)
        got_y(slot(0, "b"), k)
        if k == 0:
            send_y(slot(0, "b"), 0, ZM)
            send_y(slot(0, "b"), 0, ZP)
        got_y(slot(1, "o"), k)
        if k == 1:
            send_y(slot(1, "o"), 1, ZM)
        got_x(xo + at_x(1), k)
    for k in range(2):
        send_x(xa + x, k, XP)

    def split_first(i, c):
        split_x(lax.rem(i // 3 + ylo, 2) * 4 + at_x(lax.rem(i + i // 2, 4) * (1 - i // 3)))
        return c

    lax.fori_loop(0, 4, split_first, 0)

    for k in range(2):
        got_y(slot(0, "a"), k)
        send_y(slot(0, "a"), k, ZP)
        send_y(slot(0, "a"), k, ZM)
        send_y(slot(0, "a"), k, PB)
        got_x(xa + at_x(1), k)
        send_x(xa + at_x(1), k, XM)
        got_x(xo + at_x(2), k)
        got_y(slot(2, "o"), k)
    got_y(slot(1, "b"), 0)
    got_y(slot(3, "b"), 0)
    for k in range(2):
        send_y(slot(2, "o"), k, PB)

    def split_second(i, c):
        split_x(lax.rem(i + ylo, 2) * 4 + at_x(2 - i))
        return c

    lax.fori_loop(0, 2, split_second, 0)

    first = pl.ds(pl.multiple_of(256 * ylo, 128), 128)
    rest = pl.ds(pl.multiple_of(128 * (1 - ylo), 128), 256)
    fill_rsq(first)

    def pair_send(k, lanes):
        at = (k,) if lanes is None else (k, slice(None), lanes)
        pltpu.make_async_remote_copy(
            src_ref=ps.at[at], dst_ref=pr.at[at], send_sem=lsem.at[1], recv_sem=prs.at[k], device_id=pa, device_id_type=MESH
        ).start()

    def cross_part(hi, low, csq, lanes):
        both = dot_nt(jnp.concatenate([hi, low], axis=0), xh[lanes, :])
        cross = both[:BLK] + both[BLK:] + dot_nt(hi, xl[lanes, :])
        return (2.0 * cross - csq - rsq[0:1, lanes]) * SCALE

    def pair_first(e, k):
        hi, low, csq = split_y((1 - h) * 8 + k)
        cse[e] = jnp.broadcast_to(csq, (BLK, 128))
        ps[k, :, first] = cross_part(hi, low, csq, first)
        pair_send(k, first)

    def pair_rest(e, k):
        at = pl.ds(pl.multiple_of(((1 - h) * 8 + k) * BLK, BLK), BLK)
        ps[k, :, rest] = cross_part(yh_[at, :], yl_[at, :], cse[e, :, 0:1], rest)
        pair_send(k, rest)

    ka = yhi * 4 + z
    kc = (1 - yhi) * 4 + z
    pair_first(0, ka)

    for k in range(2):
        got_y(slot(0, "c"), k)
        if k == 0:
            send_y(slot(0, "c"), 0, ZM)
        else:
            pair_first(1, kc)
        got_y(slot(3, "a"), k)
        if k == 0:
            send_y(slot(3, "a"), 0, ZP)
            send_y(slot(0, "c"), 0, ZP)
        got_y(slot(1, "a"), k)
        if k == 1:
            send_y(slot(1, "a"), 1, ZM)
        got_x(xa + at_x(3), k)
        got_x(xa + at_x(2), k)
    for to in (ZP, ZM):
        send_y(slot(0, "c"), 1, to)
        send_y(slot(0, "b"), 1, to)

    def split_third(i, c):
        split_x(xa + at_x(2 + i))
        return c

    lax.fori_loop(0, 2, split_third, 0)
    for i in range(3):
        fill_rsq(pl.ds(128 * i, 128))

    def block(s):
        hi, low, csq = split_y(s)
        return cross_part(hi, low, csq, slice(None))

    def pair_block(dz, is_c):
        k = (is_c * (1 - yhi) + (1 - is_c) * yhi) * 4 + at_z(dz)
        ps[k] = block((1 - h) * 8 + k)
        pair_send(k, None)

    def own_block(dz, is_b):
        k = (is_b * (1 - yhi) + (1 - is_b) * yhi) * 4 + at_z(dz)
        lg[pl.ds(pl.multiple_of(k * BLK, BLK), BLK), :] = block(h * 8 + k)

    def group1(i, c):
        pair_block(1 + 2 * i, 0)
        return c

    def group3(i, c):
        own_block(i, 0)
        return c

    def group4(i, c):
        pair_block(1 + 2 * i, 1)
        return c

    def group5(i, c):
        own_block(lax.rem(i + 2, 4), (i + 2) // 4)
        return c

    pair_rest(0, ka)
    pair_rest(1, kc)
    lax.fori_loop(0, 2, group1, 0)
    for k in range(2):
        got_y(slot(2, "a"), k)
        send_y(slot(2, "a"), k, PB)
    for k in range(2):
        got_y(slot(2, "b"), k)
    pair_block(2, 0)
    lax.fori_loop(0, 2, group3, 0)
    for k in range(2):
        got_y(slot(1, "c"), k)
        got_y(slot(3, "c"), k)
    lax.fori_loop(0, 2, group4, 0)
    for k in range(2):
        got_y(slot(2, "c"), k)
    pair_block(2, 1)
    got_y(slot(1, "b"), 1)
    got_y(slot(3, "b"), 1)
    lax.fori_loop(0, 6, group5, 0)

    def rows_from(k, count):
        half = k // 384
        return pl.ds(pl.multiple_of(((1 - half) * yhi + half * (1 - yhi)) * 384 + k - half * 384, 16), count)

    def send_logits(k):
        at = rows_from(LO_AT[k], LO_AT[k + 1] - LO_AT[k])
        send(lg.at[at], lo.at[at], los.at[k], pa, lsem.at[2])

    def got_logits(k):
        at = rows_from(LO_AT[k], LO_AT[k + 1] - LO_AT[k])
        arrived(lo.at[at], los.at[k])

    def pair_wait(i, c):
        m8, s8 = c
        hi = (1 - i // 4) * yhi + (i // 4) * (1 - yhi)
        k = hi * 4 + at_z(lax.rem(3 * i, 4))
        arrived(pr.at[k], prs.at[k])
        at = pl.ds(pl.multiple_of(k * BLK, BLK), BLK)
        v = lg[at, :] + pr[k]
        lg[at, :] = v
        v = v.reshape(12, 8, ROWS)
        top = jnp.maximum(m8, jnp.max(v, axis=0))
        return top, s8 * jnp.exp(m8 - top) + jnp.sum(jnp.exp(v - top[None]), axis=0)

    stats = lax.fori_loop(0, NB // 2, pair_wait, (jnp.full((8, ROWS), -1e30, F32), jnp.zeros((8, ROWS), F32)))
    send_logits(0)
    m8, s8 = lax.fori_loop(NB // 2, NB, pair_wait, stats)

    def exchange(buf, sems, rnd, mine, peers, msg):
        buf[rnd, mine] = msg
        for dev in peers:
            pltpu.make_async_remote_copy(
                src_ref=buf.at[rnd, mine], dst_ref=buf.at[rnd, mine], send_sem=sems.at[0, rnd], recv_sem=sems.at[1, rnd],
                device_id=dev, device_id_type=MESH,
            ).start()
        every = buf.at[rnd, pl.ds(0, len(peers))]
        all_of = pltpu.make_async_remote_copy(
            src_ref=every, dst_ref=every, send_sem=sems.at[0, rnd], recv_sem=sems.at[1, rnd],
            device_id=peers[0], device_id_type=MESH,
        )
        small.append(all_of)

        def done():
            all_of.wait_recv()
            return buf[rnd]

        return done

    small = []
    row_peers = [(n, lax.rem(ylo + f, 2) * 4 + at_x(dx)) for dx in (2, 1, 3, 0) for f in (1, 0) if dx or f]
    col_peers = [
        col_dev((lax.rem(yhi + f, 2) * 4 + at_z(dz)) * 2 + lax.rem(core + o, 2))
        for dz in (2, 1, 3, 0)
        for f in (1, 0)
        for o in (1, 0)
        if dz or f or o
    ]

    def ex_rows(rnd, msg):
        return exchange(rx, rxs, rnd, d, row_peers, msg)

    def ex_cols(buf, sems, msg, rnd):
        return exchange(buf, sems, rnd, n, col_peers, msg)

    def row_msg(parts):
        parts = parts + [jnp.zeros((1, 128), F32)] * (8 - len(parts))
        return jnp.concatenate(parts, axis=0)

    def blk(k):
        return slice(BLK * k, BLK * k + BLK)

    m = jnp.max(m8, axis=0, keepdims=True)
    tot = jnp.sum(s8 * jnp.exp(m8 - m), axis=0, keepdims=True)
    done = ex_rows(0, row_msg(rows3(m) + rows3(tot)))
    send_logits(1)
    everyone = done()
    mm = everyone[:, 0:3, :]
    top = jnp.max(mm, axis=0)
    tt = jnp.sum(everyone[:, 3:6, :] * jnp.exp(mm - top[None]), axis=0)
    f1 = flat3(LOGN - top - jnp.log(tt))

    pm = jnp.zeros((8, 128), F32)
    pt = jnp.zeros((8, 128), F32)
    for k in range(NB):
        a = lg[blk(k), :] + f1
        cm = jnp.max(a, axis=1, keepdims=True)
        e = jnp.exp(a - cm)
        q_[blk(k), :] = e
        pm = pm + pack_block(k, cm)
        pt = pt + pack_block(k, jnp.sum(e, axis=1, keepdims=True))
    done = ex_cols(cx1, cx1s, jnp.concatenate([pm, pt], axis=0), 0)
    for ref, to in (
        (xb.at[pl.ds(0, 2)], PA),
        (yb.at[pl.ds(0, 4), core], PB),
        (yb.at[pl.ds(0, 5), core], ZP),
        (yb.at[pl.ds(0, 5), core], ZM),
        (xb.at[pl.ds(0, 3)], XP),
        (xb.at[pl.ds(0, 3)], XM),
        (yb.at[:, core], SIB),
    ):
        all_sent(ref, asem.at[to])
    all_sent(ps, lsem.at[1])
    everyone = done()
    mm = everyone[:, 0:8, :]
    top = jnp.max(mm, axis=0)
    tt = jnp.sum(everyone[:, 8:16, :] * jnp.exp(mm - top[None]), axis=0)
    used = lax.broadcasted_iota(jnp.int32, (8, 128), 1) < 96
    g1 = jnp.where(used, LOGN - top - jnp.log(jnp.where(used, tt, 1.0)), 0.0)
    go[0] = g1
    send(go.at[0], go.at[1], gs.at[0], pa, lsem.at[3])

    fac = jnp.exp(pm + g1)
    s8 = jnp.zeros((8, ROWS), F32)
    for k in range(NB):
        p = q_[blk(k), :] * unpack(fac, 12 * k, 12)
        q_[blk(k), :] = p
        s8 = s8 + jnp.sum(p.reshape(12, 8, ROWS), axis=0)

    def row_step(rnd, s8, between):
        done = ex_rows(rnd, row_msg(rows3(jnp.sum(s8, axis=0, keepdims=True))))
        between()
        return flat3(NSAMP / jnp.sum(done()[:, 0:3, :], axis=0))

    def col_step(rnd, u, between):
        pk = jnp.zeros((8, 128), F32)
        for k in range(NB):
            pk = pk + pack_block(k, jnp.sum(q_[blk(k), :] * u, axis=1, keepdims=True))
        done = ex_cols(cx, cxs, pk, rnd)
        between()
        tt = jnp.sum(done(), axis=0)
        return NSAMP / jnp.where(used, tt, 1.0)

    def row_sums(v):
        s8 = jnp.zeros((8, ROWS), F32)
        for k in range(NB):
            s8 = s8 + jnp.sum((q_[blk(k), :] * unpack(v, 12 * k, 12)).reshape(12, 8, ROWS), axis=0)
        return s8

    def turn(src, dst, some):
        for q in some:
            dst[:, 128 * q : 128 * q + 128] = src[128 * q : 128 * q + 128, :].T

    def far(some):
        for q in some:
            at = rows_from(128 * q, 128)
            lane = lax.broadcasted_iota(jnp.int32, (16, 8, 128), 2)
            lead = lax.broadcasted_iota(jnp.int32, (16, 8, 128), 0) + at.start // 8
            g = jnp.sum(jnp.where(lane == lead, go[1][None], 0.0), axis=2, keepdims=True).reshape(128, 1)
            po[:, pl.ds(pl.multiple_of(at.start, 128), 128)] = jnp.exp(lo[at, :] + f1 + g).T

    def in_row1():
        send_logits(2)
        send_logits(3)
        turn(q_, pn, range(0, 3))

    def in_row2():
        send_logits(4)
        arrived(go.at[1], gs.at[0])
        got_logits(0)
        got_logits(1)
        far(range(0, 2))

    def in_col2():
        got_logits(2)
        got_logits(3)
        far(range(2, 4))
        got_logits(4)
        far(range(4, 6))

    u = row_step(1, s8, in_row1)
    v = col_step(0, u, lambda: turn(q_, pn, range(3, 6)))
    u = row_step(2, row_sums(v), in_row2)
    v = col_step(1, u, in_col2)
    vo[0] = v
    send(vo.at[0], vo.at[1], gs.at[1], pa, lsem.at[4])
    total = ex_rows(3, row_msg(rows3(jnp.sum(row_sums(v), axis=0, keepdims=True))))

    hi, low = split(pn[...] * packed_row(v))
    wh[0] = hi
    wl[0] = low

    own_rows = pl.ds(pl.multiple_of(h * COLS, COLS), COLS)
    far_rows = pl.ds(pl.multiple_of((1 - h) * COLS, COLS), COLS)

    def part(i, rows, cols):
        return (
            dot_nn(wh[i], yh_[rows, cols]) + dot_nn(wh[i], yl_[rows, cols]) + dot_nn(wl[i], yh_[rows, cols])
        )

    def cols_of(c):
        return pl.ds(CUTS[c], CUTS[c + 1] - CUTS[c])

    def cut(ref, i, c):
        return ref.at[i, :, cols_of(c)]

    def compute(c):
        t = part(0, own_rows, cols_of(c))
        if c == 0:
            arrived(vo.at[1], gs.at[1])
            hi, low = split(po[...] * packed_row(vo[1]))
            wh[1] = hi
            wl[1] = low
        t = t + part(1, far_rows, cols_of(c))
        tp[:, :, cols_of(c)] = t.reshape(8, OWN, CUTS[c + 1] - CUTS[c])

    def pass_on(i, buf, k, c, to):
        sem = r1s.at[c, k] if buf is r1 else r2s.at[c, k // 2]
        send(cut(tp, i, c), cut(buf, k, c), sem, TO[to], tsem.at[to])

    def add(i, k, c):
        tp[i, :, cols_of(c)] = tp[i, :, cols_of(c)] + r1[k, :, cols_of(c)]

    def start_pair(c):
        pass_on(xa + at_x(2), r1, 0, c, XP)
        pass_on(xa + at_x(3), r2, 0, c, XM)

    def pass_pair(c):
        arrived(cut(r1, 0, c), r1s.at[c, 0])
        add(xa + at_x(1), 0, c)
        pass_on(xa + at_x(1), r2, 1, c, XP)

    def start_own(c):
        pass_on(xo + at_x(2), r1, 1, c, XM)

    def last_own(c):
        pass_on(xo + at_x(1), r2, 3, c, XP)

    def pass_own(c):
        arrived(cut(r1, 1, c), r1s.at[c, 1])
        add(xo + at_x(3), 1, c)
        pass_on(xo + at_x(3), r2, 2, c, XM)

    def both(i, c, k):
        arrived(r2.at[pl.ds(k, 2), :, cols_of(c)], r2s.at[c, k // 2])
        return tp[i, :, cols_of(c)] + r2[k, :, cols_of(c)] + r2[k + 1, :, cols_of(c)]

    def final_pair(c):
        tp[xa + x, :, cols_of(c)] = both(xa + x, c, 0)
        send(cut(tp, xa + x, c), pf.at[:, cols_of(c)], pfs, pa, tsem.at[PA])

    for c in range(CH):
        compute(c)
        start_pair(c)
        start_own(c)
        if c < 2:
            last_own(c)
        else:
            pass_pair(c - 2)
    for c in range(CH - 2, CH):
        pass_pair(c)
    for c in range(2, CH):
        last_own(c)

    fin = flat3(jnp.sum(total()[:, 0:3, :], axis=0))
    lane = lax.broadcasted_iota(jnp.int32, (OWN, ROWS), 1)
    row = lax.broadcasted_iota(jnp.int32, (OWN, ROWS), 0) + d * OWN
    norm = 1.0 / jnp.sum(jnp.where(lane == row, fin, 0.0), axis=1, keepdims=True)
    f_out[...] = EPS * (f1 + jnp.log(u))
    near = lax.broadcasted_iota(jnp.int32, (8, 128), 1) // 48 == yhi
    g_out[...] = EPS * packed_row(jnp.where(near, g1 + jnp.log(v), go[1] + jnp.log(vo[1])))

    for c in range(CH):
        final_pair(c)
        if c:
            pass_own(c - 1)
    pass_own(CH - 1)
    for c in range(CH):
        width = CUTS[c + 1] - CUTS[c]
        t_out[:, pl.ds(pl.multiple_of(h * HALF + CUTS[c], 256), width)] = both(xo + x, c, 2) * norm
    arrived(pf, pfs)
    t_out[:, kother] = pf[...] * norm

    all_sent(lg, lsem.at[2])
    all_sent(go.at[0], lsem.at[3])
    all_sent(vo.at[0], lsem.at[4])
    all_sent(pf, tsem.at[PA])
    for to in (XP, XM):
        all_sent(tp.at[pl.ds(0, 3)], tsem.at[to])
    for cp in small:
        cp.wait_send()


def hand_out(t_in, f_in, g_in, t_out, f_out, g_out, sem):
    parts = [
        pltpu.make_async_copy(t_in.at[pl.ds(8 * k, 8)], t_out.at[pl.ds(8 * k, 8)], sem.at[k]) for k in range(OWN // 8)
    ]
    for cp in parts:
        cp.start()
    f_out[...] = f_in[...].reshape(ROWS)
    g_out[...] = g_in[...].reshape(COLS)
    for cp in parts:
        cp.wait()


def body(noise_latents, data_latents):
    dma = pltpu.SemaphoreType.DMA
    vm = pltpu.VMEM
    scratch = [
        vm((8, 2, PIECE, HALF), F32),
        vm((16, 2, 2, PIECE, HALF), F32),
        vm((ROWS, HALF), BF16),
        vm((ROWS, HALF), BF16),
        vm((2 * COLS, HALF), BF16),
        vm((2 * COLS, HALF), BF16),
        vm((ROWS, 128), F32),
        vm((2, BLK, 128), F32),
        vm((8, ROWS), F32),
        vm((NB, BLK, ROWS), F32),
        vm((NB, BLK, ROWS), F32),
        vm((COLS, ROWS), F32),
        vm((COLS, ROWS), F32),
        vm((COLS, ROWS), F32),
        vm((ROWS, COLS), F32),
        vm((ROWS, COLS), F32),
        vm((2, ROWS, COLS), BF16),
        vm((2, ROWS, COLS), BF16),
        vm((8, OWN, HALF), F32),
        vm((2, OWN, HALF), F32),
        vm((4, OWN, HALF), F32),
        vm((OWN, HALF), F32),
        vm((4, 8, 8, 128), F32),
        vm((1, 16, 16, 128), F32),
        vm((2, 16, 8, 128), F32),
        vm((2, 8, 128), F32),
        vm((2, 8, 128), F32),
        dma((2, 2)),
        dma((8, 2)),
        dma((16, 2)),
        dma((16,)),
        dma((NB,)),
        dma((5,)),
        dma((5,)),
        dma((2, 4)),
        dma((2, 1)),
        dma((2, 2)),
        dma((2,)),
        dma((CH, 2)),
        dma((CH, 2)),
        dma,
        dma((7,)),
        dma((7,)),
    ]
    t, f, g = pl.pallas_call(
        kernel,
        out_shape=(
            vm((OWN, WIDTH), F32),
            vm((1, ROWS), F32),
            vm((1, COLS), F32),
        ),
        in_specs=[pl.BlockSpec(memory_space=pl.ANY)] * 2,
        out_specs=(pl.BlockSpec(memory_space=pltpu.VMEM),) * 3,
        scratch_shapes=scratch,
        compiler_params=pltpu.CompilerParams(
            collective_id=0, has_side_effects=True, vmem_limit_bytes=60 * 2**20
        ),
        name="coupling",
    )(noise_latents, data_latents)
    return pl.pallas_call(
        hand_out,
        out_shape=(
            jax.ShapeDtypeStruct((OWN, WIDTH), F32),
            jax.ShapeDtypeStruct((ROWS,), F32),
            jax.ShapeDtypeStruct((COLS,), F32),
        ),
        in_specs=[pl.BlockSpec(memory_space=pltpu.VMEM)] * 3,
        out_specs=(pl.BlockSpec(memory_space=pl.ANY),) + (pl.BlockSpec(memory_space=pltpu.VMEM),) * 2,
        scratch_shapes=[pltpu.SemaphoreType.DMA((OWN // 8,))],
        compiler_params=pltpu.CompilerParams(vmem_limit_bytes=2 * 2**20),
        name="hand_out",
    )(t, f, g)


def solution(mesh):
    placed = (P(("noise", "dp"), None), P(("dp", "noise"), None))
    return jax.shard_map(
        body,
        mesh=mesh,
        in_specs=placed,
        out_specs=(P(("noise", "dp"), None), P("noise"), P("dp")),
        check_vma=False,
    )
```
